32 devices in a mesh: ctx: 8 (over z, x), head: 4 (over y, core).
Axes of the slice: x: 2, y: 2, z: 4, core: 2. Of those that a mesh axis runs over, the one named last changes fastest.
Arguments:
- queries: bfloat16 [1024, 1024], P('ctx', 'head'), may hold values from -27 to 27
- keys: bfloat16 [1024, 128], P('ctx'), may hold values from -4 to 4
- values: bfloat16 [1024, 128], P('ctx'), may hold values from -6 to 6
- dout: bfloat16 [1024, 1024], P('ctx', 'head'), may hold values from -6 to 6
- positions: int32 [1024], P('ctx'), may hold values from 0 to 1023, as said below
- doc_ids: int32 [1024], P('ctx'), may hold values from 0 to 15, as said below
- w_query: bfloat16 [1024, 16384], P('head'), may hold values from -0.1875 to 0.1875
- w_kv: bfloat16 [256, 16384], P(None, 'head'), may hold values from -0.375 to 0.375
Outputs:
- grad_input: bfloat16 [1024, 16384], P('ctx', 'head')
The draws below stay inside these ranges and needn't reach their ends.
Inputs may be any that keep to these rules, and one draw needn't show every extreme that they name: Stored rows come in aligned runs of 64 rows that hold 64 consecutive positions in order, starting at a multiple of 64; every position of the sequence is stored once. `doc_ids`: A document is a set of consecutive positions that begins at a multiple of 64; its id is its first position divided by 64. The first and the last run of 64 positions each begin a document.
All inputs are finite; a program needn't handle non-finite values.
Results may differ from the reference program's by a relative error of at most 0.019.
Values may be sent and summed in bfloat16 or wider, within the bound.
No kernel may reach another device: no remote copies, remote signals or barrier semaphores. Data moves between devices by JAX's collectives and lax.ppermute only.
A program may use at most 128 MiB of HBM per device.

```python
import math
import jax
import jax.numpy as jnp
from jax import lax

D = 16384
HD = 128
QH = 8
ALIGN = 64
SEQ = 1024


def layout_tables(key):
    block_count = SEQ // ALIGN
    block_order = jax.random.permutation(jax.random.fold_in(key, 101), block_count).astype(jnp.int32)
    block_index = jnp.arange(block_count, dtype=jnp.int32)
    starts_flag = jax.random.randint(jax.random.fold_in(key, 102), (block_count,), 0, 6) == 0
    starts_flag = starts_flag | (block_index == 0) | (block_index == block_count - 1)
    doc_label = lax.cummax(jnp.where(starts_flag, block_index, 0), axis=0)
    offsets = jnp.arange(ALIGN, dtype=jnp.int32)
    positions = (block_order[:, None] * ALIGN + offsets[None, :]).reshape(SEQ)
    documents = jnp.broadcast_to(doc_label[block_order][:, None], (block_count, ALIGN)).reshape(SEQ)
    return (positions.astype(jnp.int32), documents.astype(jnp.int32))


def draw_positions(key, part):
    return layout_tables(key)[0]


def draw_doc_ids(key, part):
    return layout_tables(key)[1]


def draw_queries(key, part):
    result = jnp.clip(jax.random.normal(jax.random.fold_in(key, 214), (SEQ, QH, HD), jnp.float32), -4.0, 4.0)
    return result.reshape(SEQ, QH * HD).astype(jnp.bfloat16)


def draw_keys(key, part):
    result = jnp.clip(jax.random.normal(jax.random.fold_in(key, 222), (SEQ, HD), jnp.float32), -4.0, 4.0)
    return result.astype(jnp.bfloat16)


def steps_of(stream_key, shape, pieces, smallest, largest):
    def one(axis_at, parts):
        draws = jax.random.uniform(jax.random.fold_in(jax.random.fold_in(stream_key, 6), axis_at), (parts,), jnp.float32, smallest / len(pieces), largest / len(pieces))
        return jnp.repeat(jnp.exp(draws), shape[axis_at] // parts).reshape((-1,) + (1,) * (len(shape) - axis_at - 1))

    level = one(*pieces[0])
    for cut in pieces[1:]:
        level = level * one(*cut)
    return level


def gaussian(own_key, extent, deviation, reach, shards=(), kind=jnp.bfloat16):
    gain = steps_of(own_key, extent, shards, -0.22, 0.18) if shards else 1.0
    array = jax.random.normal(own_key, extent, jnp.float32) * deviation * gain
    return jnp.minimum(jnp.maximum(array, -reach), reach).astype(kind)


def setup_inputs(seed: int = 0) -> dict:
    key_of = jax.random.split(jax.random.key(seed), 9)
    queries = draw_queries(jax.random.fold_in(key_of[8], 71), 0)
    keys = draw_keys(jax.random.fold_in(key_of[8], 71), 0)
    values = gaussian(key_of[2], (SEQ, HD), 1.0, 6.0, ((0, 8),))
    dout = gaussian(key_of[3], (SEQ, QH * HD), 1.0, 6.0, ((0, 8), (1, 4)))
    positions = draw_positions(jax.random.fold_in(key_of[8], 71), 0)
    doc_ids = draw_doc_ids(jax.random.fold_in(key_of[8], 71), 0)
    w_query = gaussian(key_of[6], (QH * HD, D), (QH * HD) ** -0.5, 0.1875, ((0, 4),))
    w_kv = gaussian(key_of[7], (2 * HD, D), (2 * HD) ** -0.5, 0.375, ((1, 4),))
    return dict(queries=queries, keys=keys, values=values, dout=dout, positions=positions, doc_ids=doc_ids, w_query=w_query, w_kv=w_kv)


def reference(queries, keys, values, dout, positions, doc_ids, w_query, w_kv):
    inv_root = 1.0 / math.sqrt(HD)
    block_rows = math.gcd(SEQ, 512)
    key_rows = keys.astype(jnp.float32)
    value_rows = values.astype(jnp.float32)

    def one_block(totals, block_number):
        key_sum, value_sum = totals
        first_row = (block_number * block_rows).astype(jnp.int32)
        query_rows = lax.dynamic_slice_in_dim(queries, first_row, block_rows, 0).astype(jnp.float32).reshape(block_rows, QH, HD)
        dout_rows = lax.dynamic_slice_in_dim(dout, first_row, block_rows, 0).astype(jnp.float32).reshape(block_rows, QH, HD)
        row_positions = lax.dynamic_slice_in_dim(positions, first_row, block_rows, 0)
        row_docs = lax.dynamic_slice_in_dim(doc_ids, first_row, block_rows, 0)
        allowed = (row_docs[:, None] == doc_ids[None, :]) & (positions[None, :] <= row_positions[:, None])
        scores = jnp.einsum('qhd,kd->hqk', query_rows, key_rows) * inv_root
        scores = jnp.where(allowed[None], scores, -1e+30)
        row_max = lax.optimization_barrier(jnp.max(scores, axis=-1, keepdims=True))
        row_total = lax.optimization_barrier(jnp.sum(jnp.where(allowed[None], jnp.exp(scores - row_max), 0.0), axis=-1, keepdims=True))
        log_total = row_max + jnp.log(row_total)
        probs = jnp.where(allowed[None], jnp.exp(scores - log_total), 0.0)
        output = jnp.einsum('hqk,kd->hqd', probs, value_rows)
        row_delta = jnp.einsum('qhd,hqd->hq', dout_rows, output)
        probs_low = lax.optimization_barrier(probs.astype(jnp.bfloat16)).astype(jnp.float32)
        value_sum = value_sum + jnp.einsum('hqk,qhd->kd', probs_low, dout_rows)
        dprob = jnp.einsum('qhd,kd->hqk', dout_rows, value_rows)
        dscore = lax.optimization_barrier((probs * (dprob - row_delta[..., None])).astype(jnp.bfloat16)).astype(jnp.float32)
        query_grad = (jnp.einsum('hqk,kd->qhd', dscore, key_rows) * inv_root).astype(jnp.bfloat16).reshape(block_rows, QH * HD)
        key_sum = key_sum + jnp.einsum('hqk,qhd->kd', dscore, query_rows)
        return ((key_sum, value_sum), query_grad)
    zero_rows = jnp.zeros((SEQ, HD), jnp.float32)
    (key_sum, value_sum), grads = lax.scan(one_block, (zero_rows, zero_rows), jnp.arange(SEQ // block_rows, dtype=jnp.int32))
    query_grad = grads.reshape(SEQ, QH * HD)
    kv_grads = jnp.concatenate([key_sum * inv_root, value_sum], axis=1).astype(jnp.bfloat16)
    total = jnp.dot(query_grad, w_query, preferred_element_type=jnp.float32) + jnp.dot(kv_grads, w_kv, preferred_element_type=jnp.float32)
    return total.astype(jnp.bfloat16)
```

```python
import functools
import math

import jax
import jax.numpy as jnp
from jax import lax
from jax.experimental import pallas as pl
from jax.experimental.pallas import tpu as pltpu
from jax.sharding import PartitionSpec as P

RUN = 64
META_ROWS = 16
CHUNKS = 4
VMEM = pl.BlockSpec(memory_space=pltpu.VMEM)
SMEM = pl.BlockSpec(memory_space=pltpu.SMEM)


def params(limit_mib=32):
    return pltpu.CompilerParams(vmem_limit_bytes=limit_mib * 1024 * 1024)


def shifted(value, axis, steps):
    count = lax.axis_size(axis)
    pairs = [(source, (source + steps) % count) for source in range(count)]
    return lax.ppermute(value, axis, pairs)


def swapped(value, axis, bits):
    count = lax.axis_size(axis)
    return lax.ppermute(value, axis, [(source, source ^ bits) for source in range(count)])


def dot(a, b, contract):
    return lax.dot_general(a, b, (contract, ((), ())), preferred_element_type=jnp.float32)


def pack_kernel(pos_ref, key_ref, value_ref, piece_ref):
    rows, head_size = key_ref.shape
    piece_ref[0:rows, 0:head_size] = key_ref[...]
    piece_ref[0:rows, head_size:] = value_ref[...]
    row = lax.broadcasted_iota(jnp.int32, (META_ROWS, 2 * head_size), 0)
    meta = jnp.zeros((META_ROWS, 2 * head_size), jnp.int32)
    for run in range(rows // RUN):
        meta = jnp.where(row == run, pos_ref[run * RUN] // RUN, meta)
    piece_ref[rows:, :] = meta.astype(jnp.float32).astype(jnp.bfloat16)


def pack(positions, keys, values):
    rows, head_size = keys.shape
    return pl.pallas_call(
        pack_kernel,
        out_shape=jax.ShapeDtypeStruct((rows + META_ROWS, 2 * head_size), jnp.bfloat16),
        in_specs=[SMEM, VMEM, VMEM],
        out_specs=VMEM,
        compiler_params=params(),
        name="pack",
    )(positions, keys, values)


def attention_kernel(count, core_ref, row_ref, qm_ref, qo_ref, dm_ref, do_ref, *refs):
    pieces = refs[:count]
    dq_ref = refs[count]
    back = refs[count + 1 : 2 * count + 1]
    s_ref, dp_ref = refs[2 * count + 1 :]
    rows = qm_ref.shape[0]
    size = pieces[0].shape[1] // 2
    heads = qm_ref.shape[1] // size
    inv_root = 1.0 / math.sqrt(size)

    def stack(mine, other):
        parts = [ref[:, h * size : (h + 1) * size] for ref in (mine, other) for h in range(heads)]
        return jnp.concatenate(parts, axis=0)

    query = stack(qm_ref, qo_ref)
    grad = stack(dm_ref, do_ref)
    wide = query.shape[0]
    last = row_ref[0:1, :]
    first = row_ref[1:2, :]
    offset = lax.broadcasted_iota(jnp.int32, (RUN, wide), 0).astype(jnp.float32)

    top = jnp.full((1, wide), -1e30, jnp.float32)
    for s in range(count):
        key = pieces[s][0:rows, 0:size]
        value = pieces[s][0:rows, size:]
        score = dot(key, query, ((1,), (1,))) * inv_root
        dp_ref[s * rows : (s + 1) * rows, :] = dot(value, grad, ((1,), (1,)))
        for run in range(rows // RUN):
            meta = pieces[s][rows : rows + META_ROWS, :].astype(jnp.float32)
            start = meta[run : run + 1, 0:1] * float(RUN)
            pos = offset + start
            allowed = (pos <= last) & (pos >= first)
            part = jnp.where(allowed, score[run * RUN : (run + 1) * RUN], -1e30)
            low = s * rows + run * RUN
            s_ref[low : low + RUN, :] = part
            top = jnp.maximum(top, jnp.max(part, axis=0, keepdims=True))

    total = jnp.zeros((1, wide), jnp.float32)
    mixed = jnp.zeros((1, wide), jnp.float32)
    for s in range(count):
        at = slice(s * rows, (s + 1) * rows)
        weight = jnp.exp(s_ref[at, :] - top)
        s_ref[at, :] = weight
        total = total + jnp.sum(weight, axis=0, keepdims=True)
        mixed = mixed + jnp.sum(weight * dp_ref[at, :], axis=0, keepdims=True)
    scale = 1.0 / total
    delta = mixed * scale

    is_key = core_ref[0] == 0
    other = jnp.where(is_key, query, grad)
    dq = jnp.zeros((size, wide), jnp.float32)
    for s in range(count):
        at = slice(s * rows, (s + 1) * rows)
        prob = s_ref[at, :] * scale
        dscore = (prob * (dp_ref[at, :] - delta)).astype(jnp.bfloat16)
        picked = jnp.where(is_key, dscore, prob.astype(jnp.bfloat16))
        back[s][...] = dot(picked, other, ((1,), (0,))).astype(jnp.bfloat16)
        dq = dq + dot(pieces[s][0:rows, 0:size], dscore, ((0,), (0,)))
    dq = dq * inv_root
    for part in range(wide // rows):
        block = dq[:, part * rows : (part + 1) * rows]
        dq_ref[:, part * size : (part + 1) * size] = block.T.astype(jnp.bfloat16)


def attention(core, row_info, q_mine, q_other, d_mine, d_other, pieces):
    count = len(pieces)
    rows, width = q_mine.shape
    size = pieces[0].shape[1] // 2
    wide = 2 * rows * (width // size)
    return pl.pallas_call(
        functools.partial(attention_kernel, count),
        out_shape=[jax.ShapeDtypeStruct((rows, 2 * width), jnp.bfloat16)]
        + [jax.ShapeDtypeStruct((rows, size), jnp.bfloat16)] * count,
        in_specs=[SMEM] + [VMEM] * (5 + count),
        out_specs=[VMEM] * (1 + count),
        scratch_shapes=[pltpu.VMEM((count * rows, wide), jnp.float32)] * 2,
        compiler_params=params(52),
        cost_estimate=pl.CostEstimate(
            flops=10 * count * rows * wide * size,
            bytes_accessed=count * rows * size * 8,
            transcendentals=count * rows * wide,
        ),
        name="attention",
    )(core, row_info, q_mine, q_other, d_mine, d_other, *pieces)


def product_kernel(at_ref, dq_ref, wm_ref, wo_ref, out_ref):
    depth = wm_ref.shape[0]
    acc = dot(dq_ref[:, 0:depth], wm_ref[...], ((1,), (0,)))
    acc = acc + dot(dq_ref[:, depth:], wo_ref[...], ((1,), (0,)))
    out_ref[...] = acc.astype(out_ref.dtype)


def product(block, dq, w_mine, w_other, first, width, tile, dtype):
    rows, depth = dq.shape
    share = w_other.shape[1]
    return pl.pallas_call(
        product_kernel,
        out_shape=jax.ShapeDtypeStruct((rows, width), dtype),
        grid_spec=pltpu.PrefetchScalarGridSpec(
            num_scalar_prefetch=1,
            grid=(width // tile,),
            in_specs=[
                pl.BlockSpec((rows, depth), lambda i, at: (0, 0)),
                pl.BlockSpec(
                    (depth // 2, tile), lambda i, at: (0, at[0] * (share // tile) + first // tile + i)
                ),
                pl.BlockSpec((depth // 2, tile), lambda i, at: (0, first // tile + i)),
            ],
            out_specs=pl.BlockSpec((rows, tile), lambda i, at: (0, i)),
        ),
        compiler_params=params(),
        cost_estimate=pl.CostEstimate(
            flops=2 * rows * depth * width, bytes_accessed=2 * depth * width, transcendentals=0
        ),
        name="product",
    )(block, dq, w_mine, w_other)


def finish_kernel(chunks, core_ref, mine_ref, other_ref, wm_ref, wo_ref, acc_ref, *refs):
    out_ref = refs[chunks]
    inv_root = 1.0 / math.sqrt(mine_ref.shape[1])
    is_key = core_ref[0] == 0
    mine = (mine_ref[...] * jnp.where(is_key, inv_root, 1.0)).astype(jnp.bfloat16)
    other = (other_ref[...] * jnp.where(is_key, 1.0, inv_root)).astype(jnp.bfloat16)
    width = out_ref.shape[1] // chunks
    for c in range(chunks):
        at = slice(c * width, (c + 1) * width)
        acc = acc_ref[:, at] + refs[c][...].astype(jnp.float32)
        acc = acc + dot(mine, wm_ref[:, at], ((1,), (0,))) + dot(other, wo_ref[:, at], ((1,), (0,)))
        out_ref[:, at] = acc.astype(jnp.bfloat16)


def finish(core, mine, other, w_kv, acc, received):
    rows, width = acc.shape
    size = mine.shape[1]
    chunks = len(received)
    return pl.pallas_call(
        functools.partial(finish_kernel, chunks),
        out_shape=jax.ShapeDtypeStruct((rows, width), jnp.bfloat16),
        grid_spec=pltpu.PrefetchScalarGridSpec(
            num_scalar_prefetch=1,
            grid=(1,),
            in_specs=[
                pl.BlockSpec((rows, size), lambda i, at: (0, 0)),
                pl.BlockSpec((rows, size), lambda i, at: (0, 0)),
                pl.BlockSpec((size, width), lambda i, at: (at[0], 0)),
                pl.BlockSpec((size, width), lambda i, at: (1 - at[0], 0)),
                pl.BlockSpec((rows, width), lambda i, at: (0, 0)),
            ]
            + [pl.BlockSpec((rows, width // chunks), lambda i, at: (0, 0))] * chunks,
            out_specs=pl.BlockSpec((rows, width), lambda i, at: (0, 0)),
        ),
        compiler_params=params(),
        cost_estimate=pl.CostEstimate(
            flops=4 * rows * size * width, bytes_accessed=10 * rows * width, transcendentals=0
        ),
        name="finish",
    )(core, mine, other, w_kv, w_kv, acc, *received)


def on_device(queries, keys, values, dout, positions, doc_ids, w_query, w_kv):
    count = lax.axis_size("ctx")
    head = lax.axis_index("head")
    core = (head % 2).astype(jnp.int32).reshape(1)
    share = w_kv.shape[1]
    local_heads = queries.shape[1] // keys.shape[1]

    piece = pack(positions, keys, values)
    pieces = [piece] + [shifted(piece, "ctx", s) for s in range(1, count)]
    q_other = swapped(queries, "head", 1)
    d_other = swapped(dout, "head", 1)

    def columns(block):
        return lax.dynamic_slice_in_dim(w_query, block * share, share, axis=1)

    w_far = swapped(columns(head ^ 3), "head", 1)
    w_near = swapped(columns(head ^ 1), "head", 1)

    bounds = jnp.stack([positions, doc_ids * RUN]).astype(jnp.float32)
    row_info = jnp.tile(bounds, (1, 2 * local_heads))
    dq, *back = attention(core, row_info, queries, q_other, dout, d_other, pieces)

    far = (head ^ 2).astype(jnp.int32).reshape(1)
    near = head.astype(jnp.int32).reshape(1)
    width = share // CHUNKS
    received = []
    for c in range(CHUNKS):
        part = product(far, dq, w_query, w_far, c * width, width, width, jnp.bfloat16)
        received.append(swapped(part, "head", 2))

    mine = back[0].astype(jnp.float32)
    for s in range(1, count):
        mine = mine + shifted(back[s], "ctx", -s).astype(jnp.float32)
    mine = mine.astype(jnp.bfloat16)
    same = swapped(mine, "head", 2).astype(jnp.float32) + mine.astype(jnp.float32)
    other = swapped(mine, "head", 1).astype(jnp.float32) + swapped(mine, "head", 3).astype(jnp.float32)

    acc = product(near, dq, w_query, w_near, 0, share, min(1024, share), jnp.float32)
    return finish(core, same, other, w_kv, acc, received)


def solution(mesh):
    placed = (
        P("ctx", "head"),
        P("ctx", None),
        P("ctx", None),
        P("ctx", "head"),
        P("ctx"),
        P("ctx"),
        P("head", None),
        P(None, "head"),
    )
    return jax.shard_map(
        on_device, mesh=mesh, in_specs=placed, out_specs=P("ctx", "head"), check_vma=False
    )
```

```python
import functools
import math

import jax
import jax.numpy as jnp
from jax import lax
from jax.experimental import pallas as pl
from jax.experimental.pallas import tpu as pltpu
from jax.sharding import PartitionSpec as P

RUN = 64
META_ROWS = 16
CHUNKS = 4
VMEM = pl.BlockSpec(memory_space=pltpu.VMEM)
SMEM = pl.BlockSpec(memory_space=pltpu.SMEM)


def params(limit_mib=32):
    return pltpu.CompilerParams(vmem_limit_bytes=limit_mib * 1024 * 1024)


def swapped(value, axis, bits):
    count = lax.axis_size(axis)
    return lax.ppermute(value, axis, [(source, source ^ bits) for source in range(count)])


def dot(a, b, contract):
    return lax.dot_general(a, b, (contract, ((), ())), preferred_element_type=jnp.float32)


def each(count, body, state):
    if count > 8:
        return lax.fori_loop(0, count, body, state)
    for step in range(count):
        state = body(step, state)
    return state


def pack_kernel(pos_ref, key_ref, value_ref, query_ref, grad_ref, piece_ref, both_ref):
    count = piece_ref.shape[0]
    rows, head_size = key_ref.shape
    row = lax.broadcasted_iota(jnp.int32, (META_ROWS, 2 * head_size), 0)
    meta = jnp.zeros((META_ROWS, 2 * head_size), jnp.int32)
    for run in range(rows // RUN):
        meta = jnp.where(row == run, pos_ref[run * RUN] // RUN, meta)
    meta = meta.astype(jnp.float32).astype(jnp.bfloat16)

    def copy(c, state):
        piece_ref[c, 0:rows, 0:head_size] = key_ref[...]
        piece_ref[c, 0:rows, head_size:] = value_ref[...]
        piece_ref[c, rows:, :] = meta
        return state

    each(count, copy, 0)
    both_ref[0] = query_ref[...]
    both_ref[1] = grad_ref[...]


def pack(count, positions, keys, values, queries, dout):
    rows, head_size = keys.shape
    return pl.pallas_call(
        pack_kernel,
        out_shape=[
            jax.ShapeDtypeStruct((count, rows + META_ROWS, 2 * head_size), jnp.bfloat16),
            jax.ShapeDtypeStruct((2,) + queries.shape, jnp.bfloat16),
        ],
        in_specs=[SMEM] + [VMEM] * 4,
        out_specs=[VMEM] * 2,
        compiler_params=params(),
        name="pack",
    )(positions, keys, values, queries, dout)


def attention_kernel(core_ref, row_ref, mine_ref, swap_ref, piece_ref, dq_ref, back_ref, s_ref, dp_ref):
    count = piece_ref.shape[0]
    rows = mine_ref.shape[1]
    size = piece_ref.shape[2] // 2
    heads = mine_ref.shape[2] // size
    inv_root = 1.0 / math.sqrt(size)

    def stack(which):
        parts = [
            ref[which, :, h * size : (h + 1) * size] for ref in (mine_ref, swap_ref) for h in range(heads)
        ]
        return jnp.concatenate(parts, axis=0)

    query = stack(0)
    grad = stack(1)
    wide = query.shape[0]
    last = row_ref[0:1, :]
    first = row_ref[1:2, :]
    offset = lax.broadcasted_iota(jnp.int32, (RUN, wide), 0).astype(jnp.float32)

    def scores(s, top):
        key = piece_ref[s, 0:rows, 0:size]
        value = piece_ref[s, 0:rows, size:]
        score = dot(key, query, ((1,), (1,))) * inv_root
        dp_ref[s] = dot(value, grad, ((1,), (1,)))
        meta = piece_ref[s, rows : rows + META_ROWS, :].astype(jnp.float32)
        for run in range(rows // RUN):
            start = meta[run : run + 1, 0:1] * float(RUN)
            pos = offset + start
            allowed = (pos <= last) & (pos >= first)
            part = jnp.where(allowed, score[run * RUN : (run + 1) * RUN], -1e30)
            s_ref[s, run * RUN : (run + 1) * RUN, :] = part
            top = jnp.maximum(top, jnp.max(part, axis=0, keepdims=True))
        return top

    top = each(count, scores, jnp.full((1, wide), -1e30, jnp.float32))

    def weights(s, state):
        total, mixed = state
        weight = jnp.exp(s_ref[s] - top)
        s_ref[s] = weight
        total = total + jnp.sum(weight, axis=0, keepdims=True)
        mixed = mixed + jnp.sum(weight * dp_ref[s], axis=0, keepdims=True)
        return total, mixed

    zeros = jnp.zeros((1, wide), jnp.float32)
    total, mixed = each(count, weights, (zeros, zeros))
    scale = 1.0 / total
    delta = mixed * scale

    is_key = core_ref[0] == 0
    other = jnp.where(is_key, query, grad)

    def gradients(s, dq):
        prob = s_ref[s] * scale
        dscore = (prob * (dp_ref[s] - delta)).astype(jnp.bfloat16)
        picked = jnp.where(is_key, dscore, prob.astype(jnp.bfloat16))
        back_ref[s] = dot(picked, other, ((1,), (0,))).astype(jnp.bfloat16)
        return dq + dot(piece_ref[s, 0:rows, 0:size], dscore, ((0,), (0,)))

    dq = each(count, gradients, jnp.zeros((size, wide), jnp.float32)) * inv_root
    for part in range(wide // rows):
        block = dq[:, part * rows : (part + 1) * rows]
        dq_ref[:, part * size : (part + 1) * size] = block.T.astype(jnp.bfloat16)


def attention(core, row_info, mine, swap, pieces):
    count, _, pair = pieces.shape
    _, rows, width = mine.shape
    size = pair // 2
    wide = 2 * rows * (width // size)
    return pl.pallas_call(
        attention_kernel,
        out_shape=[
            jax.ShapeDtypeStruct((rows, 2 * width), jnp.bfloat16),
            jax.ShapeDtypeStruct((count, rows, size), jnp.bfloat16),
        ],
        in_specs=[SMEM] + [VMEM] * 4,
        out_specs=[VMEM] * 2,
        scratch_shapes=[pltpu.VMEM((count, rows, wide), jnp.float32)] * 2,
        compiler_params=params(44),
        cost_estimate=pl.CostEstimate(
            flops=10 * count * rows * wide * size,
            bytes_accessed=count * rows * size * 8,
            transcendentals=count * rows * wide,
        ),
        name="attention",
    )(core, row_info, mine, swap, pieces)


def product_kernel(at_ref, dq_ref, wm_ref, wo_ref, out_ref):
    depth = wm_ref.shape[0]
    acc = dot(dq_ref[:, 0:depth], wm_ref[...], ((1,), (0,)))
    acc = acc + dot(dq_ref[:, depth:], wo_ref[...], ((1,), (0,)))
    out_ref[...] = acc.astype(out_ref.dtype)


def product(block, dq, w_mine, w_other, which, first, width, tile, dtype):
    rows, depth = dq.shape
    share = w_other.shape[2]
    return pl.pallas_call(
        product_kernel,
        out_shape=jax.ShapeDtypeStruct((rows, width), dtype),
        grid_spec=pltpu.PrefetchScalarGridSpec(
            num_scalar_prefetch=1,
            grid=(width // tile,),
            in_specs=[
                pl.BlockSpec((rows, depth), lambda i, at: (0, 0)),
                pl.BlockSpec(
                    (depth // 2, tile), lambda i, at: (0, at[0] * (share // tile) + first // tile + i)
                ),
                pl.BlockSpec((None, depth // 2, tile), lambda i, at: (which, 0, first // tile + i)),
            ],
            out_specs=pl.BlockSpec((rows, tile), lambda i, at: (0, i)),
        ),
        compiler_params=params(52),
        cost_estimate=pl.CostEstimate(
            flops=2 * rows * depth * width, bytes_accessed=2 * depth * width, transcendentals=0
        ),
        name="product",
    )(block, dq, w_mine, w_other)


def finish_kernel(chunks, core_ref, mine_ref, other_ref, wm_ref, wo_ref, acc_ref, *refs):
    out_ref = refs[chunks]
    inv_root = 1.0 / math.sqrt(mine_ref.shape[1])
    is_key = core_ref[0] == 0
    mine = (mine_ref[...] * jnp.where(is_key, inv_root, 1.0)).astype(jnp.bfloat16)
    other = (other_ref[...] * jnp.where(is_key, 1.0, inv_root)).astype(jnp.bfloat16)
    width = out_ref.shape[1] // chunks
    for c in range(chunks):
        at = slice(c * width, (c + 1) * width)
        acc = acc_ref[:, at] + refs[c][...].astype(jnp.float32)
        acc = acc + dot(mine, wm_ref[:, at], ((1,), (0,))) + dot(other, wo_ref[:, at], ((1,), (0,)))
        out_ref[:, at] = acc.astype(jnp.bfloat16)


def finish(core, mine, other, w_kv, acc, received):
    rows, width = acc.shape
    size = mine.shape[1]
    chunks = len(received)
    return pl.pallas_call(
        functools.partial(finish_kernel, chunks),
        out_shape=jax.ShapeDtypeStruct((rows, width), jnp.bfloat16),
        grid_spec=pltpu.PrefetchScalarGridSpec(
            num_scalar_prefetch=1,
            grid=(1,),
            in_specs=[
                pl.BlockSpec((rows, size), lambda i, at: (0, 0)),
                pl.BlockSpec((rows, size), lambda i, at: (0, 0)),
                pl.BlockSpec((size, width), lambda i, at: (at[0], 0)),
                pl.BlockSpec((size, width), lambda i, at: (1 - at[0], 0)),
                pl.BlockSpec((rows, width), lambda i, at: (0, 0)),
            ]
            + [pl.BlockSpec((rows, width // chunks), lambda i, at: (0, 0))] * chunks,
            out_specs=pl.BlockSpec((rows, width), lambda i, at: (0, 0)),
        ),
        compiler_params=params(),
        cost_estimate=pl.CostEstimate(
            flops=4 * rows * size * width, bytes_accessed=10 * rows * width, transcendentals=0
        ),
        name="finish",
    )(core, mine, other, w_kv, w_kv, acc, *received)


def on_device(queries, keys, values, dout, positions, doc_ids, w_query, w_kv):
    count = lax.axis_size("ctx")
    head = lax.axis_index("head")
    core = (head % 2).astype(jnp.int32).reshape(1)
    share = w_kv.shape[1]
    local_heads = queries.shape[1] // keys.shape[1]

    piece, both = pack(count, positions, keys, values, queries, dout)
    pieces = lax.all_to_all(piece, "ctx", 0, 0)
    swap = swapped(both, "head", 1)

    w_late, _ = lax.optimization_barrier((w_query, both))

    def columns(block):
        return lax.dynamic_slice_in_dim(w_late, block * share, share, axis=1)

    w_other = swapped(jnp.stack([columns(head ^ 3), columns(head ^ 1)]), "head", 1)

    bounds = jnp.stack([positions, doc_ids * RUN]).astype(jnp.float32)
    row_info = jnp.tile(bounds, (1, 2 * local_heads))
    dq, back = attention(core, row_info, both, swap, pieces)

    far = (head ^ 2).astype(jnp.int32).reshape(1)
    near = head.astype(jnp.int32).reshape(1)
    width = share // CHUNKS
    parts = [
        product(far, dq, w_query, w_other, 0, c * width, width, width, jnp.bfloat16) for c in range(CHUNKS)
    ]
    parts, back = lax.optimization_barrier((parts, back))
    received = [swapped(part, "head", 2) for part in parts]

    back = lax.all_to_all(back, "ctx", 0, 0)
    mine = jnp.sum(back.astype(jnp.float32), axis=0).astype(jnp.bfloat16)
    same = swapped(mine, "head", 2).astype(jnp.float32) + mine.astype(jnp.float32)
    other = swapped(mine, "head", 1).astype(jnp.float32) + swapped(mine, "head", 3).astype(jnp.float32)

    acc = product(near, dq, w_query, w_other, 1, 0, share, min(1024, share), jnp.float32)
    return finish(core, same, other, w_kv, acc, received)


def solution(mesh):
    placed = (
        P("ctx", "head"),
        P("ctx", None),
        P("ctx", None),
        P("ctx", "head"),
        P("ctx"),
        P("ctx"),
        P("head", None),
        P(None, "head"),
    )
    return jax.shard_map(
        on_device, mesh=mesh, in_specs=placed, out_specs=P("ctx", "head"), check_vma=False
    )
```

```python
import functools
import math

import jax
import jax.numpy as jnp
from jax import lax
from jax.experimental import pallas as pl
from jax.experimental.pallas import tpu as pltpu
from jax.sharding import PartitionSpec as P

RUN = 64
META_ROWS = 16
CHUNKS = (2, 4, 5, 5)
ANY = pl.BlockSpec(memory_space=pl.ANY)
HBM = pl.BlockSpec(memory_space=pltpu.HBM)
SMEM = pl.BlockSpec(memory_space=pltpu.SMEM)


def params(limit_mib=32):
    return pltpu.CompilerParams(vmem_limit_bytes=limit_mib * 1024 * 1024)


def swapped(value, axis, bits):
    count = lax.axis_size(axis)
    return lax.ppermute(value, axis, [(source, source ^ bits) for source in range(count)])


def dot(a, b, contract):
    return lax.dot_general(a, b, (contract, ((), ())), preferred_element_type=jnp.float32)


def each(count, body, state):
    if count > 8:
        return lax.fori_loop(0, count, body, state)
    for step in range(count):
        state = body(step, state)
    return state


def pack(count, core, positions, keys, values):
    rows, size = keys.shape
    held = jnp.where(core == 0, keys, values)
    runs = (positions.reshape(rows // RUN, RUN)[:, :1] // RUN).astype(jnp.bfloat16)
    meta = jnp.pad(jnp.broadcast_to(runs, (rows // RUN, size)), ((0, META_ROWS - rows // RUN), (0, 0)))
    piece = jnp.concatenate([held, meta], axis=0)
    return jnp.broadcast_to(piece, (count,) + piece.shape)


def carve_kernel(block_ref, w_ref, after_ref, *refs):
    outs, sems = refs[:-1], refs[-1]
    share = outs[0].shape[1]
    copies = []
    for i, out_ref in enumerate(outs):
        at = pl.multiple_of(block_ref[i] * share, share)
        copies.append(pltpu.make_async_copy(w_ref.at[:, pl.ds(at, share)], out_ref, sems.at[i]))
        copies[i].start()
    for one in copies:
        one.wait()


def carve(blocks, w_query, after, share):
    shape = jax.ShapeDtypeStruct((w_query.shape[0], share), w_query.dtype)
    count = len(blocks)
    return pl.pallas_call(
        carve_kernel,
        out_shape=[shape] * count,
        in_specs=[SMEM, HBM, ANY],
        out_specs=[ANY] * count,
        scratch_shapes=[pltpu.SemaphoreType.DMA((count,))],
        compiler_params=params(48),
        cost_estimate=pl.CostEstimate(
            flops=0, bytes_accessed=4 * count * w_query.shape[0] * share, transcendentals=0
        ),
        name="carve",
    )(jnp.stack(blocks), w_query, after)


def attention_kernel(
    core_ref, row_ref, qm_ref, qo_ref, gm_ref, go_ref, here_ref, there_ref, dq_ref, back_ref, s_ref, dp_ref
):
    count = here_ref.shape[0]
    rows, width = qm_ref.shape
    size = here_ref.shape[2]
    is_key = core_ref[0] == 0
    heads = width // size
    inv_root = 1.0 / math.sqrt(size)

    def stack(mine_ref, other_ref):
        parts = [ref[:, h * size : (h + 1) * size] for ref in (mine_ref, other_ref) for h in range(heads)]
        return jnp.concatenate(parts, axis=0)

    query = stack(qm_ref, qo_ref)
    grad = stack(gm_ref, go_ref)
    wide = query.shape[0]
    last = row_ref[0:1, :]
    first = row_ref[1:2, :]
    offset = lax.broadcasted_iota(jnp.int32, (RUN, wide), 0).astype(jnp.float32)

    def scores(s, top):
        here = here_ref[s, 0:rows, :]
        there = there_ref[s, 0:rows, :]
        key = jnp.where(is_key, here, there)
        value = jnp.where(is_key, there, here)
        score = dot(key, query, ((1,), (1,))) * inv_root
        dp_ref[s] = dot(value, grad, ((1,), (1,)))
        meta = here_ref[s, rows : rows + META_ROWS, :].astype(jnp.float32)
        for run in range(rows // RUN):
            start = meta[run : run + 1, 0:1] * float(RUN)
            pos = offset + start
            allowed = (pos <= last) & (pos >= first)
            part = jnp.where(allowed, score[run * RUN : (run + 1) * RUN], -1e30)
            s_ref[s, run * RUN : (run + 1) * RUN, :] = part
            top = jnp.maximum(top, jnp.max(part, axis=0, keepdims=True))
        return top

    top = each(count, scores, jnp.full((1, wide), -1e30, jnp.float32))

    def weights(s, state):
        total, mixed = state
        weight = jnp.exp(s_ref[s] - top)
        s_ref[s] = weight
        total = total + jnp.sum(weight, axis=0, keepdims=True)
        mixed = mixed + jnp.sum(weight * dp_ref[s], axis=0, keepdims=True)
        return total, mixed

    zeros = jnp.zeros((1, wide), jnp.float32)
    total, mixed = each(count, weights, (zeros, zeros))
    scale = 1.0 / total
    delta = mixed * scale

    other = jnp.where(is_key, query, grad)

    def gradients(s, dq):
        prob = s_ref[s] * scale
        dscore = (prob * (dp_ref[s] - delta)).astype(jnp.bfloat16)
        picked = jnp.where(is_key, dscore, prob.astype(jnp.bfloat16))
        back_ref[s] = dot(picked, other, ((1,), (0,))).astype(jnp.bfloat16)
        key = jnp.where(is_key, here_ref[s, 0:rows, :], there_ref[s, 0:rows, :])
        return dq + dot(key, dscore, ((0,), (0,)))

    dq = each(count, gradients, jnp.zeros((size, wide), jnp.float32)) * inv_root
    for part in range(wide // rows):
        block = dq[:, part * rows : (part + 1) * rows]
        dq_ref[:, part * size : (part + 1) * size] = block.T.astype(jnp.bfloat16)


def attention(core, row_info, q_mine, q_other, g_mine, g_other, here, there):
    count, _, size = here.shape
    rows, width = q_mine.shape
    wide = 2 * rows * (width // size)
    return pl.pallas_call(
        attention_kernel,
        out_shape=[
            jax.ShapeDtypeStruct((rows, 2 * width), jnp.bfloat16),
            jax.ShapeDtypeStruct((count, rows, size), jnp.bfloat16),
        ],
        in_specs=[SMEM] + [pl.BlockSpec()] * 7,
        out_specs=[pl.BlockSpec()] * 2,
        scratch_shapes=[pltpu.VMEM((count, rows, wide), jnp.float32)] * 2,
        compiler_params=params(44),
        cost_estimate=pl.CostEstimate(
            flops=10 * count * rows * wide * size,
            bytes_accessed=count * rows * size * 8,
            transcendentals=count * rows * wide,
        ),
        name="attention",
    )(core, row_info, q_mine, q_other, g_mine, g_other, here, there)


def product_kernel(first, dq_ref, wm_ref, wo_ref, out_ref):
    depth = wm_ref.shape[0]
    at = slice(first, first + out_ref.shape[1])
    acc = dot(dq_ref[:, 0:depth], wm_ref[:, at], ((1,), (0,)))
    acc = acc + dot(dq_ref[:, depth:], wo_ref[:, at], ((1,), (0,)))
    out_ref[...] = acc.astype(out_ref.dtype)


def product(dq, w_mine, w_other, first, width, dtype):
    rows, depth = dq.shape
    return pl.pallas_call(
        functools.partial(product_kernel, first),
        out_shape=jax.ShapeDtypeStruct((rows, width), dtype),
        in_specs=[pl.BlockSpec()] * 3,
        out_specs=pl.BlockSpec(),
        compiler_params=params(16),
        cost_estimate=pl.CostEstimate(
            flops=2 * rows * depth * width, bytes_accessed=2 * depth * width, transcendentals=0
        ),
        name="product",
    )(dq, w_mine, w_other)


def finish_kernel(starts, core_ref, mine_ref, other_ref, w_ref, acc_ref, *refs):
    early = len(starts) - 2
    out_ref, left_ref = refs[early:]
    inv_root = 1.0 / math.sqrt(mine_ref.shape[1])
    size = mine_ref.shape[1]
    is_key = core_ref[0] == 0
    wm_ref = w_ref.at[pl.ds(pl.multiple_of(core_ref[0] * size, size), size), :]
    wo_ref = w_ref.at[pl.ds(pl.multiple_of((1 - core_ref[0]) * size, size), size), :]
    mine = (mine_ref[...] * jnp.where(is_key, inv_root, 1.0)).astype(jnp.bfloat16)
    other = (other_ref[...] * jnp.where(is_key, 1.0, inv_root)).astype(jnp.bfloat16)
    for c in range(early + 1):
        at = slice(starts[c], starts[c + 1])
        acc = acc_ref[:, at] + dot(mine, wm_ref[:, at], ((1,), (0,))) + dot(other, wo_ref[:, at], ((1,), (0,)))
        if c < early:
            out_ref[:, at] = (acc + refs[c][...].astype(jnp.float32)).astype(jnp.bfloat16)
        else:
            left_ref[...] = acc


def finish(core, mine, other, w_kv, acc, received, starts):
    rows, share = acc.shape
    size = mine.shape[1]
    last = starts[-2]
    return pl.pallas_call(
        functools.partial(finish_kernel, starts),
        out_shape=[
            jax.ShapeDtypeStruct((rows, share), jnp.bfloat16),
            jax.ShapeDtypeStruct((rows, share - last), jnp.float32),
        ],
        grid=(1,),
        in_specs=[SMEM] + [pl.BlockSpec()] * (4 + len(received)),
        out_specs=[
            pl.BlockSpec((rows, last), lambda i: (0, 0)),
            pl.BlockSpec((rows, share - last), lambda i: (0, 0)),
        ],
        compiler_params=params(),
        cost_estimate=pl.CostEstimate(
            flops=4 * rows * size * share, bytes_accessed=10 * rows * share, transcendentals=0
        ),
        name="finish",
    )(core, mine, other, w_kv, acc, *received)


def last_kernel(left_ref, part_ref, held_ref, out_ref, sum_ref, sem):
    sum_ref[...] = (left_ref[...] + part_ref[...].astype(jnp.float32)).astype(jnp.bfloat16)
    first = out_ref.shape[1] - sum_ref.shape[1]
    copy = pltpu.make_async_copy(sum_ref, out_ref.at[:, first:], sem)
    copy.start()
    copy.wait()


def last(left, part, held):
    return pl.pallas_call(
        last_kernel,
        out_shape=jax.ShapeDtypeStruct(held.shape, held.dtype),
        in_specs=[pl.BlockSpec(), pl.BlockSpec(), ANY],
        out_specs=ANY,
        input_output_aliases={2: 0},
        scratch_shapes=[pltpu.VMEM(part.shape, held.dtype), pltpu.SemaphoreType.DMA(())],
        compiler_params=params(),
        name="last",
    )(left, part, held)


def on_device(queries, keys, values, dout, positions, doc_ids, w_query, w_kv):
    count = lax.axis_size("ctx")
    head = lax.axis_index("head").astype(jnp.int32)
    core = (head & 1).reshape(1)
    share = w_kv.shape[1]

    here = lax.all_to_all(pack(count, core, positions, keys, values), "ctx", 0, 0)
    there = swapped(here, "head", 1)
    q_other = swapped(queries, "head", 1)
    g_other = swapped(dout, "head", 1)

    send = carve([head ^ 3, head ^ 1], w_query, positions, share)
    far_other, near_other = [swapped(part, "head", 1) for part in send]
    far_mine, near_mine = carve([head ^ 2, head], w_query, q_other, share)

    bounds = jnp.stack([positions, doc_ids * RUN]).astype(jnp.float32)
    row_info = jnp.tile(bounds, (1, 2 * (queries.shape[1] // keys.shape[1])))
    dq, back = attention(core, row_info, queries, q_other, dout, g_other, here, there)

    starts = [0]
    for units in CHUNKS:
        starts.append(starts[-1] + units * (share // sum(CHUNKS)))
    received = []
    for low, high in zip(starts, starts[1:]):
        part = product(dq, far_mine, far_other, low, high - low, jnp.bfloat16)
        received.append(swapped(part, "head", 2))

    received[0], back = lax.optimization_barrier((received[0], back))
    back = lax.all_to_all(back, "ctx", 0, 0)
    mine = jnp.sum(back.astype(jnp.float32), axis=0).astype(jnp.bfloat16)
    mine = mine.astype(jnp.float32) + swapped(mine, "head", 2).astype(jnp.float32)
    other = swapped(mine.astype(jnp.bfloat16), "head", 1).astype(jnp.float32)

    acc = product(dq, near_mine, near_other, 0, share, jnp.float32)
    held, left = finish(core, mine, other, w_kv, acc, received[:-1], starts)
    return last(left, received[-1], held)


def solution(mesh):
    placed = (
        P("ctx", "head"),
        P("ctx", None),
        P("ctx", None),
        P("ctx", "head"),
        P("ctx"),
        P("ctx"),
        P("head", None),
        P(None, "head"),
    )
    return jax.shard_map(
        on_device, mesh=mesh, in_specs=placed, out_specs=P("ctx", "head"), check_vma=False
    )
```

```python
import functools
import math

import jax
import jax.numpy as jnp
from jax import lax
from jax.experimental import pallas as pl
from jax.experimental.pallas import tpu as pltpu
from jax.sharding import PartitionSpec as P

RUN = 64
META_ROWS = 16
CHUNKS = (2, 7, 7)
ANY = pl.BlockSpec(memory_space=pl.ANY)
HBM = pl.BlockSpec(memory_space=pltpu.HBM)
SMEM = pl.BlockSpec(memory_space=pltpu.SMEM)


def params(limit_mib=16):
    return pltpu.CompilerParams(vmem_limit_bytes=limit_mib * 1024 * 1024)


def swapped(value, axis, bits):
    count = lax.axis_size(axis)
    return lax.ppermute(value, axis, [(source, source ^ bits) for source in range(count)])


def dot(a, b, contract):
    return lax.dot_general(a, b, (contract, ((), ())), preferred_element_type=jnp.float32)


def each(count, body, state):
    if count > 8:
        return lax.fori_loop(0, count, body, state)
    for step in range(count):
        state = body(step, state)
    return state


def pack(count, core, positions, keys, values):
    rows, size = keys.shape
    held = jnp.where(core == 0, keys, values)
    runs = (positions.reshape(rows // RUN, RUN)[:, :1] // RUN).astype(jnp.bfloat16)
    meta = jnp.pad(jnp.broadcast_to(runs, (rows // RUN, size)), ((0, META_ROWS - rows // RUN), (0, 0)))
    piece = jnp.concatenate([held, meta], axis=0)
    return jnp.broadcast_to(piece, (count,) + piece.shape)


def carve_kernel(block_ref, w_ref, after_ref, *refs):
    outs, sems = refs[:-1], refs[-1]
    rows, share = outs[0].shape
    parts = sems.shape[1]
    copies = []
    for i, out_ref in enumerate(outs):
        at = pl.multiple_of(block_ref[i] * share, share)
        for j in range(parts):
            part = slice(j * (rows // parts), (j + 1) * (rows // parts))
            source = w_ref.at[part, pl.ds(at, share)]
            copies.append(pltpu.make_async_copy(source, out_ref.at[part, :], sems.at[i, j]))
            copies[-1].start()
    for one in copies:
        one.wait()


def carve(blocks, w_query, after, share):
    shape = jax.ShapeDtypeStruct((w_query.shape[0], share), w_query.dtype)
    count = len(blocks)
    return pl.pallas_call(
        carve_kernel,
        out_shape=[shape] * count,
        in_specs=[SMEM, HBM, ANY],
        out_specs=[pl.BlockSpec(memory_space=pltpu.VMEM)] * count,
        scratch_shapes=[pltpu.SemaphoreType.DMA((count, 4))],
        compiler_params=params(48),
        cost_estimate=pl.CostEstimate(
            flops=0, bytes_accessed=4 * count * w_query.shape[0] * share, transcendentals=0
        ),
        name="carve",
    )(jnp.stack(blocks), w_query, after)


def attention_kernel(
    core_ref, row_ref, qm_ref, qo_ref, gm_ref, go_ref, here_ref, there_ref, dq_ref, back_ref, s_ref, dp_ref
):
    count = here_ref.shape[0]
    rows, width = qm_ref.shape
    size = here_ref.shape[2]
    is_key = core_ref[0] == 0
    heads = width // size
    inv_root = 1.0 / math.sqrt(size)

    def stack(mine_ref, other_ref):
        parts = [ref[:, h * size : (h + 1) * size] for ref in (mine_ref, other_ref) for h in range(heads)]
        return jnp.concatenate(parts, axis=0)

    query = stack(qm_ref, qo_ref)
    grad = stack(gm_ref, go_ref)
    wide = query.shape[0]
    last = row_ref[0:1, :]
    first = row_ref[1:2, :]
    offset = lax.broadcasted_iota(jnp.int32, (RUN, wide), 0).astype(jnp.float32)

    def scores(s, top):
        here = here_ref[s, 0:rows, :]
        there = there_ref[s, 0:rows, :]
        key = jnp.where(is_key, here, there)
        value = jnp.where(is_key, there, here)
        score = dot(key, query, ((1,), (1,))) * inv_root
        dp_ref[s] = dot(value, grad, ((1,), (1,)))
        meta = here_ref[s, rows : rows + META_ROWS, :].astype(jnp.float32)
        for run in range(rows // RUN):
            start = meta[run : run + 1, 0:1] * float(RUN)
            pos = offset + start
            allowed = (pos <= last) & (pos >= first)
            part = jnp.where(allowed, score[run * RUN : (run + 1) * RUN], -1e30)
            s_ref[s, run * RUN : (run + 1) * RUN, :] = part
            top = jnp.maximum(top, jnp.max(part, axis=0, keepdims=True))
        return top

    top = each(count, scores, jnp.full((1, wide), -1e30, jnp.float32))

    def weights(s, state):
        total, mixed = state
        weight = jnp.exp(s_ref[s] - top)
        s_ref[s] = weight
        total = total + jnp.sum(weight, axis=0, keepdims=True)
        mixed = mixed + jnp.sum(weight * dp_ref[s], axis=0, keepdims=True)
        return total, mixed

    zeros = jnp.zeros((1, wide), jnp.float32)
    total, mixed = each(count, weights, (zeros, zeros))
    scale = 1.0 / total
    delta = mixed * scale

    other = jnp.where(is_key, query, grad)

    def gradients(s, dq):
        prob = s_ref[s] * scale
        dscore = (prob * (dp_ref[s] - delta)).astype(jnp.bfloat16)
        picked = jnp.where(is_key, dscore, prob.astype(jnp.bfloat16))
        back_ref[s] = dot(picked, other, ((1,), (0,))).astype(jnp.bfloat16)
        key = jnp.where(is_key, here_ref[s, 0:rows, :], there_ref[s, 0:rows, :])
        return dq + dot(key, dscore, ((0,), (0,)))

    dq = each(count, gradients, jnp.zeros((size, wide), jnp.float32)) * inv_root
    for part in range(wide // rows):
        block = dq[:, part * rows : (part + 1) * rows]
        dq_ref[:, part * size : (part + 1) * size] = block.T.astype(jnp.bfloat16)


def attention(core, row_info, q_mine, q_other, g_mine, g_other, here, there):
    count, _, size = here.shape
    rows, width = q_mine.shape
    wide = 2 * rows * (width // size)
    return pl.pallas_call(
        attention_kernel,
        out_shape=[
            jax.ShapeDtypeStruct((rows, 2 * width), jnp.bfloat16),
            jax.ShapeDtypeStruct((count, rows, size), jnp.bfloat16),
        ],
        in_specs=[SMEM] + [pl.BlockSpec()] * 7,
        out_specs=[pl.BlockSpec()] * 2,
        scratch_shapes=[pltpu.VMEM((count, rows, wide), jnp.float32)] * 2,
        compiler_params=params(8 + count * rows * wide // 2**17),
        cost_estimate=pl.CostEstimate(
            flops=10 * count * rows * wide * size,
            bytes_accessed=count * rows * size * 8,
            transcendentals=count * rows * wide,
        ),
        name="attention",
    )(core, row_info, q_mine, q_other, g_mine, g_other, here, there)


def product_kernel(first, dq_ref, wm_ref, wo_ref, out_ref):
    depth = wm_ref.shape[0]
    at = slice(first, first + out_ref.shape[1])
    acc = dot(dq_ref[:, 0:depth], wm_ref[:, at], ((1,), (0,)))
    acc = acc + dot(dq_ref[:, depth:], wo_ref[:, at], ((1,), (0,)))
    out_ref[...] = acc.astype(out_ref.dtype)


def product(dq, w_mine, w_other, first, width, dtype):
    rows, depth = dq.shape
    return pl.pallas_call(
        functools.partial(product_kernel, first),
        out_shape=jax.ShapeDtypeStruct((rows, width), dtype),
        in_specs=[pl.BlockSpec()] * 3,
        out_specs=pl.BlockSpec(),
        compiler_params=params(16),
        cost_estimate=pl.CostEstimate(
            flops=2 * rows * depth * width, bytes_accessed=2 * depth * width, transcendentals=0
        ),
        name="product",
    )(dq, w_mine, w_other)


def finish_kernel(starts, core_ref, mine_ref, other_ref, w_ref, acc_ref, *refs):
    early = len(starts) - 2
    out_ref, left_ref = refs[early:]
    inv_root = 1.0 / math.sqrt(mine_ref.shape[1])
    size = mine_ref.shape[1]
    is_key = core_ref[0] == 0
    wm_ref = w_ref.at[pl.ds(pl.multiple_of(core_ref[0] * size, size), size), :]
    wo_ref = w_ref.at[pl.ds(pl.multiple_of((1 - core_ref[0]) * size, size), size), :]
    mine = (mine_ref[...] * jnp.where(is_key, inv_root, 1.0)).astype(jnp.bfloat16)
    other = (other_ref[...] * jnp.where(is_key, 1.0, inv_root)).astype(jnp.bfloat16)
    for c in range(early + 1):
        at = slice(starts[c], starts[c + 1])
        acc = acc_ref[:, at] + dot(mine, wm_ref[:, at], ((1,), (0,))) + dot(other, wo_ref[:, at], ((1,), (0,)))
        if c < early:
            out_ref[:, at] = (acc + refs[c][...].astype(jnp.float32)).astype(jnp.bfloat16)
        else:
            left_ref[...] = acc


def finish(core, mine, other, w_kv, acc, received, starts):
    rows, share = acc.shape
    size = mine.shape[1]
    last = starts[-2]
    return pl.pallas_call(
        functools.partial(finish_kernel, starts),
        out_shape=[
            jax.ShapeDtypeStruct((rows, share), jnp.bfloat16),
            jax.ShapeDtypeStruct((rows, share - last), jnp.float32),
        ],
        grid=(1,),
        in_specs=[SMEM] + [pl.BlockSpec()] * (4 + len(received)),
        out_specs=[
            pl.BlockSpec((rows, last), lambda i: (0, 0)),
            pl.BlockSpec((rows, share - last), lambda i: (0, 0)),
        ],
        compiler_params=params(),
        cost_estimate=pl.CostEstimate(
            flops=4 * rows * size * share, bytes_accessed=10 * rows * share, transcendentals=0
        ),
        name="finish",
    )(core, mine, other, w_kv, acc, *received)


def last_kernel(left_ref, part_ref, held_ref, out_ref, sum_ref, sem):
    sum_ref[...] = (left_ref[...] + part_ref[...].astype(jnp.float32)).astype(jnp.bfloat16)
    first = out_ref.shape[1] - sum_ref.shape[1]
    copy = pltpu.make_async_copy(sum_ref, out_ref.at[:, first:], sem)
    copy.start()
    copy.wait()


def last(left, part, held):
    return pl.pallas_call(
        last_kernel,
        out_shape=jax.ShapeDtypeStruct(held.shape, held.dtype),
        in_specs=[pl.BlockSpec(), pl.BlockSpec(), ANY],
        out_specs=ANY,
        input_output_aliases={2: 0},
        scratch_shapes=[pltpu.VMEM(part.shape, held.dtype), pltpu.SemaphoreType.DMA(())],
        compiler_params=params(),
        name="last",
    )(left, part, held)


def on_device(queries, keys, values, dout, positions, doc_ids, w_query, w_kv):
    count = lax.axis_size("ctx")
    head = lax.axis_index("head").astype(jnp.int32)
    core = (head & 1).reshape(1)
    share = w_kv.shape[1]

    here = lax.all_to_all(pack(count, core, positions, keys, values), "ctx", 0, 0)
    there = swapped(here, "head", 1)
    q_other = swapped(queries, "head", 1)
    g_other = swapped(dout, "head", 1)

    send = carve([head ^ 3, head ^ 1], w_query, positions, share)
    far_other, near_other = [swapped(part, "head", 1) for part in send]
    far_mine, near_mine = carve([head ^ 2, head], w_query, g_other, share)

    bounds = jnp.stack([positions, doc_ids * RUN]).astype(jnp.float32)
    row_info = jnp.tile(bounds, (1, 2 * (queries.shape[1] // keys.shape[1])))
    dq, back = attention(core, row_info, queries, q_other, dout, g_other, here, there)

    starts = [0]
    for units in CHUNKS:
        starts.append(starts[-1] + units * (share // sum(CHUNKS)))
    parts = [
        product(dq, far_mine, far_other, low, high - low, jnp.bfloat16) for low, high in zip(starts, starts[1:])
    ]
    received = [swapped(part, "head", 2) for part in parts]

    back, *_ = lax.optimization_barrier([back, received[0]] + parts)
    back = lax.all_to_all(back, "ctx", 0, 0)
    mine = jnp.sum(back.astype(jnp.float32), axis=0).astype(jnp.bfloat16)
    mine = mine.astype(jnp.float32) + swapped(mine, "head", 2).astype(jnp.float32)
    other = swapped(mine.astype(jnp.bfloat16), "head", 1).astype(jnp.float32)

    acc = product(dq, near_mine, near_other, 0, share, jnp.float32)
    held, left = finish(core, mine, other, w_kv, acc, received[:-1], starts)
    return last(left, received[-1], held)


def solution(mesh):
    placed = (
        P("ctx", "head"),
        P("ctx", None),
        P("ctx", None),
        P("ctx", "head"),
        P("ctx"),
        P("ctx"),
        P("head", None),
        P(None, "head"),
    )
    return jax.shard_map(
        on_device, mesh=mesh, in_specs=placed, out_specs=P("ctx", "head"), check_vma=False
    )
```

```python
import functools
import math

import jax
import jax.numpy as jnp
from jax import lax
from jax.experimental import pallas as pl
from jax.experimental.pallas import tpu as pltpu
from jax.sharding import PartitionSpec as P

RUN = 64
META_ROWS = 16
CHUNKS = (1, 11, 4)
ANY = pl.BlockSpec(memory_space=pl.ANY)
HBM = pl.BlockSpec(memory_space=pltpu.HBM)
SMEM = pl.BlockSpec(memory_space=pltpu.SMEM)


def params(limit_mib=16):
    return pltpu.CompilerParams(vmem_limit_bytes=limit_mib * 1024 * 1024)


def swapped(value, axis, bits):
    count = lax.axis_size(axis)
    return lax.ppermute(value, axis, [(source, source ^ bits) for source in range(count)])


def dot(a, b, contract):
    return lax.dot_general(a, b, (contract, ((), ())), preferred_element_type=jnp.float32)


def each(count, body, state):
    if count > 8:
        return lax.fori_loop(0, count, body, state)
    for step in range(count):
        state = body(step, state)
    return state


def pack(count, core, positions, keys, values):
    rows, size = keys.shape
    held = jnp.where(core == 0, keys, values)
    runs = (positions.reshape(rows // RUN, RUN)[:, :1] // RUN).astype(jnp.bfloat16)
    meta = jnp.pad(jnp.broadcast_to(runs, (rows // RUN, size)), ((0, META_ROWS - rows // RUN), (0, 0)))
    piece = jnp.concatenate([held, meta], axis=0)
    return jnp.broadcast_to(piece, (count,) + piece.shape)


def carve_kernel(block_ref, w_ref, after_ref, *refs):
    outs, sems = refs[:-1], refs[-1]
    rows, share = outs[0].shape
    parts = sems.shape[1]
    copies = []
    for i, out_ref in enumerate(outs):
        at = pl.multiple_of(block_ref[i] * share, share)
        for j in range(parts):
            part = slice(j * (rows // parts), (j + 1) * (rows // parts))
            source = w_ref.at[part, pl.ds(at, share)]
            copies.append(pltpu.make_async_copy(source, out_ref.at[part, :], sems.at[i, j]))
            copies[-1].start()
    for one in copies:
        one.wait()


def carve(blocks, w_query, after, share):
    shape = jax.ShapeDtypeStruct((w_query.shape[0], share), w_query.dtype)
    count = len(blocks)
    return pl.pallas_call(
        carve_kernel,
        out_shape=[shape] * count,
        in_specs=[SMEM, HBM, ANY],
        out_specs=[pl.BlockSpec(memory_space=pltpu.VMEM)] * count,
        scratch_shapes=[pltpu.SemaphoreType.DMA((count, 4))],
        compiler_params=params(48),
        cost_estimate=pl.CostEstimate(
            flops=0, bytes_accessed=4 * count * w_query.shape[0] * share, transcendentals=0
        ),
        name="carve",
    )(jnp.stack(blocks), w_query, after)


def attention_kernel(
    core_ref, row_ref, qm_ref, qo_ref, gm_ref, go_ref, here_ref, there_ref, dq_ref, back_ref, s_ref, dp_ref
):
    count = here_ref.shape[0]
    rows, width = qm_ref.shape
    size = here_ref.shape[2]
    is_key = core_ref[0] == 0
    heads = width // size
    inv_root = 1.0 / math.sqrt(size)

    def stack(mine_ref, other_ref):
        parts = [ref[:, h * size : (h + 1) * size] for ref in (mine_ref, other_ref) for h in range(heads)]
        return jnp.concatenate(parts, axis=0)

    query = stack(qm_ref, qo_ref)
    grad = stack(gm_ref, go_ref)
    wide = query.shape[0]
    last = row_ref[0:1, :]
    first = row_ref[1:2, :]
    offset = lax.broadcasted_iota(jnp.int32, (RUN, wide), 0).astype(jnp.float32)

    def scores(s, top):
        here = here_ref[s, 0:rows, :]
        there = there_ref[s, 0:rows, :]
        key = jnp.where(is_key, here, there)
        value = jnp.where(is_key, there, here)
        score = dot(key, query, ((1,), (1,))) * inv_root
        dp_ref[s] = dot(value, grad, ((1,), (1,)))
        meta = here_ref[s, rows : rows + META_ROWS, :].astype(jnp.float32)
        for run in range(rows // RUN):
            start = meta[run : run + 1, 0:1] * float(RUN)
            pos = offset + start
            allowed = (pos <= last) & (pos >= first)
            part = jnp.where(allowed, score[run * RUN : (run + 1) * RUN], -1e30)
            s_ref[s, run * RUN : (run + 1) * RUN, :] = part
            top = jnp.maximum(top, jnp.max(part, axis=0, keepdims=True))
        return top

    top = each(count, scores, jnp.full((1, wide), -1e30, jnp.float32))

    def weights(s, state):
        total, mixed = state
        weight = jnp.exp(s_ref[s] - top)
        s_ref[s] = weight
        total = total + jnp.sum(weight, axis=0, keepdims=True)
        mixed = mixed + jnp.sum(weight * dp_ref[s], axis=0, keepdims=True)
        return total, mixed

    zeros = jnp.zeros((1, wide), jnp.float32)
    total, mixed = each(count, weights, (zeros, zeros))
    scale = 1.0 / total
    delta = mixed * scale

    other = jnp.where(is_key, query, grad)

    def gradients(s, dq):
        prob = s_ref[s] * scale
        dscore = (prob * (dp_ref[s] - delta)).astype(jnp.bfloat16)
        picked = jnp.where(is_key, dscore, prob.astype(jnp.bfloat16))
        back_ref[s] = dot(picked, other, ((1,), (0,))).astype(jnp.bfloat16)
        key = jnp.where(is_key, here_ref[s, 0:rows, :], there_ref[s, 0:rows, :])
        return dq + dot(key, dscore, ((0,), (0,)))

    dq = each(count, gradients, jnp.zeros((size, wide), jnp.float32)) * inv_root
    for part in range(wide // rows):
        block = dq[:, part * rows : (part + 1) * rows]
        dq_ref[:, part * size : (part + 1) * size] = block.T.astype(jnp.bfloat16)


def attention(core, row_info, q_mine, q_other, g_mine, g_other, here, there):
    count, _, size = here.shape
    rows, width = q_mine.shape
    wide = 2 * rows * (width // size)
    return pl.pallas_call(
        attention_kernel,
        out_shape=[
            jax.ShapeDtypeStruct((rows, 2 * width), jnp.bfloat16),
            jax.ShapeDtypeStruct((count, rows, size), jnp.bfloat16),
        ],
        in_specs=[SMEM] + [pl.BlockSpec()] * 7,
        out_specs=[pl.BlockSpec()] * 2,
        scratch_shapes=[pltpu.VMEM((count, rows, wide), jnp.float32)] * 2,
        compiler_params=params(8 + count * rows * wide // 2**17),
        cost_estimate=pl.CostEstimate(
            flops=10 * count * rows * wide * size,
            bytes_accessed=count * rows * size * 8,
            transcendentals=count * rows * wide,
        ),
        name="attention",
    )(core, row_info, q_mine, q_other, g_mine, g_other, here, there)


def product_kernel(first, dq_ref, wm_ref, wo_ref, out_ref):
    depth = wm_ref.shape[0]
    at = slice(first, first + out_ref.shape[1])
    acc = dot(dq_ref[:, 0:depth], wm_ref[:, at], ((1,), (0,)))
    acc = acc + dot(dq_ref[:, depth:], wo_ref[:, at], ((1,), (0,)))
    out_ref[...] = acc.astype(out_ref.dtype)


def product(dq, w_mine, w_other, first, width, dtype):
    rows, depth = dq.shape
    return pl.pallas_call(
        functools.partial(product_kernel, first),
        out_shape=jax.ShapeDtypeStruct((rows, width), dtype),
        in_specs=[pl.BlockSpec()] * 3,
        out_specs=pl.BlockSpec(),
        compiler_params=params(16),
        cost_estimate=pl.CostEstimate(
            flops=2 * rows * depth * width, bytes_accessed=2 * depth * width, transcendentals=0
        ),
        name="product",
    )(dq, w_mine, w_other)


def finish_kernel(starts, core_ref, mine_ref, other_ref, w_ref, acc_ref, *refs):
    early = len(starts) - 2
    out_ref, left_ref = refs[early:]
    inv_root = 1.0 / math.sqrt(mine_ref.shape[1])
    size = mine_ref.shape[1]
    is_key = core_ref[0] == 0
    wm_ref = w_ref.at[pl.ds(pl.multiple_of(core_ref[0] * size, size), size), :]
    wo_ref = w_ref.at[pl.ds(pl.multiple_of((1 - core_ref[0]) * size, size), size), :]
    mine = (mine_ref[...] * jnp.where(is_key, inv_root, 1.0)).astype(jnp.bfloat16)
    other = (other_ref[...] * jnp.where(is_key, 1.0, inv_root)).astype(jnp.bfloat16)
    for c in range(early + 1):
        at = slice(starts[c], starts[c + 1])
        acc = acc_ref[:, at] + dot(mine, wm_ref[:, at], ((1,), (0,))) + dot(other, wo_ref[:, at], ((1,), (0,)))
        if c < early:
            out_ref[:, at] = (acc + refs[c][...].astype(jnp.float32)).astype(jnp.bfloat16)
        else:
            left_ref[...] = acc


def finish(core, mine, other, w_kv, acc, received, starts):
    rows, share = acc.shape
    size = mine.shape[1]
    last = starts[-2]
    return pl.pallas_call(
        functools.partial(finish_kernel, starts),
        out_shape=[
            jax.ShapeDtypeStruct((rows, share), jnp.bfloat16),
            jax.ShapeDtypeStruct((rows, share - last), jnp.float32),
        ],
        grid=(1,),
        in_specs=[SMEM] + [pl.BlockSpec()] * (4 + len(received)),
        out_specs=[
            pl.BlockSpec((rows, last), lambda i: (0, 0)),
            pl.BlockSpec((rows, share - last), lambda i: (0, 0)),
        ],
        compiler_params=params(),
        cost_estimate=pl.CostEstimate(
            flops=4 * rows * size * share, bytes_accessed=10 * rows * share, transcendentals=0
        ),
        name="finish",
    )(core, mine, other, w_kv, acc, *received)


def last_kernel(left_ref, part_ref, held_ref, out_ref, sum_ref, sem):
    sum_ref[...] = (left_ref[...] + part_ref[...].astype(jnp.float32)).astype(jnp.bfloat16)
    first = out_ref.shape[1] - sum_ref.shape[1]
    copy = pltpu.make_async_copy(sum_ref, out_ref.at[:, first:], sem)
    copy.start()
    copy.wait()


def last(left, part, held):
    return pl.pallas_call(
        last_kernel,
        out_shape=jax.ShapeDtypeStruct(held.shape, held.dtype),
        in_specs=[pl.BlockSpec(), pl.BlockSpec(), ANY],
        out_specs=ANY,
        input_output_aliases={2: 0},
        scratch_shapes=[pltpu.VMEM(part.shape, held.dtype), pltpu.SemaphoreType.DMA(())],
        compiler_params=params(),
        name="last",
    )(left, part, held)


def on_device(queries, keys, values, dout, positions, doc_ids, w_query, w_kv):
    count = lax.axis_size("ctx")
    head = lax.axis_index("head").astype(jnp.int32)
    core = (head & 1).reshape(1)
    share = w_kv.shape[1]

    here = lax.all_to_all(pack(count, core, positions, keys, values), "ctx", 0, 0)
    q_other = swapped(queries, "head", 1)
    g_other = swapped(dout, "head", 1)
    blocks = carve([head ^ 3, head ^ 1, head ^ 2, head], w_query, q_other, share)
    here, far_send, near_send, far_mine, near_mine = lax.optimization_barrier([here, *blocks])
    there, far_send = lax.optimization_barrier((swapped(here, "head", 1), far_send))
    far_other = swapped(far_send, "head", 1)

    bounds = jnp.stack([positions, doc_ids * RUN]).astype(jnp.float32)
    row_info = jnp.tile(bounds, (1, 2 * (queries.shape[1] // keys.shape[1])))
    dq, back = attention(core, row_info, queries, q_other, dout, g_other, here, there)

    dq, near_send = lax.optimization_barrier((dq, near_send))
    near_other = swapped(near_send, "head", 1)
    starts = [0]
    for units in CHUNKS:
        starts.append(starts[-1] + units * (share // sum(CHUNKS)))
    parts = [
        product(dq, far_mine, far_other, low, high - low, jnp.bfloat16) for low, high in zip(starts, starts[1:])
    ]
    received = [swapped(part, "head", 2) for part in parts[:-1]]
    back, *_ = lax.optimization_barrier([back, received[0]] + parts)
    back = lax.all_to_all(back, "ctx", 0, 0)
    mine = jnp.sum(back.astype(jnp.float32), axis=0).astype(jnp.bfloat16)
    mine, part = lax.optimization_barrier((mine, parts[-1]))
    mine = mine.astype(jnp.float32) + swapped(mine, "head", 2).astype(jnp.float32)
    received.append(swapped(part, "head", 2))
    other = swapped(mine.astype(jnp.bfloat16), "head", 1).astype(jnp.float32)

    acc = product(dq, near_mine, near_other, 0, share, jnp.float32)
    held, left = finish(core, mine, other, w_kv, acc, received[:-1], starts)
    return last(left, received[-1], held)


def solution(mesh):
    placed = (
        P("ctx", "head"),
        P("ctx", None),
        P("ctx", None),
        P("ctx", "head"),
        P("ctx"),
        P("ctx"),
        P("head", None),
        P(None, "head"),
    )
    return jax.shard_map(
        on_device, mesh=mesh, in_specs=placed, out_specs=P("ctx", "head"), check_vma=False
    )
```

```python
import functools
import math

import jax
import jax.numpy as jnp
from jax import lax
from jax.experimental import pallas as pl
from jax.experimental.pallas import tpu as pltpu
from jax.sharding import PartitionSpec as P

RUN = 64
META_ROWS = 16
CHUNKS = (2, 3, 3, 3, 3, 2)
ANY = pl.BlockSpec(memory_space=pl.ANY)
HBM = pl.BlockSpec(memory_space=pltpu.HBM)
SMEM = pl.BlockSpec(memory_space=pltpu.SMEM)


def params(limit_mib=16):
    return pltpu.CompilerParams(vmem_limit_bytes=limit_mib * 1024 * 1024)


def swapped(value, axis, bits):
    count = lax.axis_size(axis)
    return lax.ppermute(value, axis, [(source, source ^ bits) for source in range(count)])


def dot(a, b, contract):
    return lax.dot_general(a, b, (contract, ((), ())), preferred_element_type=jnp.float32)


def each(count, body, state):
    if count > 8:
        return lax.fori_loop(0, count, body, state)
    for step in range(count):
        state = body(step, state)
    return state


def pack(core, positions, keys, values):
    rows, size = keys.shape
    held = jnp.where(core == 0, keys, values)
    runs = (positions.reshape(rows // RUN, RUN)[:, :1] // RUN).astype(jnp.bfloat16)
    meta = jnp.pad(jnp.broadcast_to(runs, (rows // RUN, size)), ((0, META_ROWS - rows // RUN), (0, 0)))
    return jnp.concatenate([held, meta], axis=0)


def gate_kernel(value_ref, *refs):
    pass


def gate(value, *after):
    return pl.pallas_call(
        gate_kernel,
        out_shape=jax.ShapeDtypeStruct(value.shape, value.dtype),
        in_specs=[ANY] * (1 + len(after)),
        out_specs=ANY,
        input_output_aliases={0: 0},
        compiler_params=params(),
        cost_estimate=pl.CostEstimate(flops=10**11, bytes_accessed=10**8, transcendentals=0),
        name="gate",
    )(value, *after)


def carve_kernel(block_ref, w_ref, *refs):
    outs, sems = refs[1:-1], refs[-1]
    rows, share = outs[0].shape
    parts = sems.shape[1]
    copies = []
    for i, out_ref in enumerate(outs):
        at = pl.multiple_of(block_ref[i] * share, share)
        for j in range(parts):
            part = slice(j * (rows // parts), (j + 1) * (rows // parts))
            source = w_ref.at[part, pl.ds(at, share)]
            copies.append(pltpu.make_async_copy(source, out_ref.at[part, :], sems.at[i, j]))
            copies[-1].start()
    for one in copies:
        one.wait()


def carve(blocks, w_query, share, after):
    block = jax.ShapeDtypeStruct((w_query.shape[0], share), w_query.dtype)
    count = len(blocks)
    return pl.pallas_call(
        carve_kernel,
        out_shape=[block] * count,
        in_specs=[SMEM, HBM, ANY],
        out_specs=[pl.BlockSpec(memory_space=pltpu.VMEM)] * count,
        scratch_shapes=[pltpu.SemaphoreType.DMA((count, 4))],
        compiler_params=params(48),
        cost_estimate=pl.CostEstimate(
            flops=0, bytes_accessed=4 * count * w_query.shape[0] * share, transcendentals=0
        ),
        name="carve",
    )(jnp.stack(blocks), w_query, after)


def attention_kernel(core_ref, row_ref, query_ref, grad_ref, *refs):
    groups = ((refs[0], refs[1], refs[5]), (refs[2], refs[3], refs[6]))
    dq_ref = refs[4]
    s_ref, dp_ref = refs[7:]
    half, rows, size = groups[0][2].shape
    is_key = core_ref[0] == 0
    inv_root = 1.0 / math.sqrt(size)
    query = query_ref[...]
    grad = grad_ref[...]
    wide = query.shape[0]
    last = row_ref[0:1, :]
    first = row_ref[1:2, :]
    offset = lax.broadcasted_iota(jnp.int32, (RUN, wide), 0).astype(jnp.float32)

    def everywhere(body, state):
        for group, (here_ref, there_ref, back_ref) in enumerate(groups):
            state = each(
                half, lambda s, now: body(s, group * half + s, here_ref, there_ref, back_ref, now), state
            )
        return state

    def scores(s, slot, here_ref, there_ref, back_ref, top):
        here = here_ref[s, 0:rows, :]
        there = there_ref[s, 0:rows, :]
        key = jnp.where(is_key, here, there)
        value = jnp.where(is_key, there, here)
        score = dot(key, query, ((1,), (1,))) * inv_root
        dp_ref[slot] = dot(value, grad, ((1,), (1,)))
        meta = here_ref[s, rows : rows + META_ROWS, :].astype(jnp.float32)
        for run in range(rows // RUN):
            start = meta[run : run + 1, 0:1] * float(RUN)
            pos = offset + start
            allowed = (pos <= last) & (pos >= first)
            part = jnp.where(allowed, score[run * RUN : (run + 1) * RUN], -1e30)
            s_ref[slot, run * RUN : (run + 1) * RUN, :] = part
            top = jnp.maximum(top, jnp.max(part, axis=0, keepdims=True))
        return top

    top = everywhere(scores, jnp.full((1, wide), -1e30, jnp.float32))

    def weights(slot, state):
        total, mixed = state
        weight = jnp.exp(s_ref[slot] - top)
        s_ref[slot] = weight
        total = total + jnp.sum(weight, axis=0, keepdims=True)
        mixed = mixed + jnp.sum(weight * dp_ref[slot], axis=0, keepdims=True)
        return total, mixed

    zeros = jnp.zeros((1, wide), jnp.float32)
    total, mixed = each(2 * half, weights, (zeros, zeros))
    scale = 1.0 / total
    delta = mixed * scale
    other = jnp.where(is_key, query, grad)

    def gradients(s, slot, here_ref, there_ref, back_ref, dq):
        prob = s_ref[slot] * scale
        dscore = (prob * (dp_ref[slot] - delta)).astype(jnp.bfloat16)
        picked = jnp.where(is_key, dscore, prob.astype(jnp.bfloat16))
        back_ref[s] = dot(picked, other, ((1,), (0,))).astype(jnp.bfloat16)
        key = jnp.where(is_key, here_ref[s, 0:rows, :], there_ref[s, 0:rows, :])
        return dq + dot(key, dscore, ((0,), (0,)))

    dq = everywhere(gradients, jnp.zeros((size, wide), jnp.float32)) * inv_root
    for part in range(wide // rows):
        block = dq[:, part * rows : (part + 1) * rows]
        dq_ref[:, part * size : (part + 1) * size] = block.T.astype(jnp.bfloat16)


def attention(core, row_info, query, grad, pieces, rows):
    half, _, size = pieces[0].shape
    wide = query.shape[0]
    count = 2 * half
    return pl.pallas_call(
        attention_kernel,
        out_shape=[jax.ShapeDtypeStruct((rows, wide // rows * size), jnp.bfloat16)]
        + [jax.ShapeDtypeStruct((half, rows, size), jnp.bfloat16)] * 2,
        in_specs=[SMEM] + [pl.BlockSpec()] * 7,
        out_specs=[pl.BlockSpec()] * 3,
        scratch_shapes=[pltpu.VMEM((count, rows, wide), jnp.float32)] * 2,
        compiler_params=params(8 + count * rows * wide // 2**17),
        cost_estimate=pl.CostEstimate(
            flops=10 * count * rows * wide * size,
            bytes_accessed=count * rows * size * 8,
            transcendentals=count * rows * wide,
        ),
        name="attention",
    )(core, row_info, query, grad, *pieces)


def product_kernel(first, dq_ref, wm_ref, wo_ref, out_ref):
    depth = wm_ref.shape[0]
    at = slice(first, first + out_ref.shape[1])
    acc = dot(dq_ref[:, 0:depth], wm_ref[:, at], ((1,), (0,)))
    acc = acc + dot(dq_ref[:, depth:], wo_ref[:, at], ((1,), (0,)))
    out_ref[...] = acc.astype(out_ref.dtype)


def product(dq, w_mine, w_other, first, width, dtype):
    rows, depth = dq.shape
    return pl.pallas_call(
        functools.partial(product_kernel, first),
        out_shape=jax.ShapeDtypeStruct((rows, width), dtype),
        in_specs=[pl.BlockSpec()] * 3,
        out_specs=pl.BlockSpec(),
        compiler_params=params(16),
        cost_estimate=pl.CostEstimate(
            flops=2 * rows * depth * width, bytes_accessed=2 * depth * width, transcendentals=0
        ),
        name="product",
    )(dq, w_mine, w_other)


def finish_kernel(starts, core_ref, mine_ref, other_ref, w_ref, acc_ref, *refs):
    early = len(starts) - 2
    out_ref, left_ref = refs[early:]
    inv_root = 1.0 / math.sqrt(mine_ref.shape[1])
    size = mine_ref.shape[1]
    is_key = core_ref[0] == 0
    wm_ref = w_ref.at[pl.ds(pl.multiple_of(core_ref[0] * size, size), size), :]
    wo_ref = w_ref.at[pl.ds(pl.multiple_of((1 - core_ref[0]) * size, size), size), :]
    mine = (mine_ref[...] * jnp.where(is_key, inv_root, 1.0)).astype(jnp.bfloat16)
    other = (other_ref[...] * jnp.where(is_key, 1.0, inv_root)).astype(jnp.bfloat16)
    for c in range(early + 1):
        at = slice(starts[c], starts[c + 1])
        acc = acc_ref[:, at] + dot(mine, wm_ref[:, at], ((1,), (0,))) + dot(other, wo_ref[:, at], ((1,), (0,)))
        if c < early:
            out_ref[:, at] = (acc + refs[c][...].astype(jnp.float32)).astype(jnp.bfloat16)
        else:
            left_ref[...] = acc


def finish(core, mine, other, w_kv, acc, received, starts):
    rows, share = acc.shape
    size = mine.shape[1]
    last = starts[-2]
    return pl.pallas_call(
        functools.partial(finish_kernel, starts),
        out_shape=[
            jax.ShapeDtypeStruct((rows, share), jnp.bfloat16),
            jax.ShapeDtypeStruct((rows, share - last), jnp.float32),
        ],
        grid=(1,),
        in_specs=[SMEM] + [pl.BlockSpec()] * (4 + len(received)),
        out_specs=[
            pl.BlockSpec((rows, last), lambda i: (0, 0)),
            pl.BlockSpec((rows, share - last), lambda i: (0, 0)),
        ],
        compiler_params=params(),
        cost_estimate=pl.CostEstimate(
            flops=4 * rows * size * share, bytes_accessed=10 * rows * share, transcendentals=0
        ),
        name="finish",
    )(core, mine, other, w_kv, acc, *received)


def last_kernel(left_ref, part_ref, held_ref, out_ref, sum_ref, sem):
    sum_ref[...] = (left_ref[...] + part_ref[...].astype(jnp.float32)).astype(jnp.bfloat16)
    first = out_ref.shape[1] - sum_ref.shape[1]
    copy = pltpu.make_async_copy(sum_ref, out_ref.at[:, first:], sem)
    copy.start()
    copy.wait()


def last(left, part, held):
    return pl.pallas_call(
        last_kernel,
        out_shape=jax.ShapeDtypeStruct(held.shape, held.dtype),
        in_specs=[pl.BlockSpec(), pl.BlockSpec(), ANY],
        out_specs=ANY,
        input_output_aliases={2: 0},
        scratch_shapes=[pltpu.VMEM(part.shape, held.dtype), pltpu.SemaphoreType.DMA(())],
        compiler_params=params(),
        name="last",
    )(left, part, held)


def on_device(queries, keys, values, dout, positions, doc_ids, w_query, w_kv):
    half = lax.axis_size("ctx") // 2
    head = lax.axis_index("head").astype(jnp.int32)
    core = (head & 1).reshape(1)
    share = w_kv.shape[1]
    local_heads = queries.shape[1] // keys.shape[1]

    piece = pack(core, positions, keys, values)
    here_z = jnp.stack([piece] + [swapped(piece, "ctx", 2 * s) for s in range(1, half)])
    q_other = swapped(queries, "head", 1)
    g_other = swapped(dout, "head", 1)
    q_other = gate(q_other, g_other)
    far_send, far_mine = carve([head ^ 3, head ^ 2], w_query, share, q_other)
    far_other = swapped(far_send, "head", 1)

    def stacked(*arrays):
        return jnp.concatenate([part for one in arrays for part in jnp.split(one, local_heads, axis=1)], axis=0)

    query = stacked(queries, q_other)
    grad = stacked(dout, g_other)
    bounds = jnp.stack([positions, doc_ids * RUN]).astype(jnp.float32)
    row_info = jnp.tile(bounds, (1, 2 * local_heads))
    here_z, far_mine, query, grad, row_info = lax.optimization_barrier(
        (here_z, far_mine, query, grad, row_info)
    )
    here_x = swapped(here_z, "ctx", 1)
    there_z = swapped(here_z, "head", 1)
    there_x = swapped(here_x, "head", 1)
    dq, back_z, back_x = attention(
        core, row_info, query, grad, (here_z, there_z, here_x, there_x), queries.shape[0]
    )

    starts = [0]
    for units in CHUNKS:
        starts.append(starts[-1] + units * (share // sum(CHUNKS)))
    parts = [
        product(dq, far_mine, far_other, low, high - low, jnp.bfloat16) for low, high in zip(starts, starts[1:])
    ]
    received = []
    for c, part in enumerate(parts):
        if c >= 2:
            part, received[c - 2] = lax.optimization_barrier((part, received[c - 2]))
        received.append(swapped(part, "head", 2))

    back_x, back_z, *_ = lax.optimization_barrier((back_x, back_z, *parts[:2]))
    pair = back_z.astype(jnp.float32) + swapped(back_x, "ctx", 1).astype(jnp.float32)
    mine = pair[0]
    for s in range(1, half):
        mine = mine + swapped(pair[s].astype(jnp.bfloat16), "ctx", 2 * s).astype(jnp.float32)
    mine = mine.astype(jnp.bfloat16)

    near_send, near_mine = carve([head ^ 1, head], w_query, share, received[0])
    acc = product(dq, near_mine, swapped(near_send, "head", 1), 0, share, jnp.float32)
    mine, acc = lax.optimization_barrier((mine, acc))
    mine = mine.astype(jnp.float32) + swapped(mine, "head", 2).astype(jnp.float32)
    other = swapped(mine.astype(jnp.bfloat16), "head", 1).astype(jnp.float32)

    held, left = finish(core, mine, other, w_kv, acc, received[:-1], starts)
    return last(left, received[-1], held)


def solution(mesh):
    placed = (
        P("ctx", "head"),
        P("ctx", None),
        P("ctx", None),
        P("ctx", "head"),
        P("ctx"),
        P("ctx"),
        P("head", None),
        P(None, "head"),
    )
    return jax.shard_map(
        on_device, mesh=mesh, in_specs=placed, out_specs=P("ctx", "head"), check_vma=False
    )
```

```python
import functools
import math

import jax
import jax.numpy as jnp
from jax import lax
from jax.experimental import pallas as pl
from jax.experimental.pallas import tpu as pltpu
from jax.sharding import PartitionSpec as P

RUN = 64
META_ROWS = 16
CHUNKS = (13, 3)
TILES = 4
ANY = pl.BlockSpec(memory_space=pl.ANY)
HBM = pl.BlockSpec(memory_space=pltpu.HBM)
SMEM = pl.BlockSpec(memory_space=pltpu.SMEM)


def params(limit_mib=16):
    return pltpu.CompilerParams(vmem_limit_bytes=limit_mib * 1024 * 1024)


def swapped(value, axis, bits):
    count = lax.axis_size(axis)
    return lax.ppermute(value, axis, [(source, source ^ bits) for source in range(count)])


def dot(a, b, contract):
    return lax.dot_general(a, b, (contract, ((), ())), preferred_element_type=jnp.float32)


def each(count, body, state):
    if count > 8:
        return lax.fori_loop(0, count, body, state)
    for step in range(count):
        state = body(step, state)
    return state


def pack(core, positions, keys, values):
    rows, size = keys.shape
    held = jnp.where(core == 0, keys, values)
    runs = (positions.reshape(rows // RUN, RUN)[:, :1] // RUN).astype(jnp.bfloat16)
    meta = jnp.pad(jnp.broadcast_to(runs, (rows // RUN, size)), ((0, META_ROWS - rows // RUN), (0, 0)))
    return jnp.concatenate([held, meta], axis=0)


def carve_kernel(block_ref, w_ref, *refs):
    outs, sems = refs[1:-1], refs[-1]
    rows, share = outs[0].shape
    parts = sems.shape[1]
    copies = []
    for i, out_ref in enumerate(outs):
        at = pl.multiple_of(block_ref[i] * share, share)
        for j in range(parts):
            part = slice(j * (rows // parts), (j + 1) * (rows // parts))
            source = w_ref.at[part, pl.ds(at, share)]
            copies.append(pltpu.make_async_copy(source, out_ref.at[part, :], sems.at[i, j]))
            copies[-1].start()
    for one in copies:
        one.wait()


def carve(blocks, w_query, share, after):
    block = jax.ShapeDtypeStruct((w_query.shape[0], share), w_query.dtype)
    count = len(blocks)
    return pl.pallas_call(
        carve_kernel,
        out_shape=[block] * count,
        in_specs=[SMEM, HBM, ANY],
        out_specs=[pl.BlockSpec(memory_space=pltpu.VMEM)] * count,
        scratch_shapes=[pltpu.SemaphoreType.DMA((count, 4))],
        compiler_params=params(48),
        cost_estimate=pl.CostEstimate(
            flops=0, bytes_accessed=4 * count * w_query.shape[0] * share, transcendentals=0
        ),
        name="carve",
    )(jnp.stack(blocks), w_query, after)


def attention_kernel(core_ref, row_ref, query_ref, grad_ref, *refs):
    groups = ((refs[0], refs[1], refs[5]), (refs[2], refs[3], refs[6]))
    dq_ref = refs[4]
    s_ref, dp_ref = refs[7:]
    half, rows, size = groups[0][2].shape
    is_key = core_ref[0] == 0
    inv_root = 1.0 / math.sqrt(size)
    query = query_ref[...]
    grad = grad_ref[...]
    wide = query.shape[0]
    last = row_ref[0:1, :]
    first = row_ref[1:2, :]
    offset = lax.broadcasted_iota(jnp.int32, (RUN, wide), 0).astype(jnp.float32)

    def everywhere(body, state):
        for group, (here_ref, there_ref, back_ref) in enumerate(groups):
            state = each(
                half, lambda s, now: body(s, group * half + s, here_ref, there_ref, back_ref, now), state
            )
        return state

    def scores(s, slot, here_ref, there_ref, back_ref, top):
        here = here_ref[s, 0:rows, :]
        there = there_ref[s, 0:rows, :]
        key = jnp.where(is_key, here, there)
        value = jnp.where(is_key, there, here)
        score = dot(key, query, ((1,), (1,))) * inv_root
        dp_ref[slot] = dot(value, grad, ((1,), (1,)))
        meta = here_ref[s, rows : rows + META_ROWS, :].astype(jnp.float32)
        for run in range(rows // RUN):
            start = meta[run : run + 1, 0:1] * float(RUN)
            pos = offset + start
            allowed = (pos <= last) & (pos >= first)
            part = jnp.where(allowed, score[run * RUN : (run + 1) * RUN], -1e30)
            s_ref[slot, run * RUN : (run + 1) * RUN, :] = part
            top = jnp.maximum(top, jnp.max(part, axis=0, keepdims=True))
        return top

    top = everywhere(scores, jnp.full((1, wide), -1e30, jnp.float32))

    def weights(slot, state):
        total, mixed = state
        weight = jnp.exp(s_ref[slot] - top)
        s_ref[slot] = weight
        total = total + jnp.sum(weight, axis=0, keepdims=True)
        mixed = mixed + jnp.sum(weight * dp_ref[slot], axis=0, keepdims=True)
        return total, mixed

    zeros = jnp.zeros((1, wide), jnp.float32)
    total, mixed = each(2 * half, weights, (zeros, zeros))
    scale = 1.0 / total
    delta = mixed * scale
    other = jnp.where(is_key, query, grad)

    def gradients(s, slot, here_ref, there_ref, back_ref, dq):
        prob = s_ref[slot] * scale
        dscore = (prob * (dp_ref[slot] - delta)).astype(jnp.bfloat16)
        picked = jnp.where(is_key, dscore, prob.astype(jnp.bfloat16))
        back_ref[s] = dot(picked, other, ((1,), (0,))).astype(jnp.bfloat16)
        key = jnp.where(is_key, here_ref[s, 0:rows, :], there_ref[s, 0:rows, :])
        return dq + dot(key, dscore, ((0,), (0,)))

    dq = everywhere(gradients, jnp.zeros((size, wide), jnp.float32)) * inv_root
    for part in range(wide // rows):
        block = dq[:, part * rows : (part + 1) * rows]
        dq_ref[:, part * size : (part + 1) * size] = block.T.astype(jnp.bfloat16)


def attention(core, row_info, query, grad, pieces, rows):
    half, _, size = pieces[0].shape
    wide = query.shape[0]
    count = 2 * half
    return pl.pallas_call(
        attention_kernel,
        out_shape=[jax.ShapeDtypeStruct((rows, wide // rows * size), jnp.bfloat16)]
        + [jax.ShapeDtypeStruct((half, rows, size), jnp.bfloat16)] * 2,
        in_specs=[SMEM] + [pl.BlockSpec()] * 7,
        out_specs=[pl.BlockSpec()] * 3,
        scratch_shapes=[pltpu.VMEM((count, rows, wide), jnp.float32)] * 2,
        compiler_params=params(8 + count * rows * wide // 2**17),
        cost_estimate=pl.CostEstimate(
            flops=10 * count * rows * wide * size,
            bytes_accessed=count * rows * size * 8,
            transcendentals=count * rows * wide,
        ),
        name="attention",
    )(core, row_info, query, grad, *pieces)


def product_kernel(first, dq_ref, wm_ref, wo_ref, out_ref):
    depth = wm_ref.shape[0]
    at = slice(first, first + out_ref.shape[1])
    acc = dot(dq_ref[:, 0:depth], wm_ref[:, at], ((1,), (0,)))
    acc = acc + dot(dq_ref[:, depth:], wo_ref[:, at], ((1,), (0,)))
    out_ref[...] = acc.astype(out_ref.dtype)


def product(dq, w_mine, w_other, first, width, dtype):
    rows, depth = dq.shape
    return pl.pallas_call(
        functools.partial(product_kernel, first),
        out_shape=jax.ShapeDtypeStruct((rows, width), dtype),
        in_specs=[pl.BlockSpec()] * 3,
        out_specs=pl.BlockSpec(),
        compiler_params=params(16),
        cost_estimate=pl.CostEstimate(
            flops=2 * rows * depth * width, bytes_accessed=2 * depth * width, transcendentals=0
        ),
        name="product",
    )(dq, w_mine, w_other)


def finish_kernel(core_ref, kv_ref, w_ref, acc_ref, first_ref, second_ref, out_ref, hold_ref, sems):
    rows, share = acc_ref.shape
    pair = kv_ref.shape[1]
    size = pair // 2
    cut = first_ref.shape[1]
    tile = share // TILES
    inv_root = 1.0 / math.sqrt(size)
    column = lax.broadcasted_iota(jnp.int32, (1, pair), 1)
    is_key = (column < size) == (core_ref[0] == 0)
    kv = kv_ref[...].astype(jnp.float32) + second_ref[:, share - cut :].astype(jnp.float32)
    kv = (kv * jnp.where(is_key, inv_root, 1.0)).astype(jnp.bfloat16)
    at_mine = pl.ds(pl.multiple_of(core_ref[0] * size, size), size)
    at_other = pl.ds(pl.multiple_of((1 - core_ref[0]) * size, size), size)
    copies = []
    for i in range(TILES):
        low, high = i * tile, (i + 1) * tile
        w = jnp.concatenate([w_ref[at_mine, low:high], w_ref[at_other, low:high]], axis=0)
        acc = acc_ref[:, low:high] + dot(kv, w, ((1,), (0,)))
        come = []
        if low < cut:
            come.append(first_ref[:, low : min(high, cut)])
        if high > cut:
            come.append(second_ref[:, max(low, cut) - cut : high - cut])
        acc = acc + jnp.concatenate(come, axis=1).astype(jnp.float32)
        hold_ref[:, low:high] = acc.astype(jnp.bfloat16)
        copies.append(pltpu.make_async_copy(hold_ref.at[:, low:high], out_ref.at[:, low:high], sems.at[i]))
        copies[i].start()
    for one in copies:
        one.wait()


def finish(core, kv, w_kv, acc, first, second):
    rows, share = acc.shape
    return pl.pallas_call(
        finish_kernel,
        out_shape=jax.ShapeDtypeStruct((rows, share), jnp.bfloat16),
        in_specs=[SMEM] + [pl.BlockSpec()] * 5,
        out_specs=ANY,
        scratch_shapes=[pltpu.VMEM((rows, share), jnp.bfloat16), pltpu.SemaphoreType.DMA((TILES,))],
        compiler_params=params(),
        cost_estimate=pl.CostEstimate(
            flops=2 * rows * kv.shape[1] * share, bytes_accessed=10 * rows * share, transcendentals=0
        ),
        name="finish",
    )(core, kv, w_kv, acc, first, second)


def on_device(queries, keys, values, dout, positions, doc_ids, w_query, w_kv):
    half = lax.axis_size("ctx") // 2
    head = lax.axis_index("head").astype(jnp.int32)
    core = (head & 1).reshape(1)
    share = w_kv.shape[1]
    local_heads = queries.shape[1] // keys.shape[1]

    q_other = swapped(queries, "head", 1)
    g_other = swapped(dout, "head", 1)
    piece = pack(core, positions, keys, values)
    along_z = [piece] + [swapped(piece, "ctx", 2 * s) for s in range(1, half)]

    def stacked(*arrays):
        return jnp.concatenate([part for one in arrays for part in jnp.split(one, local_heads, axis=1)], axis=0)

    query = stacked(queries, q_other)
    grad = stacked(dout, g_other)
    bounds = jnp.stack([positions, doc_ids * RUN]).astype(jnp.float32)
    row_info = jnp.tile(bounds, (1, 2 * local_heads))
    far = carve([head ^ 3, head ^ 2], w_query, share, positions)
    here_z, query, grad, row_info, far_send, far_mine = lax.optimization_barrier(
        (jnp.stack(along_z), query, grad, row_info, *far)
    )
    here_x = swapped(here_z, "ctx", 1)
    far_other = swapped(far_send, "head", 1)
    there_z = swapped(here_z, "head", 1)
    near = carve([head ^ 1, head], w_query, share, here_z)
    here_x, near_send, near_mine = lax.optimization_barrier((here_x, *near))
    there_x = swapped(here_x, "head", 1)
    dq, back_z, back_x = attention(
        core, row_info, query, grad, (here_z, there_z, here_x, there_x), queries.shape[0]
    )

    cut = CHUNKS[0] * (share // sum(CHUNKS))
    first_part = product(dq, far_mine, far_other, 0, cut, jnp.bfloat16)
    second_part = product(dq, far_mine, far_other, cut, share - cut, jnp.bfloat16)
    first = swapped(first_part, "head", 2)
    dq, near_send = lax.optimization_barrier((dq, near_send))
    near_other = swapped(near_send, "head", 1)

    def exchange(trip, kv):
        sent = lax.dynamic_slice_in_dim(back_x, trip * half, half, axis=0)
        pair = back_z.astype(jnp.float32) + swapped(sent, "ctx", 1).astype(jnp.float32)
        mine = pair[0]
        for s in range(1, half):
            mine = mine + swapped(pair[s].astype(jnp.bfloat16), "ctx", 2 * s).astype(jnp.float32)
        mine = mine.astype(jnp.bfloat16)
        return jnp.concatenate([mine, swapped(mine, "head", 1)], axis=1)

    back_x, back_z, first_part, second_part = lax.optimization_barrier((back_x, back_z, first_part, second_part))
    trips = 1 + jnp.minimum(positions[0], 0)
    kv = lax.fori_loop(0, trips, exchange, jnp.zeros((queries.shape[0], 2 * keys.shape[1]), jnp.bfloat16))

    second_part = jnp.concatenate([second_part, kv], axis=1)
    second_part, first, near_mine = lax.optimization_barrier((second_part, first, near_mine))
    second = swapped(second_part, "head", 2)
    acc = product(dq, near_mine, near_other, 0, share, jnp.float32)
    return finish(core, kv, w_kv, acc, first, second)


def solution(mesh):
    placed = (
        P("ctx", "head"),
        P("ctx", None),
        P("ctx", None),
        P("ctx", "head"),
        P("ctx"),
        P("ctx"),
        P("head", None),
        P(None, "head"),
    )
    return jax.shard_map(
        on_device, mesh=mesh, in_specs=placed, out_specs=P("ctx", "head"), check_vma=False
    )
```

```python
import functools
import math

import jax
import jax.numpy as jnp
from jax import lax
from jax.experimental import pallas as pl
from jax.experimental.pallas import tpu as pltpu
from jax.sharding import PartitionSpec as P

RUN = 64
META_ROWS = 16
CHUNKS = (13, 3)
TILES = 4
ANY = pl.BlockSpec(memory_space=pl.ANY)
HBM = pl.BlockSpec(memory_space=pltpu.HBM)
SMEM = pl.BlockSpec(memory_space=pltpu.SMEM)


def params(limit_mib=16):
    return pltpu.CompilerParams(vmem_limit_bytes=limit_mib * 1024 * 1024)


def swapped(value, axis, bits):
    count = lax.axis_size(axis)
    return lax.ppermute(value, axis, [(source, source ^ bits) for source in range(count)])


def dot(a, b, contract):
    return lax.dot_general(a, b, (contract, ((), ())), preferred_element_type=jnp.float32)


def each(count, body, state):
    if count > 8:
        return lax.fori_loop(0, count, body, state)
    for step in range(count):
        state = body(step, state)
    return state


def pack(core, positions, keys, values):
    rows, size = keys.shape
    held = jnp.where(core == 0, keys, values)
    runs = (positions.reshape(rows // RUN, RUN)[:, :1] // RUN).astype(jnp.bfloat16)
    meta = jnp.pad(jnp.broadcast_to(runs, (rows // RUN, size)), ((0, META_ROWS - rows // RUN), (0, 0)))
    return jnp.concatenate([held, meta], axis=0)


def carve_kernel(block_ref, w_ref, *refs):
    outs, sems = refs[1:-1], refs[-1]
    rows, share = outs[0].shape
    parts = sems.shape[1]
    copies = []
    for i, out_ref in enumerate(outs):
        at = pl.multiple_of(block_ref[i] * share, share)
        for j in range(parts):
            part = slice(j * (rows // parts), (j + 1) * (rows // parts))
            source = w_ref.at[part, pl.ds(at, share)]
            copies.append(pltpu.make_async_copy(source, out_ref.at[part, :], sems.at[i, j]))
            copies[-1].start()
    for one in copies:
        one.wait()


def carve(blocks, w_query, share, after):
    block = jax.ShapeDtypeStruct((w_query.shape[0], share), w_query.dtype)
    count = len(blocks)
    return pl.pallas_call(
        carve_kernel,
        out_shape=[block] * count,
        in_specs=[SMEM, HBM, ANY],
        out_specs=[pl.BlockSpec(memory_space=pltpu.VMEM)] * count,
        scratch_shapes=[pltpu.SemaphoreType.DMA((count, 4))],
        compiler_params=params(48),
        cost_estimate=pl.CostEstimate(
            flops=0, bytes_accessed=4 * count * w_query.shape[0] * share, transcendentals=0
        ),
        name="carve",
    )(jnp.stack(blocks), w_query, after)


def attention_kernel(core_ref, pos_ref, doc_ref, mine_ref, swap_ref, *refs):
    groups = (refs[0:2], refs[2:4])
    dq_ref, back_ref, s_ref, dp_ref = refs[4:]
    count, rows, size = back_ref.shape
    half = count // 2
    heads = mine_ref.shape[2] // size
    is_key = core_ref[0] == 0
    inv_root = 1.0 / math.sqrt(size)

    def stack(which):
        parts = [
            ref[which, :, h * size : (h + 1) * size] for ref in (mine_ref, swap_ref) for h in range(heads)
        ]
        return jnp.concatenate(parts, axis=0)

    query = stack(0)
    grad = stack(1)
    wide = query.shape[0]
    last = jnp.concatenate([pos_ref[...].astype(jnp.float32)] * (2 * heads), axis=1)
    first = jnp.concatenate([(doc_ref[...] * RUN).astype(jnp.float32)] * (2 * heads), axis=1)
    offset = lax.broadcasted_iota(jnp.int32, (RUN, wide), 0).astype(jnp.float32)

    def everywhere(body, state):
        for group, (here_ref, there_ref) in enumerate(groups):
            state = each(half, lambda s, now: body(s, group * half + s, here_ref, there_ref, now), state)
        return state

    def scores(s, slot, here_ref, there_ref, top):
        here = here_ref[s, 0:rows, :]
        there = there_ref[s, 0:rows, :]
        key = jnp.where(is_key, here, there)
        value = jnp.where(is_key, there, here)
        score = dot(key, query, ((1,), (1,))) * inv_root
        dp_ref[slot] = dot(value, grad, ((1,), (1,)))
        meta = here_ref[s, rows : rows + META_ROWS, :].astype(jnp.float32)
        for run in range(rows // RUN):
            start = meta[run : run + 1, 0:1] * float(RUN)
            pos = offset + start
            allowed = (pos <= last) & (pos >= first)
            part = jnp.where(allowed, score[run * RUN : (run + 1) * RUN], -1e30)
            s_ref[slot, run * RUN : (run + 1) * RUN, :] = part
            top = jnp.maximum(top, jnp.max(part, axis=0, keepdims=True))
        return top

    top = everywhere(scores, jnp.full((1, wide), -1e30, jnp.float32))

    def weights(slot, state):
        total, mixed = state
        weight = jnp.exp(s_ref[slot] - top)
        s_ref[slot] = weight
        total = total + jnp.sum(weight, axis=0, keepdims=True)
        mixed = mixed + jnp.sum(weight * dp_ref[slot], axis=0, keepdims=True)
        return total, mixed

    zeros = jnp.zeros((1, wide), jnp.float32)
    total, mixed = each(count, weights, (zeros, zeros))
    scale = 1.0 / total
    delta = mixed * scale
    other = jnp.where(is_key, query, grad)

    def gradients(s, slot, here_ref, there_ref, dq):
        prob = s_ref[slot] * scale
        dscore = (prob * (dp_ref[slot] - delta)).astype(jnp.bfloat16)
        picked = jnp.where(is_key, dscore, prob.astype(jnp.bfloat16))
        back_ref[slot] = dot(picked, other, ((1,), (0,))).astype(jnp.bfloat16)
        key = jnp.where(is_key, here_ref[s, 0:rows, :], there_ref[s, 0:rows, :])
        return dq + dot(key, dscore, ((0,), (0,)))

    dq = everywhere(gradients, jnp.zeros((size, wide), jnp.float32)) * inv_root
    for part in range(wide // rows):
        block = dq[:, part * rows : (part + 1) * rows]
        dq_ref[:, part * size : (part + 1) * size] = block.T.astype(jnp.bfloat16)


def attention(core, positions, doc_ids, mine, swap, pieces):
    half, _, size = pieces[0].shape
    _, rows, width = mine.shape
    count = 2 * half
    wide = 2 * rows * (width // size)
    return pl.pallas_call(
        attention_kernel,
        out_shape=[
            jax.ShapeDtypeStruct((rows, 2 * width), jnp.bfloat16),
            jax.ShapeDtypeStruct((count, rows, size), jnp.bfloat16),
        ],
        in_specs=[SMEM] + [pl.BlockSpec()] * 8,
        out_specs=[pl.BlockSpec()] * 2,
        scratch_shapes=[pltpu.VMEM((count, rows, wide), jnp.float32)] * 2,
        compiler_params=params(8 + count * rows * wide // 2**17),
        cost_estimate=pl.CostEstimate(
            flops=10 * count * rows * wide * size,
            bytes_accessed=count * rows * size * 8,
            transcendentals=count * rows * wide,
        ),
        name="attention",
    )(core, positions.reshape(1, rows), doc_ids.reshape(1, rows), mine, swap, *pieces)


def product_kernel(first, dq_ref, wm_ref, wo_ref, out_ref):
    depth = wm_ref.shape[0]
    at = slice(first, first + out_ref.shape[1])
    acc = dot(dq_ref[:, 0:depth], wm_ref[:, at], ((1,), (0,)))
    acc = acc + dot(dq_ref[:, depth:], wo_ref[:, at], ((1,), (0,)))
    out_ref[...] = acc.astype(out_ref.dtype)


def product(dq, w_mine, w_other, first, width, dtype):
    rows, depth = dq.shape
    return pl.pallas_call(
        functools.partial(product_kernel, first),
        out_shape=jax.ShapeDtypeStruct((rows, width), dtype),
        in_specs=[pl.BlockSpec()] * 3,
        out_specs=pl.BlockSpec(),
        compiler_params=params(16),
        cost_estimate=pl.CostEstimate(
            flops=2 * rows * depth * width, bytes_accessed=2 * depth * width, transcendentals=0
        ),
        name="product",
    )(dq, w_mine, w_other)


def own_kernel(block_ref, dq_ref, w_ref, *refs):
    out_ref, wm_ref, sems = refs[TILES:]
    depth, share = wm_ref.shape
    tile = share // TILES
    copies = []
    for i in range(TILES):
        at = pl.multiple_of(block_ref[0] * share + i * tile, tile)
        target = wm_ref.at[:, i * tile : (i + 1) * tile]
        copies.append(pltpu.make_async_copy(w_ref.at[:, pl.ds(at, tile)], target, sems.at[i]))
        copies[i].start()
    for i in range(TILES):
        at = slice(i * tile, (i + 1) * tile)
        acc = dot(dq_ref[:, depth:], refs[i][...], ((1,), (0,)))
        copies[i].wait()
        out_ref[:, at] = acc + dot(dq_ref[:, 0:depth], wm_ref[:, at], ((1,), (0,)))


def own(block, dq, w_query, w_other):
    rows, depth = dq.shape
    share = TILES * w_other[0].shape[1]
    return pl.pallas_call(
        own_kernel,
        out_shape=jax.ShapeDtypeStruct((rows, share), jnp.float32),
        in_specs=[SMEM, pl.BlockSpec(), HBM] + [pl.BlockSpec()] * TILES,
        out_specs=pl.BlockSpec(),
        scratch_shapes=[pltpu.VMEM((depth // 2, share), w_query.dtype), pltpu.SemaphoreType.DMA((TILES,))],
        compiler_params=params(48),
        cost_estimate=pl.CostEstimate(
            flops=2 * rows * depth * share, bytes_accessed=2 * depth * share, transcendentals=0
        ),
        name="own",
    )(block, dq, w_query, *w_other)


def finish_kernel(core_ref, kv_ref, w_ref, acc_ref, first_ref, second_ref, out_ref, hold_ref, sems):
    rows, share = acc_ref.shape
    pair = kv_ref.shape[1]
    size = pair // 2
    cut = first_ref.shape[1]
    tile = share // TILES
    inv_root = 1.0 / math.sqrt(size)
    column = lax.broadcasted_iota(jnp.int32, (1, pair), 1)
    is_key = (column < size) == (core_ref[0] == 0)
    kv = kv_ref[...].astype(jnp.float32) + second_ref[:, share - cut :].astype(jnp.float32)
    kv = (kv * jnp.where(is_key, inv_root, 1.0)).astype(jnp.bfloat16)
    at_mine = pl.ds(pl.multiple_of(core_ref[0] * size, size), size)
    at_other = pl.ds(pl.multiple_of((1 - core_ref[0]) * size, size), size)
    copies = []
    for i in range(TILES):
        low, high = i * tile, (i + 1) * tile
        w = jnp.concatenate([w_ref[at_mine, low:high], w_ref[at_other, low:high]], axis=0)
        acc = acc_ref[:, low:high] + dot(kv, w, ((1,), (0,)))
        come = []
        if low < cut:
            come.append(first_ref[:, low : min(high, cut)])
        if high > cut:
            come.append(second_ref[:, max(low, cut) - cut : high - cut])
        acc = acc + jnp.concatenate(come, axis=1).astype(jnp.float32)
        hold_ref[:, low:high] = acc.astype(jnp.bfloat16)
        copies.append(pltpu.make_async_copy(hold_ref.at[:, low:high], out_ref.at[:, low:high], sems.at[i]))
        copies[i].start()
    for one in copies:
        one.wait()


def finish(core, kv, w_kv, acc, first, second):
    rows, share = acc.shape
    return pl.pallas_call(
        finish_kernel,
        out_shape=jax.ShapeDtypeStruct((rows, share), jnp.bfloat16),
        in_specs=[SMEM] + [pl.BlockSpec()] * 5,
        out_specs=ANY,
        scratch_shapes=[pltpu.VMEM((rows, share), jnp.bfloat16), pltpu.SemaphoreType.DMA((TILES,))],
        compiler_params=params(),
        cost_estimate=pl.CostEstimate(
            flops=2 * rows * kv.shape[1] * share, bytes_accessed=10 * rows * share, transcendentals=0
        ),
        name="finish",
    )(core, kv, w_kv, acc, first, second)


def on_device(queries, keys, values, dout, positions, doc_ids, w_query, w_kv):
    half = lax.axis_size("ctx") // 2
    head = lax.axis_index("head").astype(jnp.int32)
    core = (head & 1).reshape(1)
    share = w_kv.shape[1]
    local_heads = queries.shape[1] // keys.shape[1]

    piece = pack(core, positions, keys, values)
    along_z = [piece] + [swapped(piece, "ctx", 2 * s) for s in range(1, half)]
    both = jnp.stack([queries, dout])
    swap = swapped(both, "head", 1)
    (far_send,) = carve([head ^ 3], w_query, share, both)
    here_z, swap, far_send = lax.optimization_barrier((jnp.stack(along_z), swap, far_send))
    here_x = swapped(here_z, "ctx", 1)
    far_other = swapped(far_send, "head", 1)
    there_z = swapped(here_z, "head", 1)
    (far_mine,) = carve([head ^ 2], w_query, share, here_z)
    here_x, far_mine = lax.optimization_barrier((here_x, far_mine))
    there_x = swapped(here_x, "head", 1)
    dq, back = attention(core, positions, doc_ids, both, swap, (here_z, there_z, here_x, there_x))

    cut = CHUNKS[0] * (share // sum(CHUNKS))
    first_part = product(dq, far_mine, far_other, 0, cut, jnp.bfloat16)
    second_part = product(dq, far_mine, far_other, cut, share - cut, jnp.bfloat16)
    first = swapped(first_part, "head", 2)

    def exchange(trip, kv):
        sent = lax.dynamic_slice_in_dim(back, (1 - trip) * half, half, axis=0)
        pair = back[:half].astype(jnp.float32) + swapped(sent, "ctx", 1).astype(jnp.float32)
        mine = pair[0]
        for s in range(1, half):
            mine = mine + swapped(pair[s].astype(jnp.bfloat16), "ctx", 2 * s).astype(jnp.float32)
        mine = mine.astype(jnp.bfloat16)
        return jnp.concatenate([mine, swapped(mine, "head", 1)], axis=1)

    back, first_part, second_part = lax.optimization_barrier((back, first_part, second_part))
    trips = 1 + jnp.minimum(positions[0], 0)
    kv = lax.fori_loop(0, trips, exchange, jnp.zeros((queries.shape[0], 2 * keys.shape[1]), jnp.bfloat16))

    near_send = carve([(head ^ 1) * TILES + i for i in range(TILES)], w_query, share // TILES, kv)
    near_other = [swapped(one, "head", 1) for one in near_send]
    second_part = jnp.concatenate([second_part, kv], axis=1)
    second_part, first, dq = lax.optimization_barrier((second_part, first, dq))
    second = swapped(second_part, "head", 2)
    acc = own(head.reshape(1), dq, w_query, near_other)
    return finish(core, kv, w_kv, acc, first, second)


def solution(mesh):
    placed = (
        P("ctx", "head"),
        P("ctx", None),
        P("ctx", None),
        P("ctx", "head"),
        P("ctx"),
        P("ctx"),
        P("head", None),
        P(None, "head"),
    )
    return jax.shard_map(
        on_device, mesh=mesh, in_specs=placed, out_specs=P("ctx", "head"), check_vma=False
    )
```

```python
import functools
import math

import jax
import jax.numpy as jnp
from jax import lax
from jax.experimental import pallas as pl
from jax.experimental.pallas import tpu as pltpu
from jax.sharding import PartitionSpec as P

RUN = 64
META_ROWS = 16
CHUNKS = (13, 3)
TILES = 4
ANY = pl.BlockSpec(memory_space=pl.ANY)
HBM = pl.BlockSpec(memory_space=pltpu.HBM)
SMEM = pl.BlockSpec(memory_space=pltpu.SMEM)


def params(limit_mib=16):
    return pltpu.CompilerParams(vmem_limit_bytes=limit_mib * 1024 * 1024)


def swapped(value, axis, bits):
    count = lax.axis_size(axis)
    return lax.ppermute(value, axis, [(source, source ^ bits) for source in range(count)])


def dot(a, b, contract):
    return lax.dot_general(a, b, (contract, ((), ())), preferred_element_type=jnp.float32)


def each(count, body, state):
    if count > 8:
        return lax.fori_loop(0, count, body, state)
    for step in range(count):
        state = body(step, state)
    return state


def pack(core, positions, keys, values):
    rows, size = keys.shape
    held = jnp.where(core == 0, keys, values)
    runs = (positions.reshape(rows // RUN, RUN)[:, :1] // RUN).astype(jnp.bfloat16)
    meta = jnp.pad(jnp.broadcast_to(runs, (rows // RUN, size)), ((0, META_ROWS - rows // RUN), (0, 0)))
    return jnp.concatenate([held, meta], axis=0)


def carve_kernel(block_ref, w_ref, *refs):
    outs, sems = refs[1:-1], refs[-1]
    rows, share = outs[0].shape
    parts = sems.shape[1]
    copies = []
    for i, out_ref in enumerate(outs):
        at = pl.multiple_of(block_ref[i] * share, share)
        for j in range(parts):
            part = slice(j * (rows // parts), (j + 1) * (rows // parts))
            source = w_ref.at[part, pl.ds(at, share)]
            copies.append(pltpu.make_async_copy(source, out_ref.at[part, :], sems.at[i, j]))
            copies[-1].start()
    for one in copies:
        one.wait()


def carve(blocks, w_query, share, after):
    block = jax.ShapeDtypeStruct((w_query.shape[0], share), w_query.dtype)
    count = len(blocks)
    return pl.pallas_call(
        carve_kernel,
        out_shape=[block] * count,
        in_specs=[SMEM, HBM, ANY],
        out_specs=[pl.BlockSpec(memory_space=pltpu.VMEM)] * count,
        scratch_shapes=[pltpu.SemaphoreType.DMA((count, 4))],
        compiler_params=params(45),
        cost_estimate=pl.CostEstimate(
            flops=0, bytes_accessed=4 * count * w_query.shape[0] * share, transcendentals=0
        ),
        name="carve",
    )(jnp.stack(blocks), w_query, after)


def attention_kernel(core_ref, pos_ref, doc_ref, mine_ref, swap_ref, *refs):
    groups = (refs[0:2], refs[2:4])
    dq_ref, back_ref, s_ref, dp_ref = refs[4:]
    count, rows, size = back_ref.shape
    half = count // 2
    heads = mine_ref.shape[2] // size
    is_key = core_ref[0] == 0
    inv_root = 1.0 / math.sqrt(size)

    def stack(which):
        parts = [
            ref[which, :, h * size : (h + 1) * size] for ref in (mine_ref, swap_ref) for h in range(heads)
        ]
        return jnp.concatenate(parts, axis=0)

    query = stack(0)
    grad = stack(1)
    wide = query.shape[0]
    last = jnp.concatenate([pos_ref[...].astype(jnp.float32)] * (2 * heads), axis=1)
    first = jnp.concatenate([(doc_ref[...] * RUN).astype(jnp.float32)] * (2 * heads), axis=1)
    offset = lax.broadcasted_iota(jnp.int32, (RUN, wide), 0).astype(jnp.float32)

    def everywhere(body, state):
        for group, (here_ref, there_ref) in enumerate(groups):
            state = each(half, lambda s, now: body(s, group * half + s, here_ref, there_ref, now), state)
        return state

    def scores(s, slot, here_ref, there_ref, top):
        here = here_ref[s, 0:rows, :]
        there = there_ref[s, 0:rows, :]
        key = jnp.where(is_key, here, there)
        value = jnp.where(is_key, there, here)
        score = dot(key, query, ((1,), (1,))) * inv_root
        dp_ref[slot] = dot(value, grad, ((1,), (1,)))
        meta = here_ref[s, rows : rows + META_ROWS, :].astype(jnp.float32)
        for run in range(rows // RUN):
            start = meta[run : run + 1, 0:1] * float(RUN)
            pos = offset + start
            allowed = (pos <= last) & (pos >= first)
            part = jnp.where(allowed, score[run * RUN : (run + 1) * RUN], -1e30)
            s_ref[slot, run * RUN : (run + 1) * RUN, :] = part
            top = jnp.maximum(top, jnp.max(part, axis=0, keepdims=True))
        return top

    top = everywhere(scores, jnp.full((1, wide), -1e30, jnp.float32))

    def weights(slot, state):
        total, mixed = state
        weight = jnp.exp(s_ref[slot] - top)
        s_ref[slot] = weight
        total = total + jnp.sum(weight, axis=0, keepdims=True)
        mixed = mixed + jnp.sum(weight * dp_ref[slot], axis=0, keepdims=True)
        return total, mixed

    zeros = jnp.zeros((1, wide), jnp.float32)
    total, mixed = each(count, weights, (zeros, zeros))
    scale = 1.0 / total
    delta = mixed * scale
    other = jnp.where(is_key, query, grad)

    def gradients(s, slot, here_ref, there_ref, dq):
        prob = s_ref[slot] * scale
        dscore = (prob * (dp_ref[slot] - delta)).astype(jnp.bfloat16)
        picked = jnp.where(is_key, dscore, prob.astype(jnp.bfloat16))
        back_ref[slot] = dot(picked, other, ((1,), (0,))).astype(jnp.bfloat16)
        key = jnp.where(is_key, here_ref[s, 0:rows, :], there_ref[s, 0:rows, :])
        return dq + dot(key, dscore, ((0,), (0,)))

    dq = everywhere(gradients, jnp.zeros((size, wide), jnp.float32)) * inv_root
    for part in range(wide // rows):
        block = dq[:, part * rows : (part + 1) * rows]
        dq_ref[:, part * size : (part + 1) * size] = block.T.astype(jnp.bfloat16)


def attention(core, positions, doc_ids, mine, swap, pieces):
    half, _, size = pieces[0].shape
    _, rows, width = mine.shape
    count = 2 * half
    wide = 2 * rows * (width // size)
    return pl.pallas_call(
        attention_kernel,
        out_shape=[
            jax.ShapeDtypeStruct((rows, 2 * width), jnp.bfloat16),
            jax.ShapeDtypeStruct((count, rows, size), jnp.bfloat16),
        ],
        in_specs=[SMEM] + [pl.BlockSpec()] * 8,
        out_specs=[pl.BlockSpec()] * 2,
        scratch_shapes=[pltpu.VMEM((count, rows, wide), jnp.float32)] * 2,
        compiler_params=params(8 + count * rows * wide // 2**17),
        cost_estimate=pl.CostEstimate(
            flops=10 * count * rows * wide * size,
            bytes_accessed=count * rows * size * 8,
            transcendentals=count * rows * wide,
        ),
        name="attention",
    )(core, positions.reshape(1, rows), doc_ids.reshape(1, rows), mine, swap, *pieces)


def product_kernel(first, dq_ref, wm_ref, wo_ref, out_ref):
    depth = wm_ref.shape[0]
    at = slice(first, first + out_ref.shape[1])
    acc = dot(dq_ref[:, 0:depth], wm_ref[:, at], ((1,), (0,)))
    acc = acc + dot(dq_ref[:, depth:], wo_ref[:, at], ((1,), (0,)))
    out_ref[...] = acc.astype(out_ref.dtype)


def product(dq, w_mine, w_other, first, width, dtype):
    rows, depth = dq.shape
    return pl.pallas_call(
        functools.partial(product_kernel, first),
        out_shape=jax.ShapeDtypeStruct((rows, width), dtype),
        in_specs=[pl.BlockSpec()] * 3,
        out_specs=pl.BlockSpec(),
        compiler_params=params(16),
        cost_estimate=pl.CostEstimate(
            flops=2 * rows * depth * width, bytes_accessed=2 * depth * width, transcendentals=0
        ),
        name="product",
    )(dq, w_mine, w_other)


def own_kernel(blocks_ref, dq_ref, w_ref, acc_ref, low_ref, high_ref, hold_ref, sems):
    depth, share = hold_ref.shape[1:]
    tile = share // TILES
    copies = []
    for k in range(2):
        for i in range(TILES):
            at = pl.multiple_of(blocks_ref[k] * share + i * tile, tile)
            target = hold_ref.at[k, :, i * tile : (i + 1) * tile]
            copies.append(pltpu.make_async_copy(w_ref.at[:, pl.ds(at, tile)], target, sems.at[k, i]))
            copies[-1].start()
    for k in range(2):
        for i in range(TILES):
            at = slice(i * tile, (i + 1) * tile)
            copies[k * TILES + i].wait()
            part = dot(dq_ref[:, 0:depth], hold_ref[k, :, at], ((1,), (0,)))
            if k == 1:
                acc_ref[:, at] = part
            elif i < TILES // 2:
                low_ref[:, at] = part.astype(jnp.bfloat16)
            else:
                high_ref[:, i * tile - share // 2 : (i + 1) * tile - share // 2] = part.astype(jnp.bfloat16)


def own(blocks, dq, w_query, share):
    rows, depth = dq.shape[0], w_query.shape[0]
    return pl.pallas_call(
        own_kernel,
        out_shape=[
            jax.ShapeDtypeStruct((rows, share), jnp.float32),
            jax.ShapeDtypeStruct((rows, share // 2), jnp.bfloat16),
            jax.ShapeDtypeStruct((rows, share // 2), jnp.bfloat16),
        ],
        in_specs=[SMEM, pl.BlockSpec(), HBM],
        out_specs=[pl.BlockSpec()] * 3,
        scratch_shapes=[
            pltpu.VMEM((2, depth, share), w_query.dtype),
            pltpu.SemaphoreType.DMA((2, TILES)),
        ],
        compiler_params=params(45),
        name="own",
    )(jnp.stack(blocks), dq, w_query)


def finish_kernel(core_ref, kv_ref, w_ref, acc_ref, low_ref, high_ref, first_ref, second_ref, out_ref, hold_ref, sems):
    rows, share = acc_ref.shape
    pair = kv_ref.shape[1]
    size = pair // 2
    cut = first_ref.shape[1]
    tile = share // TILES
    inv_root = 1.0 / math.sqrt(size)
    column = lax.broadcasted_iota(jnp.int32, (1, pair), 1)
    is_key = (column < size) == (core_ref[0] == 0)
    kv = kv_ref[...].astype(jnp.float32) + second_ref[:, share - cut :].astype(jnp.float32)
    kv = (kv * jnp.where(is_key, inv_root, 1.0)).astype(jnp.bfloat16)
    at_mine = pl.ds(pl.multiple_of(core_ref[0] * size, size), size)
    at_other = pl.ds(pl.multiple_of((1 - core_ref[0]) * size, size), size)
    copies = []
    for i in range(TILES):
        low, high = i * tile, (i + 1) * tile
        w = jnp.concatenate([w_ref[at_mine, low:high], w_ref[at_other, low:high]], axis=0)
        given_ref, skip = (low_ref, 0) if high <= share // 2 else (high_ref, share // 2)
        given = given_ref[:, low - skip : high - skip].astype(jnp.float32)
        acc = acc_ref[:, low:high] + given + dot(kv, w, ((1,), (0,)))
        come = []
        if low < cut:
            come.append(first_ref[:, low : min(high, cut)])
        if high > cut:
            come.append(second_ref[:, max(low, cut) - cut : high - cut])
        acc = acc + jnp.concatenate(come, axis=1).astype(jnp.float32)
        hold_ref[:, low:high] = acc.astype(jnp.bfloat16)
        copies.append(pltpu.make_async_copy(hold_ref.at[:, low:high], out_ref.at[:, low:high], sems.at[i]))
        copies[i].start()
    for one in copies:
        one.wait()


def finish(core, kv, w_kv, acc, low, high, first, second):
    rows, share = acc.shape
    return pl.pallas_call(
        finish_kernel,
        out_shape=jax.ShapeDtypeStruct((rows, share), jnp.bfloat16),
        in_specs=[SMEM] + [pl.BlockSpec()] * 7,
        out_specs=ANY,
        scratch_shapes=[pltpu.VMEM((rows, share), jnp.bfloat16), pltpu.SemaphoreType.DMA((TILES,))],
        compiler_params=params(),
        cost_estimate=pl.CostEstimate(
            flops=2 * rows * kv.shape[1] * share, bytes_accessed=10 * rows * share, transcendentals=0
        ),
        name="finish",
    )(core, kv, w_kv, acc, low, high, first, second)


def on_device(queries, keys, values, dout, positions, doc_ids, w_query, w_kv):
    half = lax.axis_size("ctx") // 2
    head = lax.axis_index("head").astype(jnp.int32)
    core = (head & 1).reshape(1)
    share = w_kv.shape[1]
    local_heads = queries.shape[1] // keys.shape[1]

    piece = pack(core, positions, keys, values)
    along_z = [piece] + [swapped(piece, "ctx", 2 * s) for s in range(1, half)]
    both = jnp.stack([queries, dout])
    swap = swapped(both, "head", 1)
    (far_send,) = carve([head ^ 3], w_query, share, both)
    here_z, swap, far_send = lax.optimization_barrier((jnp.stack(along_z), swap, far_send))
    here_x = swapped(here_z, "ctx", 1)
    far_other = swapped(far_send, "head", 1)
    there_z = swapped(here_z, "head", 1)
    (far_mine,) = carve([head ^ 2], w_query, share, here_z)
    here_x, far_mine = lax.optimization_barrier((here_x, far_mine))
    there_x = swapped(here_x, "head", 1)
    dq, back = attention(core, positions, doc_ids, both, swap, (here_z, there_z, here_x, there_x))

    cut = CHUNKS[0] * (share // sum(CHUNKS))
    first_part = product(dq, far_mine, far_other, 0, cut, jnp.bfloat16)
    second_part = product(dq, far_mine, far_other, cut, share - cut, jnp.bfloat16)
    first = swapped(first_part, "head", 2)

    def exchange(trip, kv):
        sent = lax.dynamic_slice_in_dim(back, (1 - trip) * half, half, axis=0)
        pair = back[:half].astype(jnp.float32) + swapped(sent, "ctx", 1).astype(jnp.float32)
        mine = pair[0]
        for s in range(1, half):
            mine = mine + swapped(pair[s].astype(jnp.bfloat16), "ctx", 2 * s).astype(jnp.float32)
        mine = mine.astype(jnp.bfloat16)
        return jnp.concatenate([mine, swapped(mine, "head", 1)], axis=1)

    back, first_part, second_part = lax.optimization_barrier((back, first_part, second_part))
    trips = 1 + jnp.minimum(positions[0], 0)
    kv = lax.fori_loop(0, trips, exchange, jnp.zeros((queries.shape[0], 2 * keys.shape[1]), jnp.bfloat16))

    kv, dq = lax.optimization_barrier((kv, dq))
    second = swapped(jnp.concatenate([second_part, kv], axis=1), "head", 2)
    acc, *give = own([head ^ 1, head], dq, w_query, share)
    low, high = [swapped(one, "head", 1) for one in give]
    return finish(core, kv, w_kv, acc, low, high, first, second)


def solution(mesh):
    placed = (
        P("ctx", "head"),
        P("ctx", None),
        P("ctx", None),
        P("ctx", "head"),
        P("ctx"),
        P("ctx"),
        P("head", None),
        P(None, "head"),
    )
    return jax.shard_map(
        on_device, mesh=mesh, in_specs=placed, out_specs=P("ctx", "head"), check_vma=False
    )
```

```python
import functools
import math

import jax
import jax.numpy as jnp
from jax import lax
from jax.experimental import pallas as pl
from jax.experimental.pallas import tpu as pltpu
from jax.sharding import PartitionSpec as P

RUN = 64
META_ROWS = 16
CHUNKS = (12, 4)
TILES = 4
ANY = pl.BlockSpec(memory_space=pl.ANY)
HBM = pl.BlockSpec(memory_space=pltpu.HBM)
SMEM = pl.BlockSpec(memory_space=pltpu.SMEM)


def params(limit_mib=16):
    return pltpu.CompilerParams(vmem_limit_bytes=limit_mib * 1024 * 1024)


def swapped(value, axis, bits):
    count = lax.axis_size(axis)
    return lax.ppermute(value, axis, [(source, source ^ bits) for source in range(count)])


def dot(a, b, contract):
    return lax.dot_general(a, b, (contract, ((), ())), preferred_element_type=jnp.float32)


def each(count, body, state):
    if count > 8:
        return lax.fori_loop(0, count, body, state)
    for step in range(count):
        state = body(step, state)
    return state


def pack(core, positions, keys, values):
    rows, size = keys.shape
    held = jnp.where(core == 0, keys, values)
    runs = (positions.reshape(rows // RUN, RUN)[:, :1] // RUN).astype(jnp.bfloat16)
    meta = jnp.pad(jnp.broadcast_to(runs, (rows // RUN, size)), ((0, META_ROWS - rows // RUN), (0, 0)))
    return jnp.concatenate([held, meta], axis=0)


def column_block(block_ref, w_ref, share, first, width):
    return w_ref.at[:, pl.ds(pl.multiple_of(block_ref[0] * share + first, 128), width)]


def carve_kernel(block_ref, w_ref, after_ref, out_ref):
    share = out_ref.shape[1]
    tile = share // TILES
    for i in range(TILES):
        out_ref[:, i * tile : (i + 1) * tile] = column_block(block_ref, w_ref, share, i * tile, tile)[...]


def carve(block, w_query, share, after):
    return pl.pallas_call(
        carve_kernel,
        out_shape=jax.ShapeDtypeStruct((w_query.shape[0], share), w_query.dtype),
        in_specs=[SMEM, pl.BlockSpec(), ANY],
        out_specs=pl.BlockSpec(),
        compiler_params=params(),
        cost_estimate=pl.CostEstimate(
            flops=0, bytes_accessed=4 * w_query.shape[0] * share, transcendentals=0
        ),
        name="carve",
    )(block.reshape(1), w_query, after)


def attention_kernel(core_ref, pos_ref, doc_ref, mine_ref, swap_ref, *refs):
    groups = (refs[0:2], refs[2:4])
    dq_ref, back_ref, s_ref, dp_ref = refs[4:]
    count, rows, size = back_ref.shape
    half = count // 2
    heads = mine_ref.shape[2] // size
    is_key = core_ref[0] == 0
    inv_root = 1.0 / math.sqrt(size)

    def stack(which):
        parts = [
            ref[which, :, h * size : (h + 1) * size] for ref in (mine_ref, swap_ref) for h in range(heads)
        ]
        return jnp.concatenate(parts, axis=0)

    query = stack(0)
    grad = stack(1)
    wide = query.shape[0]
    last = jnp.concatenate([pos_ref[...].astype(jnp.float32)] * (2 * heads), axis=1)
    first = jnp.concatenate([(doc_ref[...] * RUN).astype(jnp.float32)] * (2 * heads), axis=1)
    offset = lax.broadcasted_iota(jnp.int32, (RUN, wide), 0).astype(jnp.float32)

    def everywhere(body, state):
        for group, (here_ref, there_ref) in enumerate(groups):
            state = each(half, lambda s, now: body(s, group * half + s, here_ref, there_ref, now), state)
        return state

    def scores(s, slot, here_ref, there_ref, top):
        here = here_ref[s, 0:rows, :]
        there = there_ref[s, 0:rows, :]
        key = jnp.where(is_key, here, there)
        value = jnp.where(is_key, there, here)
        score = dot(key, query, ((1,), (1,))) * inv_root
        dp_ref[slot] = dot(value, grad, ((1,), (1,)))
        meta = here_ref[s, rows : rows + META_ROWS, :].astype(jnp.float32)
        for run in range(rows // RUN):
            start = meta[run : run + 1, 0:1] * float(RUN)
            pos = offset + start
            allowed = (pos <= last) & (pos >= first)
            part = jnp.where(allowed, score[run * RUN : (run + 1) * RUN], -1e30)
            s_ref[slot, run * RUN : (run + 1) * RUN, :] = part
            top = jnp.maximum(top, jnp.max(part, axis=0, keepdims=True))
        return top

    top = everywhere(scores, jnp.full((1, wide), -1e30, jnp.float32))

    def weights(slot, state):
        total, mixed = state
        weight = jnp.exp(s_ref[slot] - top)
        s_ref[slot] = weight
        total = total + jnp.sum(weight, axis=0, keepdims=True)
        mixed = mixed + jnp.sum(weight * dp_ref[slot], axis=0, keepdims=True)
        return total, mixed

    zeros = jnp.zeros((1, wide), jnp.float32)
    total, mixed = each(count, weights, (zeros, zeros))
    scale = 1.0 / total
    delta = mixed * scale
    other = jnp.where(is_key, query, grad)

    def gradients(s, slot, here_ref, there_ref, dq):
        prob = s_ref[slot] * scale
        dscore = (prob * (dp_ref[slot] - delta)).astype(jnp.bfloat16)
        picked = jnp.where(is_key, dscore, prob.astype(jnp.bfloat16))
        back_ref[slot] = dot(picked, other, ((1,), (0,))).astype(jnp.bfloat16)
        key = jnp.where(is_key, here_ref[s, 0:rows, :], there_ref[s, 0:rows, :])
        return dq + dot(key, dscore, ((0,), (0,)))

    dq = everywhere(gradients, jnp.zeros((size, wide), jnp.float32)) * inv_root
    for part in range(wide // rows):
        block = dq[:, part * rows : (part + 1) * rows]
        dq_ref[:, part * size : (part + 1) * size] = block.T.astype(jnp.bfloat16)


def attention(core, positions, doc_ids, mine, swap, pieces):
    half, _, size = pieces[0].shape
    _, rows, width = mine.shape
    count = 2 * half
    wide = 2 * rows * (width // size)
    return pl.pallas_call(
        attention_kernel,
        out_shape=[
            jax.ShapeDtypeStruct((rows, 2 * width), jnp.bfloat16),
            jax.ShapeDtypeStruct((count, rows, size), jnp.bfloat16),
        ],
        in_specs=[SMEM] + [pl.BlockSpec()] * 8,
        out_specs=[pl.BlockSpec()] * 2,
        scratch_shapes=[pltpu.VMEM((count, rows, wide), jnp.float32)] * 2,
        compiler_params=params(8 + count * rows * wide // 2**17),
        cost_estimate=pl.CostEstimate(
            flops=10 * count * rows * wide * size,
            bytes_accessed=count * rows * size * 8,
            transcendentals=count * rows * wide,
        ),
        name="attention",
    )(core, positions.reshape(1, rows), doc_ids.reshape(1, rows), mine, swap, *pieces)


def product_kernel(share, first, block_ref, dq_ref, w_ref, wo_ref, out_ref):
    depth = w_ref.shape[0]
    width = out_ref.shape[1]
    mine = column_block(block_ref, w_ref, share, first, width)
    acc = dot(dq_ref[:, 0:depth], mine[...], ((1,), (0,)))
    acc = acc + dot(dq_ref[:, depth:], wo_ref[:, first : first + width], ((1,), (0,)))
    out_ref[...] = acc.astype(out_ref.dtype)


def product(block, dq, w_query, w_other, first, width):
    rows, depth = dq.shape
    return pl.pallas_call(
        functools.partial(product_kernel, w_other.shape[1], first),
        out_shape=jax.ShapeDtypeStruct((rows, width), dq.dtype),
        in_specs=[SMEM] + [pl.BlockSpec()] * 3,
        out_specs=pl.BlockSpec(),
        compiler_params=params(),
        cost_estimate=pl.CostEstimate(
            flops=2 * rows * depth * width, bytes_accessed=2 * depth * width, transcendentals=0
        ),
        name="product",
    )(block.reshape(1), dq, w_query, w_other)


def own_kernel(block_ref, other_ref, dq_ref, w_ref, acc_ref, *give_refs):
    depth = w_ref.shape[0]
    share = acc_ref.shape[1]
    tile = share // TILES
    dq = dq_ref[:, 0:depth]
    for i, give_ref in enumerate(give_refs):
        block = column_block(other_ref, w_ref, share, i * tile, tile)
        give_ref[...] = dot(dq, block[...], ((1,), (0,))).astype(jnp.bfloat16)
    for i in range(TILES):
        block = column_block(block_ref, w_ref, share, i * tile, tile)
        acc_ref[:, i * tile : (i + 1) * tile] = dot(dq, block[...], ((1,), (0,)))


def own(block, other, dq, w_query, share):
    rows = dq.shape[0]
    return pl.pallas_call(
        own_kernel,
        out_shape=[jax.ShapeDtypeStruct((rows, share), jnp.float32)]
        + [jax.ShapeDtypeStruct((rows, share // TILES), jnp.bfloat16)] * TILES,
        in_specs=[SMEM] * 2 + [pl.BlockSpec()] * 2,
        out_specs=[pl.BlockSpec()] * (1 + TILES),
        compiler_params=params(),
        name="own",
    )(block.reshape(1), other.reshape(1), dq, w_query)


def finish_kernel(core_ref, kv_ref, w_ref, acc_ref, first_ref, second_ref, *refs):
    out_ref, hold_ref, sems = refs[TILES:]
    rows, share = acc_ref.shape
    pair = kv_ref.shape[1]
    size = pair // 2
    cut = first_ref.shape[1]
    tile = share // TILES
    inv_root = 1.0 / math.sqrt(size)
    column = lax.broadcasted_iota(jnp.int32, (1, pair), 1)
    is_key = (column < size) == (core_ref[0] == 0)
    kv = kv_ref[...].astype(jnp.float32) + second_ref[:, share - cut :].astype(jnp.float32)
    kv = (kv * jnp.where(is_key, inv_root, 1.0)).astype(jnp.bfloat16)
    at_mine = pl.ds(pl.multiple_of(core_ref[0] * size, size), size)
    at_other = pl.ds(pl.multiple_of((1 - core_ref[0]) * size, size), size)
    copies = []
    for i in range(TILES):
        low, high = i * tile, (i + 1) * tile
        w = jnp.concatenate([w_ref[at_mine, low:high], w_ref[at_other, low:high]], axis=0)
        acc = acc_ref[:, low:high] + refs[i][...].astype(jnp.float32) + dot(kv, w, ((1,), (0,)))
        come = []
        if low < cut:
            come.append(first_ref[:, low : min(high, cut)])
        if high > cut:
            come.append(second_ref[:, max(low, cut) - cut : high - cut])
        acc = acc + jnp.concatenate(come, axis=1).astype(jnp.float32)
        hold_ref[:, low:high] = acc.astype(jnp.bfloat16)
        copies.append(pltpu.make_async_copy(hold_ref.at[:, low:high], out_ref.at[:, low:high], sems.at[i]))
        copies[i].start()
    for one in copies:
        one.wait()


def finish(core, kv, w_kv, acc, first, second, given):
    rows, share = acc.shape
    return pl.pallas_call(
        finish_kernel,
        out_shape=jax.ShapeDtypeStruct((rows, share), jnp.bfloat16),
        in_specs=[SMEM] + [pl.BlockSpec()] * (5 + TILES),
        out_specs=ANY,
        scratch_shapes=[pltpu.VMEM((rows, share), jnp.bfloat16), pltpu.SemaphoreType.DMA((TILES,))],
        compiler_params=params(),
        cost_estimate=pl.CostEstimate(
            flops=2 * rows * kv.shape[1] * share, bytes_accessed=10 * rows * share, transcendentals=0
        ),
        name="finish",
    )(core, kv, w_kv, acc, first, second, *given)


def on_device(queries, keys, values, dout, positions, doc_ids, w_query, w_kv):
    half = lax.axis_size("ctx") // 2
    head = lax.axis_index("head").astype(jnp.int32)
    core = (head & 1).reshape(1)
    share = w_kv.shape[1]
    local_heads = queries.shape[1] // keys.shape[1]

    piece = pack(core, positions, keys, values)
    along_z = [piece] + [swapped(piece, "ctx", 2 * s) for s in range(1, half)]
    both = jnp.stack([queries, dout])
    swap = swapped(both, "head", 1)
    far_send = carve(head ^ 3, w_query, share, both)
    here_z, swap, far_send = lax.optimization_barrier((jnp.stack(along_z), swap, far_send))
    here_x = swapped(here_z, "ctx", 1)
    far_other = swapped(far_send, "head", 1)
    there_z = swapped(here_z, "head", 1)
    there_x = swapped(here_x, "head", 1)
    dq, back = attention(core, positions, doc_ids, both, swap, (here_z, there_z, here_x, there_x))

    cut = CHUNKS[0] * (share // sum(CHUNKS))
    first_part = product(head ^ 2, dq, w_query, far_other, 0, cut)
    second_part = product(head ^ 2, dq, w_query, far_other, cut, share - cut)
    first = swapped(first_part, "head", 2)

    def exchange(trip, kv):
        sent = lax.dynamic_slice_in_dim(back, (1 - trip) * half, half, axis=0)
        pair = back[:half].astype(jnp.float32) + swapped(sent, "ctx", 1).astype(jnp.float32)
        mine = pair[0]
        for s in range(1, half):
            mine = mine + swapped(pair[s].astype(jnp.bfloat16), "ctx", 2 * s).astype(jnp.float32)
        mine = mine.astype(jnp.bfloat16)
        return jnp.concatenate([mine, swapped(mine, "head", 1)], axis=1)

    back, first_part, second_part = lax.optimization_barrier((back, first_part, second_part))
    trips = 1 + jnp.minimum(positions[0], 0)
    kv = lax.fori_loop(0, trips, exchange, jnp.zeros((queries.shape[0], 2 * keys.shape[1]), jnp.bfloat16))

    kv, dq = lax.optimization_barrier((kv, dq))
    second = swapped(jnp.concatenate([second_part, kv], axis=1), "head", 2)
    acc, *give = own(head, head ^ 1, dq, w_query, share)
    given = [swapped(one, "head", 1) for one in give]
    return finish(core, kv, w_kv, acc, first, second, given)


def solution(mesh):
    placed = (
        P("ctx", "head"),
        P("ctx", None),
        P("ctx", None),
        P("ctx", "head"),
        P("ctx"),
        P("ctx"),
        P("head", None),
        P(None, "head"),
    )
    return jax.shard_map(
        on_device, mesh=mesh, in_specs=placed, out_specs=P("ctx", "head"), check_vma=False
    )
```

```python
import functools
import math

import jax
import jax.numpy as jnp
from jax import lax
from jax.experimental import pallas as pl
from jax.experimental.pallas import tpu as pltpu
from jax.sharding import PartitionSpec as P

RUN = 64
META_ROWS = 16
CHUNKS = (13, 3)
TILES = 4
ANY = pl.BlockSpec(memory_space=pl.ANY)
HBM = pl.BlockSpec(memory_space=pltpu.HBM)
SMEM = pl.BlockSpec(memory_space=pltpu.SMEM)


def params(limit_mib=16):
    return pltpu.CompilerParams(vmem_limit_bytes=limit_mib * 1024 * 1024)


def swapped(value, axis, bits):
    count = lax.axis_size(axis)
    return lax.ppermute(value, axis, [(source, source ^ bits) for source in range(count)])


def dot(a, b, contract):
    return lax.dot_general(a, b, (contract, ((), ())), preferred_element_type=jnp.float32)


def each(count, body, state):
    if count > 8:
        return lax.fori_loop(0, count, body, state)
    for step in range(count):
        state = body(step, state)
    return state


def pack(core, positions, keys, values):
    rows, size = keys.shape
    held = jnp.where(core == 0, keys, values)
    runs = (positions.reshape(rows // RUN, RUN)[:, :1] // RUN).astype(jnp.bfloat16)
    meta = jnp.pad(jnp.broadcast_to(runs, (rows // RUN, size)), ((0, META_ROWS - rows // RUN), (0, 0)))
    return jnp.concatenate([held, meta], axis=0)


def column_block(w_query, block, share, after):
    w_query, _ = lax.optimization_barrier((w_query, after))
    return lax.dynamic_slice_in_dim(w_query, block * share, share, axis=1)


def attention_kernel(core_ref, pos_ref, doc_ref, mine_ref, swap_ref, *refs):
    groups = (refs[0:2], refs[2:4])
    dq_ref, back_ref, s_ref, dp_ref = refs[4:]
    count, rows, size = back_ref.shape
    half = count // 2
    heads = mine_ref.shape[2] // size
    is_key = core_ref[0] == 0
    inv_root = 1.0 / math.sqrt(size)

    def stack(which):
        parts = [
            ref[which, :, h * size : (h + 1) * size] for ref in (mine_ref, swap_ref) for h in range(heads)
        ]
        return jnp.concatenate(parts, axis=0)

    query = stack(0)
    grad = stack(1)
    wide = query.shape[0]
    last = jnp.concatenate([pos_ref[...].astype(jnp.float32)] * (2 * heads), axis=1)
    first = jnp.concatenate([(doc_ref[...] * RUN).astype(jnp.float32)] * (2 * heads), axis=1)
    offset = lax.broadcasted_iota(jnp.int32, (RUN, wide), 0).astype(jnp.float32)

    def everywhere(body, state):
        for group, (here_ref, there_ref) in enumerate(groups):
            state = each(half, lambda s, now: body(s, group * half + s, here_ref, there_ref, now), state)
        return state

    def scores(s, slot, here_ref, there_ref, top):
        here = here_ref[s, 0:rows, :]
        there = there_ref[s, 0:rows, :]
        key = jnp.where(is_key, here, there)
        value = jnp.where(is_key, there, here)
        score = dot(key, query, ((1,), (1,))) * inv_root
        dp_ref[slot] = dot(value, grad, ((1,), (1,)))
        meta = here_ref[s, rows : rows + META_ROWS, :].astype(jnp.float32)
        for run in range(rows // RUN):
            start = meta[run : run + 1, 0:1] * float(RUN)
            pos = offset + start
            allowed = (pos <= last) & (pos >= first)
            part = jnp.where(allowed, score[run * RUN : (run + 1) * RUN], -1e30)
            s_ref[slot, run * RUN : (run + 1) * RUN, :] = part
            top = jnp.maximum(top, jnp.max(part, axis=0, keepdims=True))
        return top

    top = everywhere(scores, jnp.full((1, wide), -1e30, jnp.float32))

    def weights(slot, state):
        total, mixed = state
        weight = jnp.exp(s_ref[slot] - top)
        s_ref[slot] = weight
        total = total + jnp.sum(weight, axis=0, keepdims=True)
        mixed = mixed + jnp.sum(weight * dp_ref[slot], axis=0, keepdims=True)
        return total, mixed

    zeros = jnp.zeros((1, wide), jnp.float32)
    total, mixed = each(count, weights, (zeros, zeros))
    scale = 1.0 / total
    delta = mixed * scale
    other = jnp.where(is_key, query, grad)

    def gradients(s, slot, here_ref, there_ref, dq):
        prob = s_ref[slot] * scale
        dscore = (prob * (dp_ref[slot] - delta)).astype(jnp.bfloat16)
        picked = jnp.where(is_key, dscore, prob.astype(jnp.bfloat16))
        back_ref[slot] = dot(picked, other, ((1,), (0,))).astype(jnp.bfloat16)
        key = jnp.where(is_key, here_ref[s, 0:rows, :], there_ref[s, 0:rows, :])
        return dq + dot(key, dscore, ((0,), (0,)))

    dq = everywhere(gradients, jnp.zeros((size, wide), jnp.float32)) * inv_root
    for part in range(wide // rows):
        block = dq[:, part * rows : (part + 1) * rows]
        dq_ref[:, part * size : (part + 1) * size] = block.T.astype(jnp.bfloat16)


def attention(core, positions, doc_ids, mine, swap, pieces):
    half, _, size = pieces[0].shape
    _, rows, width = mine.shape
    count = 2 * half
    wide = 2 * rows * (width // size)
    return pl.pallas_call(
        attention_kernel,
        out_shape=[
            jax.ShapeDtypeStruct((rows, 2 * width), jnp.bfloat16),
            jax.ShapeDtypeStruct((count, rows, size), jnp.bfloat16),
        ],
        in_specs=[SMEM] + [pl.BlockSpec()] * 8,
        out_specs=[pl.BlockSpec()] * 2,
        scratch_shapes=[pltpu.VMEM((count, rows, wide), jnp.float32)] * 2,
        compiler_params=params(8 + count * rows * wide // 2**17),
        cost_estimate=pl.CostEstimate(
            flops=10 * count * rows * wide * size,
            bytes_accessed=count * rows * size * 8,
            transcendentals=count * rows * wide,
        ),
        name="attention",
    )(core, positions.reshape(1, rows), doc_ids.reshape(1, rows), mine, swap, *pieces)


def product_kernel(first, dq_ref, wm_ref, wo_ref, out_ref):
    depth = wm_ref.shape[0]
    at = slice(first, first + out_ref.shape[1])
    acc = dot(dq_ref[:, 0:depth], wm_ref[:, at], ((1,), (0,)))
    acc = acc + dot(dq_ref[:, depth:], wo_ref[:, at], ((1,), (0,)))
    out_ref[...] = acc.astype(out_ref.dtype)


def product(dq, w_mine, w_other, first, width, dtype):
    rows, depth = dq.shape
    return pl.pallas_call(
        functools.partial(product_kernel, first),
        out_shape=jax.ShapeDtypeStruct((rows, width), dtype),
        in_specs=[pl.BlockSpec()] * 3,
        out_specs=pl.BlockSpec(),
        compiler_params=params(),
        cost_estimate=pl.CostEstimate(
            flops=2 * rows * depth * width, bytes_accessed=2 * depth * width, transcendentals=0
        ),
        name="product",
    )(dq, w_mine, w_other)


def finish_kernel(core_ref, kv_ref, w_ref, acc_ref, first_ref, second_ref, out_ref, hold_ref, sems):
    rows, share = acc_ref.shape
    pair = kv_ref.shape[1]
    size = pair // 2
    cut = first_ref.shape[1]
    tile = share // TILES
    inv_root = 1.0 / math.sqrt(size)
    column = lax.broadcasted_iota(jnp.int32, (1, pair), 1)
    is_key = (column < size) == (core_ref[0] == 0)
    kv = kv_ref[...].astype(jnp.float32) + second_ref[:, share - cut :].astype(jnp.float32)
    kv = (kv * jnp.where(is_key, inv_root, 1.0)).astype(jnp.bfloat16)
    at_mine = pl.ds(pl.multiple_of(core_ref[0] * size, size), size)
    at_other = pl.ds(pl.multiple_of((1 - core_ref[0]) * size, size), size)
    copies = []
    for i in range(TILES):
        low, high = i * tile, (i + 1) * tile
        w = jnp.concatenate([w_ref[at_mine, low:high], w_ref[at_other, low:high]], axis=0)
        acc = acc_ref[:, low:high] + dot(kv, w, ((1,), (0,)))
        come = []
        if low < cut:
            come.append(first_ref[:, low : min(high, cut)])
        if high > cut:
            come.append(second_ref[:, max(low, cut) - cut : high - cut])
        acc = acc + jnp.concatenate(come, axis=1).astype(jnp.float32)
        hold_ref[:, low:high] = acc.astype(jnp.bfloat16)
        copies.append(pltpu.make_async_copy(hold_ref.at[:, low:high], out_ref.at[:, low:high], sems.at[i]))
        copies[i].start()
    for one in copies:
        one.wait()


def finish(core, kv, w_kv, acc, first, second):
    rows, share = acc.shape
    return pl.pallas_call(
        finish_kernel,
        out_shape=jax.ShapeDtypeStruct((rows, share), jnp.bfloat16),
        in_specs=[SMEM] + [pl.BlockSpec()] * 5,
        out_specs=ANY,
        scratch_shapes=[pltpu.VMEM((rows, share), jnp.bfloat16), pltpu.SemaphoreType.DMA((TILES,))],
        compiler_params=params(),
        cost_estimate=pl.CostEstimate(
            flops=2 * rows * kv.shape[1] * share, bytes_accessed=10 * rows * share, transcendentals=0
        ),
        name="finish",
    )(core, kv, w_kv, acc, first, second)


def on_device(queries, keys, values, dout, positions, doc_ids, w_query, w_kv):
    half = lax.axis_size("ctx") // 2
    head = lax.axis_index("head").astype(jnp.int32)
    core = (head & 1).reshape(1)
    share = w_kv.shape[1]
    local_heads = queries.shape[1] // keys.shape[1]

    piece = pack(core, positions, keys, values)
    along_z = [piece] + [swapped(piece, "ctx", 2 * s) for s in range(1, half)]
    both = jnp.stack([queries, dout])
    swap = swapped(both, "head", 1)
    far_send = column_block(w_query, head ^ 3, share, both)
    here_z, swap, far_send = lax.optimization_barrier((jnp.stack(along_z), swap, far_send))
    here_x = swapped(here_z, "ctx", 1)
    far_other = swapped(far_send, "head", 1)
    there_z = swapped(here_z, "head", 1)
    far_mine = column_block(w_query, head ^ 2, share, here_z)
    near_send = column_block(w_query, head ^ 1, share, here_z)
    here_x, far_mine, near_send = lax.optimization_barrier((here_x, far_mine, near_send))
    there_x = swapped(here_x, "head", 1)
    there_x, near_send = lax.optimization_barrier((there_x, near_send))
    near_other = swapped(near_send, "head", 1)
    dq, back = attention(core, positions, doc_ids, both, swap, (here_z, there_z, here_x, there_x))

    cut = CHUNKS[0] * (share // sum(CHUNKS))
    first_part = product(dq, far_mine, far_other, 0, cut, jnp.bfloat16)
    second_part = product(dq, far_mine, far_other, cut, share - cut, jnp.bfloat16)
    first = swapped(first_part, "head", 2)

    def exchange(trip, kv):
        sent = lax.dynamic_slice_in_dim(back, (1 - trip) * half, half, axis=0)
        pair = back[:half].astype(jnp.float32) + swapped(sent, "ctx", 1).astype(jnp.float32)
        mine = pair[0]
        for s in range(1, half):
            mine = mine + swapped(pair[s].astype(jnp.bfloat16), "ctx", 2 * s).astype(jnp.float32)
        mine = mine.astype(jnp.bfloat16)
        return jnp.concatenate([mine, swapped(mine, "head", 1)], axis=1)

    back, first_part, second_part = lax.optimization_barrier((back, first_part, second_part))
    trips = 1 + jnp.minimum(positions[0], 0)
    kv = lax.fori_loop(0, trips, exchange, jnp.zeros((queries.shape[0], 2 * keys.shape[1]), jnp.bfloat16))

    second = swapped(jnp.concatenate([second_part, kv], axis=1), "head", 2)
    near_mine = column_block(w_query, head, share, kv)
    acc = product(dq, near_mine, near_other, 0, share, jnp.float32)
    return finish(core, kv, w_kv, acc, first, second)


def solution(mesh):
    placed = (
        P("ctx", "head"),
        P("ctx", None),
        P("ctx", None),
        P("ctx", "head"),
        P("ctx"),
        P("ctx"),
        P("head", None),
        P(None, "head"),
    )
    return jax.shard_map(
        on_device, mesh=mesh, in_specs=placed, out_specs=P("ctx", "head"), check_vma=False
    )
```

```python
import functools
import math

import jax
import jax.numpy as jnp
from jax import lax
from jax.experimental import pallas as pl
from jax.experimental.pallas import tpu as pltpu
from jax.sharding import PartitionSpec as P

RUN = 64
META_ROWS = 16
TILES = 4
GIVES = 2
ANY = pl.BlockSpec(memory_space=pl.ANY)
HBM = pl.BlockSpec(memory_space=pltpu.HBM)
SMEM = pl.BlockSpec(memory_space=pltpu.SMEM)


def params(limit_mib=16):
    return pltpu.CompilerParams(vmem_limit_bytes=limit_mib * 1024 * 1024)


def swapped(value, axis, bits):
    count = lax.axis_size(axis)
    return lax.ppermute(value, axis, [(source, source ^ bits) for source in range(count)])


def dot(a, b, contract):
    return lax.dot_general(a, b, (contract, ((), ())), preferred_element_type=jnp.float32)


def each(count, body, state):
    if count > 8:
        return lax.fori_loop(0, count, body, state)
    for step in range(count):
        state = body(step, state)
    return state


def pack(core, positions, keys, values):
    rows, size = keys.shape
    held = jnp.where(core == 0, keys, values)
    runs = (positions.reshape(rows // RUN, RUN)[:, :1] // RUN).astype(jnp.bfloat16)
    meta = jnp.pad(jnp.broadcast_to(runs, (rows // RUN, size)), ((0, META_ROWS - rows // RUN), (0, 0)))
    return jnp.concatenate([held, meta], axis=0)


def column_block(w_query, block, share, after):
    w_query, _ = lax.optimization_barrier((w_query, after))
    return lax.dynamic_slice_in_dim(w_query, block * share, share, axis=1)


def attention_kernel(core_ref, pos_ref, doc_ref, qm_ref, qo_ref, gm_ref, go_ref, *refs):
    groups = (refs[0:2], refs[2:4])
    dq_ref, back_ref, s_ref, dp_ref = refs[4:]
    count, rows, size = back_ref.shape
    half = count // 2
    heads = qm_ref.shape[1] // size
    is_key = core_ref[0] == 0
    inv_root = 1.0 / math.sqrt(size)

    def stack(mine_ref, other_ref):
        parts = [ref[:, h * size : (h + 1) * size] for ref in (mine_ref, other_ref) for h in range(heads)]
        return jnp.concatenate(parts, axis=0)

    query = stack(qm_ref, qo_ref)
    grad = stack(gm_ref, go_ref)
    wide = query.shape[0]
    last = jnp.concatenate([pos_ref[...].astype(jnp.float32)] * (2 * heads), axis=1)
    first = jnp.concatenate([(doc_ref[...] * RUN).astype(jnp.float32)] * (2 * heads), axis=1)
    offset = lax.broadcasted_iota(jnp.int32, (RUN, wide), 0).astype(jnp.float32)

    def everywhere(body, state):
        for group, (here_ref, there_ref) in enumerate(groups):
            state = each(half, lambda s, now: body(s, group * half + s, here_ref, there_ref, now), state)
        return state

    def scores(s, slot, here_ref, there_ref, top):
        here = here_ref[s, 0:rows, :]
        there = there_ref[s, 0:rows, :]
        key = jnp.where(is_key, here, there)
        value = jnp.where(is_key, there, here)
        score = dot(key, query, ((1,), (1,))) * inv_root
        dp_ref[slot] = dot(value, grad, ((1,), (1,)))
        meta = here_ref[s, rows : rows + META_ROWS, :].astype(jnp.float32)
        for run in range(rows // RUN):
            start = meta[run : run + 1, 0:1] * float(RUN)
            pos = offset + start
            allowed = (pos <= last) & (pos >= first)
            part = jnp.where(allowed, score[run * RUN : (run + 1) * RUN], -1e30)
            s_ref[slot, run * RUN : (run + 1) * RUN, :] = part
            top = jnp.maximum(top, jnp.max(part, axis=0, keepdims=True))
        return top

    top = everywhere(scores, jnp.full((1, wide), -1e30, jnp.float32))

    def weights(slot, state):
        total, mixed = state
        weight = jnp.exp(s_ref[slot] - top)
        s_ref[slot] = weight
        total = total + jnp.sum(weight, axis=0, keepdims=True)
        mixed = mixed + jnp.sum(weight * dp_ref[slot], axis=0, keepdims=True)
        return total, mixed

    zeros = jnp.zeros((1, wide), jnp.float32)
    total, mixed = each(count, weights, (zeros, zeros))
    scale = 1.0 / total
    delta = mixed * scale
    other = jnp.where(is_key, query, grad)

    def gradients(s, slot, here_ref, there_ref, dq):
        prob = s_ref[slot] * scale
        dscore = (prob * (dp_ref[slot] - delta)).astype(jnp.bfloat16)
        picked = jnp.where(is_key, dscore, prob.astype(jnp.bfloat16))
        back_ref[slot] = dot(picked, other, ((1,), (0,))).astype(jnp.bfloat16)
        key = jnp.where(is_key, here_ref[s, 0:rows, :], there_ref[s, 0:rows, :])
        return dq + dot(key, dscore, ((0,), (0,)))

    dq = everywhere(gradients, jnp.zeros((size, wide), jnp.float32)) * inv_root
    for part in range(wide // rows):
        block = dq[:, part * rows : (part + 1) * rows]
        dq_ref[:, part * size : (part + 1) * size] = block.T.astype(jnp.bfloat16)


def attention(core, positions, doc_ids, q_mine, q_other, g_mine, g_other, pieces):
    half, _, size = pieces[0].shape
    rows, width = q_mine.shape
    count = 2 * half
    wide = 2 * rows * (width // size)
    return pl.pallas_call(
        attention_kernel,
        out_shape=[
            jax.ShapeDtypeStruct((rows, 2 * width), jnp.bfloat16),
            jax.ShapeDtypeStruct((count, rows, size), jnp.bfloat16),
        ],
        in_specs=[SMEM] + [pl.BlockSpec()] * 10,
        out_specs=[pl.BlockSpec()] * 2,
        scratch_shapes=[pltpu.VMEM((count, rows, wide), jnp.float32)] * 2,
        compiler_params=params(8 + count * rows * wide // 2**17),
        cost_estimate=pl.CostEstimate(
            flops=10 * count * rows * wide * size,
            bytes_accessed=count * rows * size * 8,
            transcendentals=count * rows * wide,
        ),
        name="attention",
    )(
        core, positions.reshape(1, rows), doc_ids.reshape(1, rows), q_mine, q_other, g_mine, g_other, *pieces
    )


def product_kernel(first, dq_ref, wm_ref, wo_ref, out_ref):
    depth = wm_ref.shape[0]
    at = slice(first, first + out_ref.shape[1])
    acc = dot(dq_ref[:, 0:depth], wm_ref[:, at], ((1,), (0,)))
    acc = acc + dot(dq_ref[:, depth:], wo_ref[:, at], ((1,), (0,)))
    out_ref[...] = acc.astype(out_ref.dtype)


def product(dq, w_mine, w_other, first, width, dtype):
    rows, depth = dq.shape
    return pl.pallas_call(
        functools.partial(product_kernel, first),
        out_shape=jax.ShapeDtypeStruct((rows, width), dtype),
        in_specs=[pl.BlockSpec()] * 3,
        out_specs=pl.BlockSpec(),
        compiler_params=params(),
        cost_estimate=pl.CostEstimate(
            flops=2 * rows * depth * width, bytes_accessed=2 * depth * width, transcendentals=0
        ),
        name="product",
    )(dq, w_mine, w_other)


def own_kernel(dq_ref, wn_ref, wo_ref, acc_ref, *give_refs):
    depth, share = wn_ref.shape
    dq = dq_ref[:, 0:depth]
    width = share // len(give_refs)
    for i, give_ref in enumerate(give_refs):
        give_ref[...] = dot(dq, wo_ref[:, i * width : (i + 1) * width], ((1,), (0,))).astype(jnp.bfloat16)
    acc_ref[...] = dot(dq, wn_ref[...], ((1,), (0,)))


def own(dq, w_near, w_other):
    rows = dq.shape[0]
    share = w_near.shape[1]
    return pl.pallas_call(
        own_kernel,
        out_shape=[jax.ShapeDtypeStruct((rows, share), jnp.float32)]
        + [jax.ShapeDtypeStruct((rows, share // GIVES), jnp.bfloat16)] * GIVES,
        in_specs=[pl.BlockSpec()] * 3,
        out_specs=[pl.BlockSpec()] * (1 + GIVES),
        compiler_params=params(),
        name="own",
    )(dq, w_near, w_other)


def finish_kernel(core_ref, kv_ref, kv_far_ref, w_ref, acc_ref, far_ref, *refs):
    out_ref, hold_ref, sems = refs[GIVES:]
    rows, share = acc_ref.shape
    pair = kv_ref.shape[1]
    size = pair // 2
    tile = share // TILES
    inv_root = 1.0 / math.sqrt(size)
    column = lax.broadcasted_iota(jnp.int32, (1, pair), 1)
    is_key = (column < size) == (core_ref[0] == 0)
    kv = kv_ref[...].astype(jnp.float32) + kv_far_ref[...].astype(jnp.float32)
    kv = (kv * jnp.where(is_key, inv_root, 1.0)).astype(jnp.bfloat16)
    at_mine = pl.ds(pl.multiple_of(core_ref[0] * size, size), size)
    at_other = pl.ds(pl.multiple_of((1 - core_ref[0]) * size, size), size)
    copies = []
    for i in range(TILES):
        at = slice(i * tile, (i + 1) * tile)
        w = jnp.concatenate([w_ref[at_mine, at], w_ref[at_other, at]], axis=0)
        given_ref = refs[i * GIVES // TILES]
        skip = i * GIVES // TILES * (share // GIVES)
        given = given_ref[:, i * tile - skip : (i + 1) * tile - skip]
        acc = acc_ref[:, at] + far_ref[:, at].astype(jnp.float32) + given.astype(jnp.float32)
        acc = acc + dot(kv, w, ((1,), (0,)))
        hold_ref[:, at] = acc.astype(jnp.bfloat16)
        copies.append(pltpu.make_async_copy(hold_ref.at[:, at], out_ref.at[:, at], sems.at[i]))
        copies[i].start()
    for one in copies:
        one.wait()


def finish(core, kv, kv_far, w_kv, acc, far, given):
    rows, share = acc.shape
    return pl.pallas_call(
        finish_kernel,
        out_shape=jax.ShapeDtypeStruct((rows, share), jnp.bfloat16),
        in_specs=[SMEM] + [pl.BlockSpec()] * (5 + GIVES),
        out_specs=ANY,
        scratch_shapes=[pltpu.VMEM((rows, share), jnp.bfloat16), pltpu.SemaphoreType.DMA((TILES,))],
        compiler_params=params(),
        cost_estimate=pl.CostEstimate(
            flops=2 * rows * kv.shape[1] * share, bytes_accessed=10 * rows * share, transcendentals=0
        ),
        name="finish",
    )(core, kv, kv_far, w_kv, acc, far, *given)


def on_device(queries, keys, values, dout, positions, doc_ids, w_query, w_kv):
    half = lax.axis_size("ctx") // 2
    head = lax.axis_index("head").astype(jnp.int32)
    core = (head & 1).reshape(1)
    share = w_kv.shape[1]
    local_heads = queries.shape[1] // keys.shape[1]

    q_other = swapped(queries, "head", 1)
    g_other = swapped(dout, "head", 1)
    piece = pack(core, positions, keys, values)
    along_z = [piece] + [swapped(piece, "ctx", 2 * s) for s in range(1, half)]
    far_send = column_block(w_query, head ^ 3, share, piece)
    far_mine = column_block(w_query, head ^ 2, share, piece)
    here_z, q_other, g_other, far_send, far_mine = lax.optimization_barrier(
        (jnp.stack(along_z), q_other, g_other, far_send, far_mine)
    )
    here_x = swapped(here_z, "ctx", 1)
    far_other = swapped(far_send, "head", 1)
    there_z = swapped(here_z, "head", 1)
    there_x = swapped(here_x, "head", 1)
    dq, back = attention(
        core, positions, doc_ids, queries, q_other, dout, g_other, (here_z, there_z, here_x, there_x)
    )

    part = product(dq, far_mine, far_other, 0, share, jnp.bfloat16)
    far = swapped(part, "head", 2)

    def exchange(state):
        left, _ = state
        sent = lax.dynamic_slice_in_dim(back, left * half, half, axis=0)
        pair = back[:half].astype(jnp.float32) + swapped(sent, "ctx", 1).astype(jnp.float32)
        mine = pair[0]
        for s in range(1, half):
            mine = mine + swapped(pair[s].astype(jnp.bfloat16), "ctx", 2 * s).astype(jnp.float32)
        mine = mine.astype(jnp.bfloat16)
        return left - 1, jnp.concatenate([mine, swapped(mine, "head", 1)], axis=1)

    back, part, positions = lax.optimization_barrier((back, part, positions))
    trips = 1 + jnp.minimum(positions[0], 0)
    _, kv = lax.while_loop(lambda state: state[0] > 0, exchange, (trips, q_other))
    kv_far = swapped(kv, "head", 2)

    acc, *give = own(dq, column_block(w_query, head, share, kv), column_block(w_query, head ^ 1, share, kv))
    given = [swapped(one, "head", 1) for one in give]
    return finish(core, kv, kv_far, w_kv, acc, far, given)


def solution(mesh):
    placed = (
        P("ctx", "head"),
        P("ctx", None),
        P("ctx", None),
        P("ctx", "head"),
        P("ctx"),
        P("ctx"),
        P("head", None),
        P(None, "head"),
    )
    return jax.shard_map(
        on_device, mesh=mesh, in_specs=placed, out_specs=P("ctx", "head"), check_vma=False
    )
```

```python
import functools
import math

import jax
import jax.numpy as jnp
from jax import lax
from jax.experimental import pallas as pl
from jax.experimental.pallas import tpu as pltpu
from jax.sharding import PartitionSpec as P

RUN = 64
META_ROWS = 16
TILES = 4
GIVES = 2
ANY = pl.BlockSpec(memory_space=pl.ANY)
HBM = pl.BlockSpec(memory_space=pltpu.HBM)
SMEM = pl.BlockSpec(memory_space=pltpu.SMEM)


def params(limit_mib=16):
    return pltpu.CompilerParams(vmem_limit_bytes=limit_mib * 1024 * 1024)


def swapped(value, axis, bits):
    count = lax.axis_size(axis)
    return lax.ppermute(value, axis, [(source, source ^ bits) for source in range(count)])


def dot(a, b, contract):
    return lax.dot_general(a, b, (contract, ((), ())), preferred_element_type=jnp.float32)


def each(count, body, state):
    if count > 8:
        return lax.fori_loop(0, count, body, state)
    for step in range(count):
        state = body(step, state)
    return state


def pack(core, positions, keys, values):
    rows, size = keys.shape
    held = jnp.where(core == 0, keys, values)
    runs = (positions.reshape(rows // RUN, RUN)[:, :1] // RUN).astype(jnp.bfloat16)
    meta = jnp.pad(jnp.broadcast_to(runs, (rows // RUN, size)), ((0, META_ROWS - rows // RUN), (0, 0)))
    return jnp.concatenate([held, meta], axis=0)


def column_block(w_query, block, share, after):
    w_query, _ = lax.optimization_barrier((w_query, after))
    return lax.dynamic_slice_in_dim(w_query, block * share, share, axis=1)


def carve_kernel(block_ref, w_ref, *refs):
    outs, sems = refs[1:-1], refs[-1]
    rows, share = outs[0].shape
    parts = sems.shape[1]
    copies = []
    for i, out_ref in enumerate(outs):
        at = pl.multiple_of(block_ref[i] * share, share)
        for j in range(parts):
            part = slice(j * (rows // parts), (j + 1) * (rows // parts))
            source = w_ref.at[part, pl.ds(at, share)]
            copies.append(pltpu.make_async_copy(source, out_ref.at[part, :], sems.at[i, j]))
            copies[-1].start()
    for one in copies:
        one.wait()


def carve(blocks, w_query, share, after):
    block = jax.ShapeDtypeStruct((w_query.shape[0], share), w_query.dtype)
    count = len(blocks)
    return pl.pallas_call(
        carve_kernel,
        out_shape=[block] * count,
        in_specs=[SMEM, HBM, ANY],
        out_specs=[pl.BlockSpec(memory_space=pltpu.VMEM)] * count,
        scratch_shapes=[pltpu.SemaphoreType.DMA((count, 4))],
        compiler_params=params(48),
        cost_estimate=pl.CostEstimate(flops=0, bytes_accessed=0, transcendentals=0),
        name="carve",
    )(jnp.stack(blocks), w_query, after)


def attention_kernel(core_ref, pos_ref, doc_ref, qm_ref, qo_ref, gm_ref, go_ref, *refs):
    groups = (refs[0:2], refs[2:4])
    dq_ref, back_ref, s_ref, dp_ref = refs[4:]
    count, rows, size = back_ref.shape
    half = count // 2
    heads = qm_ref.shape[1] // size
    is_key = core_ref[0] == 0
    inv_root = 1.0 / math.sqrt(size)

    def stack(mine_ref, other_ref):
        parts = [ref[:, h * size : (h + 1) * size] for ref in (mine_ref, other_ref) for h in range(heads)]
        return jnp.concatenate(parts, axis=0)

    query = stack(qm_ref, qo_ref)
    grad = stack(gm_ref, go_ref)
    wide = query.shape[0]
    last = jnp.concatenate([pos_ref[...].astype(jnp.float32)] * (2 * heads), axis=1)
    first = jnp.concatenate([(doc_ref[...] * RUN).astype(jnp.float32)] * (2 * heads), axis=1)
    offset = lax.broadcasted_iota(jnp.int32, (RUN, wide), 0).astype(jnp.float32)

    def everywhere(body, state):
        for group, (here_ref, there_ref) in enumerate(groups):
            state = each(half, lambda s, now: body(s, group * half + s, here_ref, there_ref, now), state)
        return state

    def scores(s, slot, here_ref, there_ref, top):
        here = here_ref[s, 0:rows, :]
        there = there_ref[s, 0:rows, :]
        key = jnp.where(is_key, here, there)
        value = jnp.where(is_key, there, here)
        score = dot(key, query, ((1,), (1,))) * inv_root
        dp_ref[slot] = dot(value, grad, ((1,), (1,)))
        meta = here_ref[s, rows : rows + META_ROWS, :].astype(jnp.float32)
        for run in range(rows // RUN):
            start = meta[run : run + 1, 0:1] * float(RUN)
            pos = offset + start
            allowed = (pos <= last) & (pos >= first)
            part = jnp.where(allowed, score[run * RUN : (run + 1) * RUN], -1e30)
            s_ref[slot, run * RUN : (run + 1) * RUN, :] = part
            top = jnp.maximum(top, jnp.max(part, axis=0, keepdims=True))
        return top

    top = everywhere(scores, jnp.full((1, wide), -1e30, jnp.float32))

    def weights(slot, state):
        total, mixed = state
        weight = jnp.exp(s_ref[slot] - top)
        s_ref[slot] = weight
        total = total + jnp.sum(weight, axis=0, keepdims=True)
        mixed = mixed + jnp.sum(weight * dp_ref[slot], axis=0, keepdims=True)
        return total, mixed

    zeros = jnp.zeros((1, wide), jnp.float32)
    total, mixed = each(count, weights, (zeros, zeros))
    scale = 1.0 / total
    delta = mixed * scale
    other = jnp.where(is_key, query, grad)

    def gradients(s, slot, here_ref, there_ref, dq):
        prob = s_ref[slot] * scale
        dscore = (prob * (dp_ref[slot] - delta)).astype(jnp.bfloat16)
        picked = jnp.where(is_key, dscore, prob.astype(jnp.bfloat16))
        back_ref[slot] = dot(picked, other, ((1,), (0,))).astype(jnp.bfloat16)
        key = jnp.where(is_key, here_ref[s, 0:rows, :], there_ref[s, 0:rows, :])
        return dq + dot(key, dscore, ((0,), (0,)))

    dq = everywhere(gradients, jnp.zeros((size, wide), jnp.float32)) * inv_root
    for part in range(wide // rows):
        block = dq[:, part * rows : (part + 1) * rows]
        dq_ref[:, part * size : (part + 1) * size] = block.T.astype(jnp.bfloat16)


def attention(core, positions, doc_ids, q_mine, q_other, g_mine, g_other, pieces):
    half, _, size = pieces[0].shape
    rows, width = q_mine.shape
    count = 2 * half
    wide = 2 * rows * (width // size)
    return pl.pallas_call(
        attention_kernel,
        out_shape=[
            jax.ShapeDtypeStruct((rows, 2 * width), jnp.bfloat16),
            jax.ShapeDtypeStruct((count, rows, size), jnp.bfloat16),
        ],
        in_specs=[SMEM] + [pl.BlockSpec()] * 10,
        out_specs=[pl.BlockSpec()] * 2,
        scratch_shapes=[pltpu.VMEM((count, rows, wide), jnp.float32)] * 2,
        compiler_params=params(8 + count * rows * wide // 2**17),
        cost_estimate=pl.CostEstimate(
            flops=10 * count * rows * wide * size,
            bytes_accessed=count * rows * size * 8,
            transcendentals=count * rows * wide,
        ),
        name="attention",
    )(
        core, positions.reshape(1, rows), doc_ids.reshape(1, rows), q_mine, q_other, g_mine, g_other, *pieces
    )


def product_kernel(first, dq_ref, wm_ref, wo_ref, out_ref):
    depth = wm_ref.shape[0]
    at = slice(first, first + out_ref.shape[1])
    acc = dot(dq_ref[:, 0:depth], wm_ref[:, at], ((1,), (0,)))
    acc = acc + dot(dq_ref[:, depth:], wo_ref[:, at], ((1,), (0,)))
    out_ref[...] = acc.astype(out_ref.dtype)


def product(dq, w_mine, w_other, first, width, dtype):
    rows, depth = dq.shape
    return pl.pallas_call(
        functools.partial(product_kernel, first),
        out_shape=jax.ShapeDtypeStruct((rows, width), dtype),
        in_specs=[pl.BlockSpec()] * 3,
        out_specs=pl.BlockSpec(),
        compiler_params=params(),
        cost_estimate=pl.CostEstimate(
            flops=2 * rows * depth * width, bytes_accessed=2 * depth * width, transcendentals=0
        ),
        name="product",
    )(dq, w_mine, w_other)


def own_kernel(dq_ref, wn_ref, wo_ref, acc_ref, *give_refs):
    depth, share = wn_ref.shape
    dq = dq_ref[:, 0:depth]
    width = share // len(give_refs)
    for i, give_ref in enumerate(give_refs):
        give_ref[...] = dot(dq, wo_ref[:, i * width : (i + 1) * width], ((1,), (0,))).astype(jnp.bfloat16)
    acc_ref[...] = dot(dq, wn_ref[...], ((1,), (0,)))


def own(dq, w_near, w_other):
    rows = dq.shape[0]
    share = w_near.shape[1]
    return pl.pallas_call(
        own_kernel,
        out_shape=[jax.ShapeDtypeStruct((rows, share), jnp.float32)]
        + [jax.ShapeDtypeStruct((rows, share // GIVES), jnp.bfloat16)] * GIVES,
        in_specs=[pl.BlockSpec()] * 3,
        out_specs=[pl.BlockSpec()] * (1 + GIVES),
        compiler_params=params(),
        cost_estimate=pl.CostEstimate(flops=0, bytes_accessed=0, transcendentals=0),
        name="own",
    )(dq, w_near, w_other)


def finish_kernel(core_ref, kv_ref, kv_far_ref, w_ref, acc_ref, far_ref, *refs):
    out_ref, hold_ref, sems = refs[GIVES:]
    rows, share = acc_ref.shape
    pair = kv_ref.shape[1]
    size = pair // 2
    tile = share // TILES
    inv_root = 1.0 / math.sqrt(size)
    column = lax.broadcasted_iota(jnp.int32, (1, pair), 1)
    is_key = (column < size) == (core_ref[0] == 0)
    kv = kv_ref[...].astype(jnp.float32) + kv_far_ref[...].astype(jnp.float32)
    kv = (kv * jnp.where(is_key, inv_root, 1.0)).astype(jnp.bfloat16)
    at_mine = pl.ds(pl.multiple_of(core_ref[0] * size, size), size)
    at_other = pl.ds(pl.multiple_of((1 - core_ref[0]) * size, size), size)
    copies = []
    for i in range(TILES):
        at = slice(i * tile, (i + 1) * tile)
        w = jnp.concatenate([w_ref[at_mine, at], w_ref[at_other, at]], axis=0)
        given_ref = refs[i * GIVES // TILES]
        skip = i * GIVES // TILES * (share // GIVES)
        given = given_ref[:, i * tile - skip : (i + 1) * tile - skip]
        acc = acc_ref[:, at] + far_ref[:, at].astype(jnp.float32) + given.astype(jnp.float32)
        acc = acc + dot(kv, w, ((1,), (0,)))
        hold_ref[:, at] = acc.astype(jnp.bfloat16)
        copies.append(pltpu.make_async_copy(hold_ref.at[:, at], out_ref.at[:, at], sems.at[i]))
        copies[i].start()
    for one in copies:
        one.wait()


def finish(core, kv, kv_far, w_kv, acc, far, given):
    rows, share = acc.shape
    return pl.pallas_call(
        finish_kernel,
        out_shape=jax.ShapeDtypeStruct((rows, share), jnp.bfloat16),
        in_specs=[SMEM] + [pl.BlockSpec()] * (5 + GIVES),
        out_specs=ANY,
        scratch_shapes=[pltpu.VMEM((rows, share), jnp.bfloat16), pltpu.SemaphoreType.DMA((TILES,))],
        compiler_params=params(),
        cost_estimate=pl.CostEstimate(
            flops=2 * rows * kv.shape[1] * share, bytes_accessed=10 * rows * share, transcendentals=0
        ),
        name="finish",
    )(core, kv, kv_far, w_kv, acc, far, *given)


def on_device(queries, keys, values, dout, positions, doc_ids, w_query, w_kv):
    half = lax.axis_size("ctx") // 2
    head = lax.axis_index("head").astype(jnp.int32)
    core = (head & 1).reshape(1)
    share = w_kv.shape[1]
    local_heads = queries.shape[1] // keys.shape[1]

    q_other = swapped(queries, "head", 1)
    g_other = swapped(dout, "head", 1)
    piece = pack(core, positions, keys, values)
    along_z = [piece] + [swapped(piece, "ctx", 2 * s) for s in range(1, half)]
    far_send = column_block(w_query, head ^ 3, share, piece)
    far_mine = column_block(w_query, head ^ 2, share, piece)
    here_z, q_other, g_other, far_send, far_mine = lax.optimization_barrier(
        (jnp.stack(along_z), q_other, g_other, far_send, far_mine)
    )
    here_x = swapped(here_z, "ctx", 1)
    far_other = swapped(far_send, "head", 1)
    there_z = swapped(here_z, "head", 1)
    there_x = swapped(here_x, "head", 1)
    dq, back = attention(
        core, positions, doc_ids, queries, q_other, dout, g_other, (here_z, there_z, here_x, there_x)
    )

    part = product(dq, far_mine, far_other, 0, share, jnp.bfloat16)
    far = swapped(part, "head", 2)

    back, part = lax.optimization_barrier((back, part))
    pair = back[:half].astype(jnp.float32) + swapped(back[half:], "ctx", 1).astype(jnp.float32)
    mine = pair[0]
    for s in range(1, half):
        mine = mine + swapped(pair[s].astype(jnp.bfloat16), "ctx", 2 * s).astype(jnp.float32)
    mine = mine.astype(jnp.bfloat16)
    kv = jnp.concatenate([mine, swapped(mine, "head", 1)], axis=1)
    kv_far = swapped(kv, "head", 2)

    acc, *give = own(dq, *carve([head, head ^ 1], w_query, share, kv))
    given = [swapped(one, "head", 1) for one in give]
    return finish(core, kv, kv_far, w_kv, acc, far, given)


def solution(mesh):
    placed = (
        P("ctx", "head"),
        P("ctx", None),
        P("ctx", None),
        P("ctx", "head"),
        P("ctx"),
        P("ctx"),
        P("head", None),
        P(None, "head"),
    )
    return jax.shard_map(
        on_device, mesh=mesh, in_specs=placed, out_specs=P("ctx", "head"), check_vma=False
    )
```

```python
import functools
import math

import jax
import jax.numpy as jnp
from jax import lax
from jax.experimental import pallas as pl
from jax.experimental.pallas import tpu as pltpu
from jax.sharding import PartitionSpec as P

RUN = 64
META_ROWS = 16
TILES = 4
GIVES = 2
ANY = pl.BlockSpec(memory_space=pl.ANY)
HBM = pl.BlockSpec(memory_space=pltpu.HBM)
SMEM = pl.BlockSpec(memory_space=pltpu.SMEM)


def params(limit_mib=16):
    return pltpu.CompilerParams(vmem_limit_bytes=limit_mib * 1024 * 1024)


def swapped(value, axis, bits):
    count = lax.axis_size(axis)
    return lax.ppermute(value, axis, [(source, source ^ bits) for source in range(count)])


def dot(a, b, contract):
    return lax.dot_general(a, b, (contract, ((), ())), preferred_element_type=jnp.float32)


def each(count, body, state):
    if count > 8:
        return lax.fori_loop(0, count, body, state)
    for step in range(count):
        state = body(step, state)
    return state


def pack(core, positions, keys, values):
    rows, size = keys.shape
    held = jnp.where(core == 0, keys, values)
    runs = (positions.reshape(rows // RUN, RUN)[:, :1] // RUN).astype(jnp.bfloat16)
    meta = jnp.pad(jnp.broadcast_to(runs, (rows // RUN, size)), ((0, META_ROWS - rows // RUN), (0, 0)))
    return jnp.concatenate([held, meta], axis=0)


def column_block(w_query, block, share, after):
    w_query, _ = lax.optimization_barrier((w_query, after))
    return lax.dynamic_slice_in_dim(w_query, block * share, share, axis=1)


def carve_kernel(block_ref, w_ref, *refs):
    outs, sems = refs[1:-1], refs[-1]
    rows, share = outs[0].shape
    parts = sems.shape[1]
    copies = []
    for i, out_ref in enumerate(outs):
        at = pl.multiple_of(block_ref[i] * share, share)
        for j in range(parts):
            part = slice(j * (rows // parts), (j + 1) * (rows // parts))
            source = w_ref.at[part, pl.ds(at, share)]
            copies.append(pltpu.make_async_copy(source, out_ref.at[part, :], sems.at[i, j]))
            copies[-1].start()
    for one in copies:
        one.wait()


def carve(blocks, w_query, share, after):
    block = jax.ShapeDtypeStruct((w_query.shape[0], share), w_query.dtype)
    count = len(blocks)
    return pl.pallas_call(
        carve_kernel,
        out_shape=[block] * count,
        in_specs=[SMEM, HBM, ANY],
        out_specs=[pl.BlockSpec(memory_space=pltpu.VMEM)] * count,
        scratch_shapes=[pltpu.SemaphoreType.DMA((count, 4))],
        compiler_params=params(48),
        cost_estimate=pl.CostEstimate(flops=0, bytes_accessed=0, transcendentals=0),
        name="carve",
    )(jnp.stack(blocks), w_query, after)


def attention_kernel(core_ref, pos_ref, doc_ref, qm_ref, qo_ref, gm_ref, go_ref, *refs):
    groups = (refs[0:2], refs[2:4])
    dq_ref, back_ref, s_ref, dp_ref = refs[4:]
    count, rows, size = back_ref.shape
    half = count // 2
    heads = qm_ref.shape[1] // size
    is_key = core_ref[0] == 0
    inv_root = 1.0 / math.sqrt(size)

    def stack(mine_ref, other_ref):
        parts = [ref[:, h * size : (h + 1) * size] for ref in (mine_ref, other_ref) for h in range(heads)]
        return jnp.concatenate(parts, axis=0)

    query = stack(qm_ref, qo_ref)
    grad = stack(gm_ref, go_ref)
    wide = query.shape[0]
    last = jnp.concatenate([pos_ref[...].astype(jnp.float32)] * (2 * heads), axis=1)
    first = jnp.concatenate([(doc_ref[...] * RUN).astype(jnp.float32)] * (2 * heads), axis=1)
    offset = lax.broadcasted_iota(jnp.int32, (RUN, wide), 0).astype(jnp.float32)

    def everywhere(body, state):
        for group, (here_ref, there_ref) in enumerate(groups):
            state = each(half, lambda s, now: body(s, group * half + s, here_ref, there_ref, now), state)
        return state

    def scores(s, slot, here_ref, there_ref, top):
        here = here_ref[s, 0:rows, :]
        there = there_ref[s, 0:rows, :]
        key = jnp.where(is_key, here, there)
        value = jnp.where(is_key, there, here)
        score = dot(key, query, ((1,), (1,))) * inv_root
        dp_ref[slot] = dot(value, grad, ((1,), (1,)))
        meta = here_ref[s, rows : rows + META_ROWS, :].astype(jnp.float32)
        for run in range(rows // RUN):
            start = meta[run : run + 1, 0:1] * float(RUN)
            pos = offset + start
            allowed = (pos <= last) & (pos >= first)
            part = jnp.where(allowed, score[run * RUN : (run + 1) * RUN], -1e30)
            s_ref[slot, run * RUN : (run + 1) * RUN, :] = part
            top = jnp.maximum(top, jnp.max(part, axis=0, keepdims=True))
        return top

    top = everywhere(scores, jnp.full((1, wide), -1e30, jnp.float32))

    def weights(slot, state):
        total, mixed = state
        weight = jnp.exp(s_ref[slot] - top)
        s_ref[slot] = weight
        total = total + jnp.sum(weight, axis=0, keepdims=True)
        mixed = mixed + jnp.sum(weight * dp_ref[slot], axis=0, keepdims=True)
        return total, mixed

    zeros = jnp.zeros((1, wide), jnp.float32)
    total, mixed = each(count, weights, (zeros, zeros))
    scale = 1.0 / total
    delta = mixed * scale
    other = jnp.where(is_key, query, grad)

    def gradients(s, slot, here_ref, there_ref, dq):
        prob = s_ref[slot] * scale
        dscore = (prob * (dp_ref[slot] - delta)).astype(jnp.bfloat16)
        picked = jnp.where(is_key, dscore, prob.astype(jnp.bfloat16))
        back_ref[slot] = dot(picked, other, ((1,), (0,))).astype(jnp.bfloat16)
        key = jnp.where(is_key, here_ref[s, 0:rows, :], there_ref[s, 0:rows, :])
        return dq + dot(key, dscore, ((0,), (0,)))

    dq = everywhere(gradients, jnp.zeros((size, wide), jnp.float32)) * inv_root
    for part in range(wide // rows):
        block = dq[:, part * rows : (part + 1) * rows]
        dq_ref[:, part * size : (part + 1) * size] = block.T.astype(jnp.bfloat16)


def attention(core, positions, doc_ids, q_mine, q_other, g_mine, g_other, pieces):
    half, _, size = pieces[0].shape
    rows, width = q_mine.shape
    count = 2 * half
    wide = 2 * rows * (width // size)
    return pl.pallas_call(
        attention_kernel,
        out_shape=[
            jax.ShapeDtypeStruct((rows, 2 * width), jnp.bfloat16),
            jax.ShapeDtypeStruct((count, rows, size), jnp.bfloat16),
        ],
        in_specs=[SMEM] + [pl.BlockSpec()] * 10,
        out_specs=[pl.BlockSpec()] * 2,
        scratch_shapes=[pltpu.VMEM((count, rows, wide), jnp.float32)] * 2,
        compiler_params=params(8 + count * rows * wide // 2**17),
        cost_estimate=pl.CostEstimate(
            flops=10 * count * rows * wide * size,
            bytes_accessed=count * rows * size * 8,
            transcendentals=count * rows * wide,
        ),
        name="attention",
    )(
        core, positions.reshape(1, rows), doc_ids.reshape(1, rows), q_mine, q_other, g_mine, g_other, *pieces
    )


def product_kernel(first, dq_ref, wm_ref, wo_ref, out_ref):
    depth = wm_ref.shape[0]
    at = slice(first, first + out_ref.shape[1])
    acc = dot(dq_ref[:, 0:depth], wm_ref[:, at], ((1,), (0,)))
    acc = acc + dot(dq_ref[:, depth:], wo_ref[:, at], ((1,), (0,)))
    out_ref[...] = acc.astype(out_ref.dtype)


def product(dq, w_mine, w_other, first, width, dtype):
    rows, depth = dq.shape
    return pl.pallas_call(
        functools.partial(product_kernel, first),
        out_shape=jax.ShapeDtypeStruct((rows, width), dtype),
        in_specs=[pl.BlockSpec()] * 3,
        out_specs=pl.BlockSpec(),
        compiler_params=params(),
        cost_estimate=pl.CostEstimate(
            flops=2 * rows * depth * width, bytes_accessed=2 * depth * width, transcendentals=0
        ),
        name="product",
    )(dq, w_mine, w_other)


def own_kernel(dq_ref, wn_ref, wo_ref, acc_ref, *give_refs):
    depth, share = wn_ref.shape
    dq = dq_ref[:, 0:depth]
    width = share // len(give_refs)
    for i, give_ref in enumerate(give_refs):
        give_ref[...] = dot(dq, wo_ref[:, i * width : (i + 1) * width], ((1,), (0,))).astype(jnp.bfloat16)
    acc_ref[...] = dot(dq, wn_ref[...], ((1,), (0,)))


def own(dq, w_near, w_other):
    rows = dq.shape[0]
    share = w_near.shape[1]
    return pl.pallas_call(
        own_kernel,
        out_shape=[jax.ShapeDtypeStruct((rows, share), jnp.float32)]
        + [jax.ShapeDtypeStruct((rows, share // GIVES), jnp.bfloat16)] * GIVES,
        in_specs=[pl.BlockSpec()] * 3,
        out_specs=[pl.BlockSpec()] * (1 + GIVES),
        compiler_params=params(),
        cost_estimate=pl.CostEstimate(flops=0, bytes_accessed=0, transcendentals=0),
        name="own",
    )(dq, w_near, w_other)


def finish_kernel(core_ref, kv_ref, kv_far_ref, w_ref, acc_ref, far_ref, *refs):
    out_ref, hold_ref, sems = refs[GIVES:]
    rows, share = acc_ref.shape
    pair = kv_ref.shape[1]
    size = pair // 2
    tile = share // TILES
    inv_root = 1.0 / math.sqrt(size)
    column = lax.broadcasted_iota(jnp.int32, (1, pair), 1)
    is_key = (column < size) == (core_ref[0] == 0)
    kv = kv_ref[...].astype(jnp.float32) + kv_far_ref[...].astype(jnp.float32)
    kv = (kv * jnp.where(is_key, inv_root, 1.0)).astype(jnp.bfloat16)
    at_mine = pl.ds(pl.multiple_of(core_ref[0] * size, size), size)
    at_other = pl.ds(pl.multiple_of((1 - core_ref[0]) * size, size), size)
    copies = []
    for i in range(TILES):
        at = slice(i * tile, (i + 1) * tile)
        w = jnp.concatenate([w_ref[at_mine, at], w_ref[at_other, at]], axis=0)
        given_ref = refs[i * GIVES // TILES]
        skip = i * GIVES // TILES * (share // GIVES)
        given = given_ref[:, i * tile - skip : (i + 1) * tile - skip]
        acc = acc_ref[:, at] + far_ref[:, at].astype(jnp.float32) + given.astype(jnp.float32)
        acc = acc + dot(kv, w, ((1,), (0,)))
        hold_ref[:, at] = acc.astype(jnp.bfloat16)
        copies.append(pltpu.make_async_copy(hold_ref.at[:, at], out_ref.at[:, at], sems.at[i]))
        copies[i].start()
    for one in copies:
        one.wait()


def finish(core, kv, kv_far, w_kv, acc, far, given):
    rows, share = acc.shape
    return pl.pallas_call(
        finish_kernel,
        out_shape=jax.ShapeDtypeStruct((rows, share), jnp.bfloat16),
        in_specs=[SMEM] + [pl.BlockSpec()] * (5 + GIVES),
        out_specs=ANY,
        scratch_shapes=[pltpu.VMEM((rows, share), jnp.bfloat16), pltpu.SemaphoreType.DMA((TILES,))],
        compiler_params=params(),
        cost_estimate=pl.CostEstimate(
            flops=2 * rows * kv.shape[1] * share, bytes_accessed=10 * rows * share, transcendentals=0
        ),
        name="finish",
    )(core, kv, kv_far, w_kv, acc, far, *given)


def on_device(queries, keys, values, dout, positions, doc_ids, w_query, w_kv):
    half = lax.axis_size("ctx") // 2
    head = lax.axis_index("head").astype(jnp.int32)
    core = (head & 1).reshape(1)
    share = w_kv.shape[1]
    local_heads = queries.shape[1] // keys.shape[1]

    q_other = swapped(queries, "head", 1)
    g_other = swapped(dout, "head", 1)
    piece = pack(core, positions, keys, values)
    piece, q_other, g_other = lax.optimization_barrier((piece, q_other, g_other))
    along_z = [piece] + [swapped(piece, "ctx", 2 * s) for s in range(1, half)]
    far_send = column_block(w_query, head ^ 3, share, piece)
    far_mine = column_block(w_query, head ^ 2, share, piece)
    here_z, far_send, far_mine = lax.optimization_barrier((jnp.stack(along_z), far_send, far_mine))
    here_x = swapped(here_z, "ctx", 1)
    far_other = swapped(far_send, "head", 1)
    there_z = swapped(here_z, "head", 1)
    there_x = swapped(here_x, "head", 1)
    dq, back = attention(
        core, positions, doc_ids, queries, q_other, dout, g_other, (here_z, there_z, here_x, there_x)
    )

    part = product(dq, far_mine, far_other, 0, share, jnp.bfloat16)
    far = swapped(part, "head", 2)

    back, part = lax.optimization_barrier((back, part))
    pair = back[:half].astype(jnp.float32) + swapped(back[half:], "ctx", 1).astype(jnp.float32)
    mine = pair[0]
    for s in range(1, half):
        mine = mine + swapped(pair[s].astype(jnp.bfloat16), "ctx", 2 * s).astype(jnp.float32)
    mine = mine.astype(jnp.bfloat16)
    kv = jnp.concatenate([mine, swapped(mine, "head", 1)], axis=1)
    kv_far = swapped(kv, "head", 2)

    acc, *give = own(dq, *carve([head, head ^ 1], w_query, share, kv))
    given = [swapped(one, "head", 1) for one in give]
    return finish(core, kv, kv_far, w_kv, acc, far, given)


def solution(mesh):
    placed = (
        P("ctx", "head"),
        P("ctx", None),
        P("ctx", None),
        P("ctx", "head"),
        P("ctx"),
        P("ctx"),
        P("head", None),
        P(None, "head"),
    )
    return jax.shard_map(
        on_device, mesh=mesh, in_specs=placed, out_specs=P("ctx", "head"), check_vma=False
    )
```

```python
import functools
import math

import jax
import jax.numpy as jnp
from jax import lax
from jax.experimental import pallas as pl
from jax.experimental.pallas import tpu as pltpu
from jax.sharding import PartitionSpec as P

RUN = 64
META_ROWS = 16
TILES = 4
GIVES = 2
ANY = pl.BlockSpec(memory_space=pl.ANY)
HBM = pl.BlockSpec(memory_space=pltpu.HBM)
SMEM = pl.BlockSpec(memory_space=pltpu.SMEM)


def params(limit_mib=16):
    return pltpu.CompilerParams(vmem_limit_bytes=limit_mib * 1024 * 1024)


def swapped(value, axis, bits):
    count = lax.axis_size(axis)
    return lax.ppermute(value, axis, [(source, source ^ bits) for source in range(count)])


def dot(a, b, contract):
    return lax.dot_general(a, b, (contract, ((), ())), preferred_element_type=jnp.float32)


def each(count, body, state):
    if count > 8:
        return lax.fori_loop(0, count, body, state)
    for step in range(count):
        state = body(step, state)
    return state


def pack(core, positions, keys, values):
    rows, size = keys.shape
    held = jnp.where(core == 0, keys, values)
    runs = (positions.reshape(rows // RUN, RUN)[:, :1] // RUN).astype(jnp.bfloat16)
    meta = jnp.pad(jnp.broadcast_to(runs, (rows // RUN, size)), ((0, META_ROWS - rows // RUN), (0, 0)))
    return jnp.concatenate([held, meta], axis=0)


def column_block(w_query, block, share, after):
    w_query, _ = lax.optimization_barrier((w_query, after))
    return lax.dynamic_slice_in_dim(w_query, block * share, share, axis=1)


def carve_kernel(block_ref, w_ref, *refs):
    outs, sems = refs[1:-1], refs[-1]
    rows, share = outs[0].shape
    parts = sems.shape[1]
    copies = []
    for i, out_ref in enumerate(outs):
        at = pl.multiple_of(block_ref[i] * share, share)
        for j in range(parts):
            part = slice(j * (rows // parts), (j + 1) * (rows // parts))
            source = w_ref.at[part, pl.ds(at, share)]
            copies.append(pltpu.make_async_copy(source, out_ref.at[part, :], sems.at[i, j]))
            copies[-1].start()
    for one in copies:
        one.wait()


def carve(blocks, w_query, share, after):
    block = jax.ShapeDtypeStruct((w_query.shape[0], share), w_query.dtype)
    count = len(blocks)
    return pl.pallas_call(
        carve_kernel,
        out_shape=[block] * count,
        in_specs=[SMEM, HBM, ANY],
        out_specs=[pl.BlockSpec(memory_space=pltpu.VMEM)] * count,
        scratch_shapes=[pltpu.SemaphoreType.DMA((count, 4))],
        compiler_params=params(48),
        cost_estimate=pl.CostEstimate(flops=0, bytes_accessed=0, transcendentals=0),
        name="carve",
    )(jnp.stack(blocks), w_query, after)


def attention_kernel(core_ref, pos_ref, doc_ref, qm_ref, qo_ref, gm_ref, go_ref, *refs):
    groups = [refs[i : i + 2] for i in range(0, len(refs) - 4, 2)]
    dq_ref, back_ref, s_ref, dp_ref = refs[-4:]
    count, rows, size = back_ref.shape
    part = count // len(groups)
    heads = qm_ref.shape[1] // size
    is_key = core_ref[0] == 0
    inv_root = 1.0 / math.sqrt(size)

    def stack(mine_ref, other_ref):
        parts = [ref[:, h * size : (h + 1) * size] for ref in (mine_ref, other_ref) for h in range(heads)]
        return jnp.concatenate(parts, axis=0)

    query = stack(qm_ref, qo_ref)
    grad = stack(gm_ref, go_ref)
    wide = query.shape[0]
    last = jnp.concatenate([pos_ref[...].astype(jnp.float32)] * (2 * heads), axis=1)
    first = jnp.concatenate([(doc_ref[...] * RUN).astype(jnp.float32)] * (2 * heads), axis=1)
    offset = lax.broadcasted_iota(jnp.int32, (RUN, wide), 0).astype(jnp.float32)

    def everywhere(body, state):
        for group, (here_ref, there_ref) in enumerate(groups):
            state = each(part, lambda s, now: body(s, group * part + s, here_ref, there_ref, now), state)
        return state

    def scores(s, slot, here_ref, there_ref, top):
        here = here_ref[s, 0:rows, :]
        there = there_ref[s, 0:rows, :]
        key = jnp.where(is_key, here, there)
        value = jnp.where(is_key, there, here)
        score = dot(key, query, ((1,), (1,))) * inv_root
        dp_ref[slot] = dot(value, grad, ((1,), (1,)))
        meta = here_ref[s, rows : rows + META_ROWS, :].astype(jnp.float32)
        for run in range(rows // RUN):
            start = meta[run : run + 1, 0:1] * float(RUN)
            pos = offset + start
            allowed = (pos <= last) & (pos >= first)
            held = jnp.where(allowed, score[run * RUN : (run + 1) * RUN], -1e30)
            s_ref[slot, run * RUN : (run + 1) * RUN, :] = held
            top = jnp.maximum(top, jnp.max(held, axis=0, keepdims=True))
        return top

    top = everywhere(scores, jnp.full((1, wide), -1e30, jnp.float32))

    def weights(slot, state):
        total, mixed = state
        weight = jnp.exp(s_ref[slot] - top)
        s_ref[slot] = weight
        total = total + jnp.sum(weight, axis=0, keepdims=True)
        mixed = mixed + jnp.sum(weight * dp_ref[slot], axis=0, keepdims=True)
        return total, mixed

    zeros = jnp.zeros((1, wide), jnp.float32)
    total, mixed = each(count, weights, (zeros, zeros))
    scale = 1.0 / total
    delta = mixed * scale
    other = jnp.where(is_key, query, grad)

    def gradients(s, slot, here_ref, there_ref, dq):
        prob = s_ref[slot] * scale
        dscore = (prob * (dp_ref[slot] - delta)).astype(jnp.bfloat16)
        picked = jnp.where(is_key, dscore, prob.astype(jnp.bfloat16))
        back_ref[slot] = dot(picked, other, ((1,), (0,))).astype(jnp.bfloat16)
        key = jnp.where(is_key, here_ref[s, 0:rows, :], there_ref[s, 0:rows, :])
        return dq + dot(key, dscore, ((0,), (0,)))

    dq = everywhere(gradients, jnp.zeros((size, wide), jnp.float32)) * inv_root
    for h in range(wide // rows):
        block = dq[:, h * rows : (h + 1) * rows]
        dq_ref[:, h * size : (h + 1) * size] = block.T.astype(jnp.bfloat16)


def attention(core, positions, doc_ids, q_mine, q_other, g_mine, g_other, pieces):
    rows, width = q_mine.shape
    size = pieces[0].shape[2]
    count = sum(one.shape[0] for one in pieces) // 2
    wide = 2 * rows * (width // size)
    return pl.pallas_call(
        attention_kernel,
        out_shape=[
            jax.ShapeDtypeStruct((rows, 2 * width), jnp.bfloat16),
            jax.ShapeDtypeStruct((count, rows, size), jnp.bfloat16),
        ],
        in_specs=[SMEM] + [pl.BlockSpec()] * (6 + len(pieces)),
        out_specs=[pl.BlockSpec()] * 2,
        scratch_shapes=[pltpu.VMEM((count, rows, wide), jnp.float32)] * 2,
        compiler_params=params(8 + count * rows * wide // 2**17),
        cost_estimate=pl.CostEstimate(
            flops=10 * count * rows * wide * size,
            bytes_accessed=count * rows * size * 8,
            transcendentals=count * rows * wide,
        ),
        name="attention",
    )(
        core, positions.reshape(1, rows), doc_ids.reshape(1, rows), q_mine, q_other, g_mine, g_other, *pieces
    )


def product_kernel(first, dq_ref, wm_ref, wo_ref, out_ref):
    depth = wm_ref.shape[0]
    at = slice(first, first + out_ref.shape[1])
    acc = dot(dq_ref[:, 0:depth], wm_ref[:, at], ((1,), (0,)))
    acc = acc + dot(dq_ref[:, depth:], wo_ref[:, at], ((1,), (0,)))
    out_ref[...] = acc.astype(out_ref.dtype)


def product(dq, w_mine, w_other, first, width, dtype):
    rows, depth = dq.shape
    return pl.pallas_call(
        functools.partial(product_kernel, first),
        out_shape=jax.ShapeDtypeStruct((rows, width), dtype),
        in_specs=[pl.BlockSpec()] * 3,
        out_specs=pl.BlockSpec(),
        compiler_params=params(),
        cost_estimate=pl.CostEstimate(
            flops=2 * rows * depth * width, bytes_accessed=2 * depth * width, transcendentals=0
        ),
        name="product",
    )(dq, w_mine, w_other)


def own_kernel(dq_ref, wn_ref, wo_ref, acc_ref, *give_refs):
    depth, share = wn_ref.shape
    dq = dq_ref[:, 0:depth]
    width = share // len(give_refs)
    for i, give_ref in enumerate(give_refs):
        give_ref[...] = dot(dq, wo_ref[:, i * width : (i + 1) * width], ((1,), (0,))).astype(jnp.bfloat16)
    acc_ref[...] = dot(dq, wn_ref[...], ((1,), (0,)))


def own(dq, w_near, w_other):
    rows = dq.shape[0]
    share = w_near.shape[1]
    return pl.pallas_call(
        own_kernel,
        out_shape=[jax.ShapeDtypeStruct((rows, share), jnp.float32)]
        + [jax.ShapeDtypeStruct((rows, share // GIVES), jnp.bfloat16)] * GIVES,
        in_specs=[pl.BlockSpec()] * 3,
        out_specs=[pl.BlockSpec()] * (1 + GIVES),
        compiler_params=params(),
        cost_estimate=pl.CostEstimate(flops=0, bytes_accessed=0, transcendentals=0),
        name="own",
    )(dq, w_near, w_other)


def finish_kernel(core_ref, kv_ref, kv_far_ref, w_ref, acc_ref, far_ref, *refs):
    out_ref, hold_ref, sems = refs[GIVES:]
    rows, share = acc_ref.shape
    pair = kv_ref.shape[1]
    size = pair // 2
    tile = share // TILES
    inv_root = 1.0 / math.sqrt(size)
    column = lax.broadcasted_iota(jnp.int32, (1, pair), 1)
    is_key = (column < size) == (core_ref[0] == 0)
    kv = kv_ref[...].astype(jnp.float32) + kv_far_ref[...].astype(jnp.float32)
    kv = (kv * jnp.where(is_key, inv_root, 1.0)).astype(jnp.bfloat16)
    at_mine = pl.ds(pl.multiple_of(core_ref[0] * size, size), size)
    at_other = pl.ds(pl.multiple_of((1 - core_ref[0]) * size, size), size)
    copies = []
    for i in range(TILES):
        at = slice(i * tile, (i + 1) * tile)
        w = jnp.concatenate([w_ref[at_mine, at], w_ref[at_other, at]], axis=0)
        given_ref = refs[i * GIVES // TILES]
        skip = i * GIVES // TILES * (share // GIVES)
        given = given_ref[:, i * tile - skip : (i + 1) * tile - skip]
        acc = acc_ref[:, at] + far_ref[:, at].astype(jnp.float32) + given.astype(jnp.float32)
        acc = acc + dot(kv, w, ((1,), (0,)))
        hold_ref[:, at] = acc.astype(jnp.bfloat16)
        copies.append(pltpu.make_async_copy(hold_ref.at[:, at], out_ref.at[:, at], sems.at[i]))
        copies[i].start()
    for one in copies:
        one.wait()


def finish(core, kv, kv_far, w_kv, acc, far, given):
    rows, share = acc.shape
    return pl.pallas_call(
        finish_kernel,
        out_shape=jax.ShapeDtypeStruct((rows, share), jnp.bfloat16),
        in_specs=[SMEM] + [pl.BlockSpec()] * (5 + GIVES),
        out_specs=ANY,
        scratch_shapes=[pltpu.VMEM((rows, share), jnp.bfloat16), pltpu.SemaphoreType.DMA((TILES,))],
        compiler_params=params(),
        cost_estimate=pl.CostEstimate(
            flops=2 * rows * kv.shape[1] * share, bytes_accessed=10 * rows * share, transcendentals=0
        ),
        name="finish",
    )(core, kv, kv_far, w_kv, acc, far, *given)


def on_device(queries, keys, values, dout, positions, doc_ids, w_query, w_kv):
    half = lax.axis_size("ctx") // 2
    head = lax.axis_index("head").astype(jnp.int32)
    core = (head & 1).reshape(1)
    share = w_kv.shape[1]
    local_heads = queries.shape[1] // keys.shape[1]

    q_other = swapped(queries, "head", 1)
    g_other = swapped(dout, "head", 1)
    piece = pack(core, positions, keys, values)
    piece, q_other, g_other = lax.optimization_barrier((piece, q_other, g_other))
    along_z = [piece] + [swapped(piece, "ctx", 2 * s) for s in range(1, half)]
    early = (half + 1) // 2
    z_early, z_late = jnp.stack(along_z[:early]), jnp.stack(along_z[early:])
    x_early = swapped(z_early, "ctx", 1)
    far_send = column_block(w_query, head ^ 3, share, z_early)
    far_mine = column_block(w_query, head ^ 2, share, z_early)
    there_early = swapped(z_early, "head", 1)
    z_late, x_early, there_early, far_send, far_mine = lax.optimization_barrier(
        (z_late, x_early, there_early, far_send, far_mine)
    )
    x_late = swapped(z_late, "ctx", 1)
    far_other = swapped(far_send, "head", 1)
    pieces = [z_early, there_early]
    for here in (z_late, x_early, x_late):
        pieces += [here, swapped(here, "head", 1)]
    dq, back = attention(core, positions, doc_ids, queries, q_other, dout, g_other, pieces)

    part = product(dq, far_mine, far_other, 0, share, jnp.bfloat16)
    far = swapped(part, "head", 2)

    back, part = lax.optimization_barrier((back, part))
    pair = back[:half].astype(jnp.float32) + swapped(back[half:], "ctx", 1).astype(jnp.float32)
    mine = pair[0]
    for s in range(1, half):
        mine = mine + swapped(pair[s].astype(jnp.bfloat16), "ctx", 2 * s).astype(jnp.float32)
    mine = mine.astype(jnp.bfloat16)
    kv = jnp.concatenate([mine, swapped(mine, "head", 1)], axis=1)
    kv_far = swapped(kv, "head", 2)

    acc, *give = own(dq, *carve([head, head ^ 1], w_query, share, kv))
    given = [swapped(one, "head", 1) for one in give]
    return finish(core, kv, kv_far, w_kv, acc, far, given)


def solution(mesh):
    placed = (
        P("ctx", "head"),
        P("ctx", None),
        P("ctx", None),
        P("ctx", "head"),
        P("ctx"),
        P("ctx"),
        P("head", None),
        P(None, "head"),
    )
    return jax.shard_map(
        on_device, mesh=mesh, in_specs=placed, out_specs=P("ctx", "head"), check_vma=False
    )
```

```python
import functools
import math

import jax
import jax.numpy as jnp
from jax import lax
from jax.experimental import pallas as pl
from jax.experimental.pallas import tpu as pltpu
from jax.sharding import PartitionSpec as P

RUN = 64
META_ROWS = 16
TILES = 4
HALVES = 2
GIVES = 2
ANY = pl.BlockSpec(memory_space=pl.ANY)
HBM = pl.BlockSpec(memory_space=pltpu.HBM)
SMEM = pl.BlockSpec(memory_space=pltpu.SMEM)


def params(limit_mib=16):
    return pltpu.CompilerParams(vmem_limit_bytes=limit_mib * 1024 * 1024)


def swapped(value, axis, bits):
    count = lax.axis_size(axis)
    return lax.ppermute(value, axis, [(source, source ^ bits) for source in range(count)])


def dot(a, b, contract):
    return lax.dot_general(a, b, (contract, ((), ())), preferred_element_type=jnp.float32)


def each(count, body, state):
    if count > 8:
        return lax.fori_loop(0, count, body, state)
    for step in range(count):
        state = body(step, state)
    return state


def pack(core, positions, keys, values):
    rows, size = keys.shape
    held = jnp.where(core == 0, keys, values)
    runs = (positions.reshape(rows // RUN, RUN)[:, :1] // RUN).astype(jnp.bfloat16)
    meta = jnp.pad(jnp.broadcast_to(runs, (rows // RUN, size)), ((0, META_ROWS - rows // RUN), (0, 0)))
    return jnp.concatenate([held, meta], axis=0)


def column_block(w_query, block, share, after):
    w_query, _ = lax.optimization_barrier((w_query, after))
    return lax.dynamic_slice_in_dim(w_query, block * share, share, axis=1)


def carve_kernel(block_ref, w_ref, *refs):
    outs, sems = refs[1:-1], refs[-1]
    rows, share = outs[0].shape
    parts = sems.shape[1]
    copies = []
    for i, out_ref in enumerate(outs):
        at = pl.multiple_of(block_ref[i] * share, share)
        for j in range(parts):
            part = slice(j * (rows // parts), (j + 1) * (rows // parts))
            source = w_ref.at[part, pl.ds(at, share)]
            copies.append(pltpu.make_async_copy(source, out_ref.at[part, :], sems.at[i, j]))
            copies[-1].start()
    for one in copies:
        one.wait()


def carve(blocks, w_query, share, after):
    block = jax.ShapeDtypeStruct((w_query.shape[0], share), w_query.dtype)
    count = len(blocks)
    return pl.pallas_call(
        carve_kernel,
        out_shape=[block] * count,
        in_specs=[SMEM, HBM, ANY],
        out_specs=[pl.BlockSpec(memory_space=pltpu.VMEM)] * count,
        scratch_shapes=[pltpu.SemaphoreType.DMA((count, 4))],
        compiler_params=params(48),
        cost_estimate=pl.CostEstimate(flops=0, bytes_accessed=0, transcendentals=0),
        name="carve",
    )(jnp.stack(blocks), w_query, after)


def attention_kernel(core_ref, pos_ref, doc_ref, qm_ref, qo_ref, gm_ref, go_ref, *refs):
    groups = [refs[i : i + 2] for i in range(0, len(refs) - 4, 2)]
    dq_ref, back_ref, s_ref, dp_ref = refs[-4:]
    count, rows, size = back_ref.shape
    part = count // len(groups)
    heads = qm_ref.shape[1] // size
    is_key = core_ref[0] == 0
    inv_root = 1.0 / math.sqrt(size)

    def stack(mine_ref, other_ref):
        parts = [ref[:, h * size : (h + 1) * size] for ref in (mine_ref, other_ref) for h in range(heads)]
        return jnp.concatenate(parts, axis=0)

    query = stack(qm_ref, qo_ref)
    grad = stack(gm_ref, go_ref)
    wide = query.shape[0]
    last = jnp.concatenate([pos_ref[...].astype(jnp.float32)] * (2 * heads), axis=1)
    first = jnp.concatenate([(doc_ref[...] * RUN).astype(jnp.float32)] * (2 * heads), axis=1)
    offset = lax.broadcasted_iota(jnp.int32, (RUN, wide), 0).astype(jnp.float32)

    def everywhere(body, state):
        for group, (here_ref, there_ref) in enumerate(groups):
            state = each(part, lambda s, now: body(s, group * part + s, here_ref, there_ref, now), state)
        return state

    def scores(s, slot, here_ref, there_ref, top):
        here = here_ref[s, 0:rows, :]
        there = there_ref[s, 0:rows, :]
        key = jnp.where(is_key, here, there)
        value = jnp.where(is_key, there, here)
        score = dot(key, query, ((1,), (1,))) * inv_root
        dp_ref[slot] = dot(value, grad, ((1,), (1,)))
        meta = here_ref[s, rows : rows + META_ROWS, :].astype(jnp.float32)
        for run in range(rows // RUN):
            start = meta[run : run + 1, 0:1] * float(RUN)
            pos = offset + start
            allowed = (pos <= last) & (pos >= first)
            held = jnp.where(allowed, score[run * RUN : (run + 1) * RUN], -1e30)
            s_ref[slot, run * RUN : (run + 1) * RUN, :] = held
            top = jnp.maximum(top, jnp.max(held, axis=0, keepdims=True))
        return top

    top = everywhere(scores, jnp.full((1, wide), -1e30, jnp.float32))

    def weights(slot, state):
        total, mixed = state
        weight = jnp.exp(s_ref[slot] - top)
        s_ref[slot] = weight
        total = total + jnp.sum(weight, axis=0, keepdims=True)
        mixed = mixed + jnp.sum(weight * dp_ref[slot], axis=0, keepdims=True)
        return total, mixed

    zeros = jnp.zeros((1, wide), jnp.float32)
    total, mixed = each(count, weights, (zeros, zeros))
    scale = 1.0 / total
    delta = mixed * scale
    other = jnp.where(is_key, query, grad)

    def gradients(s, slot, here_ref, there_ref, dq):
        prob = s_ref[slot] * scale
        dscore = (prob * (dp_ref[slot] - delta)).astype(jnp.bfloat16)
        picked = jnp.where(is_key, dscore, prob.astype(jnp.bfloat16))
        back_ref[slot] = dot(picked, other, ((1,), (0,))).astype(jnp.bfloat16)
        key = jnp.where(is_key, here_ref[s, 0:rows, :], there_ref[s, 0:rows, :])
        return dq + dot(key, dscore, ((0,), (0,)))

    dq = everywhere(gradients, jnp.zeros((size, wide), jnp.float32)) * inv_root
    for h in range(wide // rows):
        block = dq[:, h * rows : (h + 1) * rows]
        dq_ref[:, h * size : (h + 1) * size] = block.T.astype(jnp.bfloat16)


def attention(core, positions, doc_ids, q_mine, q_other, g_mine, g_other, pieces):
    rows, width = q_mine.shape
    size = pieces[0].shape[2]
    count = sum(one.shape[0] for one in pieces) // 2
    wide = 2 * rows * (width // size)
    return pl.pallas_call(
        attention_kernel,
        out_shape=[
            jax.ShapeDtypeStruct((rows, 2 * width), jnp.bfloat16),
            jax.ShapeDtypeStruct((count, rows, size), jnp.bfloat16),
        ],
        in_specs=[SMEM] + [pl.BlockSpec()] * (6 + len(pieces)),
        out_specs=[pl.BlockSpec()] * 2,
        scratch_shapes=[pltpu.VMEM((count, rows, wide), jnp.float32)] * 2,
        compiler_params=params(8 + count * rows * wide // 2**17),
        cost_estimate=pl.CostEstimate(
            flops=10 * count * rows * wide * size,
            bytes_accessed=count * rows * size * 8,
            transcendentals=count * rows * wide,
        ),
        name="attention",
    )(
        core, positions.reshape(1, rows), doc_ids.reshape(1, rows), q_mine, q_other, g_mine, g_other, *pieces
    )


def product_kernel(dq_ref, wm_ref, *refs):
    others, out_ref = refs[:-1], refs[-1]
    depth, share = wm_ref.shape
    width = share // len(others)
    for i, wo_ref in enumerate(others):
        at = slice(i * width, (i + 1) * width)
        acc = dot(dq_ref[:, 0:depth], wm_ref[:, at], ((1,), (0,)))
        acc = acc + dot(dq_ref[:, depth:], wo_ref[...], ((1,), (0,)))
        out_ref[:, at] = acc.astype(out_ref.dtype)


def product(dq, w_mine, w_other, dtype):
    rows, depth = dq.shape
    share = w_mine.shape[1]
    return pl.pallas_call(
        product_kernel,
        out_shape=jax.ShapeDtypeStruct((rows, share), dtype),
        in_specs=[pl.BlockSpec()] * (2 + len(w_other)),
        out_specs=pl.BlockSpec(),
        compiler_params=params(),
        cost_estimate=pl.CostEstimate(
            flops=2 * rows * depth * share, bytes_accessed=2 * depth * share, transcendentals=0
        ),
        name="product",
    )(dq, w_mine, *w_other)


def own_kernel(dq_ref, wn_ref, wo_ref, acc_ref, *give_refs):
    depth, share = wn_ref.shape
    dq = dq_ref[:, 0:depth]
    width = share // len(give_refs)
    for i, give_ref in enumerate(give_refs):
        give_ref[...] = dot(dq, wo_ref[:, i * width : (i + 1) * width], ((1,), (0,))).astype(jnp.bfloat16)
    acc_ref[...] = dot(dq, wn_ref[...], ((1,), (0,)))


def own(dq, w_near, w_other):
    rows = dq.shape[0]
    share = w_near.shape[1]
    return pl.pallas_call(
        own_kernel,
        out_shape=[jax.ShapeDtypeStruct((rows, share), jnp.float32)]
        + [jax.ShapeDtypeStruct((rows, share // GIVES), jnp.bfloat16)] * GIVES,
        in_specs=[pl.BlockSpec()] * 3,
        out_specs=[pl.BlockSpec()] * (1 + GIVES),
        compiler_params=params(),
        cost_estimate=pl.CostEstimate(flops=0, bytes_accessed=0, transcendentals=0),
        name="own",
    )(dq, w_near, w_other)


def finish_kernel(core_ref, kv_ref, kv_far_ref, w_ref, acc_ref, far_ref, *refs):
    out_ref, hold_ref, sems = refs[GIVES:]
    rows, share = acc_ref.shape
    pair = kv_ref.shape[1]
    size = pair // 2
    tile = share // TILES
    inv_root = 1.0 / math.sqrt(size)
    column = lax.broadcasted_iota(jnp.int32, (1, pair), 1)
    is_key = (column < size) == (core_ref[0] == 0)
    kv = kv_ref[...].astype(jnp.float32) + kv_far_ref[...].astype(jnp.float32)
    kv = (kv * jnp.where(is_key, inv_root, 1.0)).astype(jnp.bfloat16)
    at_mine = pl.ds(pl.multiple_of(core_ref[0] * size, size), size)
    at_other = pl.ds(pl.multiple_of((1 - core_ref[0]) * size, size), size)
    copies = []
    for i in range(TILES):
        at = slice(i * tile, (i + 1) * tile)
        w = jnp.concatenate([w_ref[at_mine, at], w_ref[at_other, at]], axis=0)
        given_ref = refs[i * GIVES // TILES]
        skip = i * GIVES // TILES * (share // GIVES)
        given = given_ref[:, i * tile - skip : (i + 1) * tile - skip]
        acc = acc_ref[:, at] + far_ref[:, at].astype(jnp.float32) + given.astype(jnp.float32)
        acc = acc + dot(kv, w, ((1,), (0,)))
        hold_ref[:, at] = acc.astype(jnp.bfloat16)
        copies.append(pltpu.make_async_copy(hold_ref.at[:, at], out_ref.at[:, at], sems.at[i]))
        copies[i].start()
    for one in copies:
        one.wait()


def finish(core, kv, kv_far, w_kv, acc, far, given):
    rows, share = acc.shape
    return pl.pallas_call(
        finish_kernel,
        out_shape=jax.ShapeDtypeStruct((rows, share), jnp.bfloat16),
        in_specs=[SMEM] + [pl.BlockSpec()] * (5 + GIVES),
        out_specs=ANY,
        scratch_shapes=[pltpu.VMEM((rows, share), jnp.bfloat16), pltpu.SemaphoreType.DMA((TILES,))],
        compiler_params=params(),
        cost_estimate=pl.CostEstimate(
            flops=2 * rows * kv.shape[1] * share, bytes_accessed=10 * rows * share, transcendentals=0
        ),
        name="finish",
    )(core, kv, kv_far, w_kv, acc, far, *given)


def on_device(queries, keys, values, dout, positions, doc_ids, w_query, w_kv):
    half = lax.axis_size("ctx") // 2
    head = lax.axis_index("head").astype(jnp.int32)
    core = (head & 1).reshape(1)
    share = w_kv.shape[1]
    local_heads = queries.shape[1] // keys.shape[1]

    q_other = swapped(queries, "head", 1)
    g_other = swapped(dout, "head", 1)
    piece = pack(core, positions, keys, values)
    piece, q_other, g_other = lax.optimization_barrier((piece, q_other, g_other))
    along_z = [piece] + [swapped(piece, "ctx", 2 * s) for s in range(1, half)]
    early = (half + 1) // 2
    z_early, z_late = jnp.stack(along_z[:early]), jnp.stack(along_z[early:])
    x_early = swapped(z_early, "ctx", 1)
    there_early = swapped(z_early, "head", 1)
    z_late, x_early, there_early = lax.optimization_barrier((z_late, x_early, there_early))
    x_late = swapped(z_late, "ctx", 1)
    far_send = [column_block(w_query, (head ^ 3) * HALVES + i, share // HALVES, z_late) for i in range(HALVES)]
    far_mine = column_block(w_query, head ^ 2, share, z_late)
    pieces = [z_early, there_early]
    for here in (z_late, x_early):
        pieces += [here, swapped(here, "head", 1)]
    x_late, far_mine, *rest = lax.optimization_barrier((x_late, far_mine, *far_send, *pieces))
    far_send, pieces = rest[:HALVES], rest[HALVES:]
    pieces += [x_late, swapped(x_late, "head", 1)]
    far_other = [swapped(one, "head", 1) for one in far_send[:1]]
    pieces[-1], *rest = lax.optimization_barrier((pieces[-1], *far_send[1:]))
    far_other += [swapped(one, "head", 1) for one in rest]
    dq, back = attention(core, positions, doc_ids, queries, q_other, dout, g_other, pieces)

    part = product(dq, far_mine, far_other, jnp.bfloat16)
    far = swapped(part, "head", 2)

    back, part = lax.optimization_barrier((back, part))
    pair = back[:half].astype(jnp.float32) + swapped(back[half:], "ctx", 1).astype(jnp.float32)
    mine = pair[0]
    for s in range(1, half):
        mine = mine + swapped(pair[s].astype(jnp.bfloat16), "ctx", 2 * s).astype(jnp.float32)
    mine = mine.astype(jnp.bfloat16)
    kv = jnp.concatenate([mine, swapped(mine, "head", 1)], axis=1)
    kv_far = swapped(kv, "head", 2)

    acc, *give = own(dq, *carve([head, head ^ 1], w_query, share, kv))
    given = [swapped(one, "head", 1) for one in give]
    return finish(core, kv, kv_far, w_kv, acc, far, given)


def solution(mesh):
    placed = (
        P("ctx", "head"),
        P("ctx", None),
        P("ctx", None),
        P("ctx", "head"),
        P("ctx"),
        P("ctx"),
        P("head", None),
        P(None, "head"),
    )
    return jax.shard_map(
        on_device, mesh=mesh, in_specs=placed, out_specs=P("ctx", "head"), check_vma=False
    )
```

```python
import functools
import math

import jax
import jax.numpy as jnp
from jax import lax
from jax.experimental import pallas as pl
from jax.experimental.pallas import tpu as pltpu
from jax.sharding import PartitionSpec as P

RUN = 64
META_ROWS = 16
TILES = 4
GIVES = 2
ANY = pl.BlockSpec(memory_space=pl.ANY)
HBM = pl.BlockSpec(memory_space=pltpu.HBM)
SMEM = pl.BlockSpec(memory_space=pltpu.SMEM)


def params(limit_mib=16):
    return pltpu.CompilerParams(vmem_limit_bytes=limit_mib * 1024 * 1024)


def swapped(value, axis, bits):
    count = lax.axis_size(axis)
    return lax.ppermute(value, axis, [(source, source ^ bits) for source in range(count)])


def dot(a, b, contract):
    return lax.dot_general(a, b, (contract, ((), ())), preferred_element_type=jnp.float32)


def each(count, body, state):
    if count > 8:
        return lax.fori_loop(0, count, body, state)
    for step in range(count):
        state = body(step, state)
    return state


def pack(core, positions, keys, values):
    rows, size = keys.shape
    held = jnp.where(core == 0, keys, values)
    runs = (positions.reshape(rows // RUN, RUN)[:, :1] // RUN).astype(jnp.bfloat16)
    meta = jnp.pad(jnp.broadcast_to(runs, (rows // RUN, size)), ((0, META_ROWS - rows // RUN), (0, 0)))
    return jnp.concatenate([held, meta], axis=0)


def column_block(w_query, block, share, after):
    w_query, _ = lax.optimization_barrier((w_query, after))
    return lax.dynamic_slice_in_dim(w_query, block * share, share, axis=1)


def carve_kernel(block_ref, w_ref, *refs):
    outs, sems = refs[1:-1], refs[-1]
    rows, share = outs[0].shape
    parts = sems.shape[1]
    copies = []
    for i, out_ref in enumerate(outs):
        at = pl.multiple_of(block_ref[i] * share, share)
        for j in range(parts):
            part = slice(j * (rows // parts), (j + 1) * (rows // parts))
            source = w_ref.at[part, pl.ds(at, share)]
            copies.append(pltpu.make_async_copy(source, out_ref.at[part, :], sems.at[i, j]))
            copies[-1].start()
    for one in copies:
        one.wait()


def carve(blocks, w_query, share, after):
    block = jax.ShapeDtypeStruct((w_query.shape[0], share), w_query.dtype)
    count = len(blocks)
    return pl.pallas_call(
        carve_kernel,
        out_shape=[block] * count,
        in_specs=[SMEM, HBM, ANY],
        out_specs=[pl.BlockSpec(memory_space=pltpu.VMEM)] * count,
        scratch_shapes=[pltpu.SemaphoreType.DMA((count, 4))],
        compiler_params=params(48),
        cost_estimate=pl.CostEstimate(flops=0, bytes_accessed=0, transcendentals=0),
        name="carve",
    )(jnp.stack(blocks), w_query, after)


def attention_kernel(core_ref, pos_ref, doc_ref, qm_ref, qo_ref, gm_ref, go_ref, *refs):
    groups = [refs[i : i + 2] for i in range(0, len(refs) - 4, 2)]
    dq_ref, back_ref, s_ref, dp_ref = refs[-4:]
    count, rows, size = back_ref.shape
    part = count // len(groups)
    heads = qm_ref.shape[1] // size
    is_key = core_ref[0] == 0
    inv_root = 1.0 / math.sqrt(size)

    def stack(mine_ref, other_ref):
        parts = [ref[:, h * size : (h + 1) * size] for ref in (mine_ref, other_ref) for h in range(heads)]
        return jnp.concatenate(parts, axis=0)

    query = stack(qm_ref, qo_ref)
    grad = stack(gm_ref, go_ref)
    wide = query.shape[0]
    last = jnp.concatenate([pos_ref[...].astype(jnp.float32)] * (2 * heads), axis=1)
    first = jnp.concatenate([(doc_ref[...] * RUN).astype(jnp.float32)] * (2 * heads), axis=1)
    offset = lax.broadcasted_iota(jnp.int32, (RUN, wide), 0).astype(jnp.float32)

    def everywhere(body, state):
        for group, (here_ref, there_ref) in enumerate(groups):
            state = each(part, lambda s, now: body(s, group * part + s, here_ref, there_ref, now), state)
        return state

    def scores(s, slot, here_ref, there_ref, top):
        here = here_ref[s, 0:rows, :]
        there = there_ref[s, 0:rows, :]
        key = jnp.where(is_key, here, there)
        value = jnp.where(is_key, there, here)
        score = dot(key, query, ((1,), (1,))) * inv_root
        dp_ref[slot] = dot(value, grad, ((1,), (1,)))
        meta = here_ref[s, rows : rows + META_ROWS, :].astype(jnp.float32)
        for run in range(rows // RUN):
            start = meta[run : run + 1, 0:1] * float(RUN)
            pos = offset + start
            allowed = (pos <= last) & (pos >= first)
            held = jnp.where(allowed, score[run * RUN : (run + 1) * RUN], -1e30)
            s_ref[slot, run * RUN : (run + 1) * RUN, :] = held
            top = jnp.maximum(top, jnp.max(held, axis=0, keepdims=True))
        return top

    top = everywhere(scores, jnp.full((1, wide), -1e30, jnp.float32))

    def weights(slot, state):
        total, mixed = state
        weight = jnp.exp(s_ref[slot] - top)
        s_ref[slot] = weight
        total = total + jnp.sum(weight, axis=0, keepdims=True)
        mixed = mixed + jnp.sum(weight * dp_ref[slot], axis=0, keepdims=True)
        return total, mixed

    zeros = jnp.zeros((1, wide), jnp.float32)
    total, mixed = each(count, weights, (zeros, zeros))
    scale = 1.0 / total
    delta = mixed * scale
    other = jnp.where(is_key, query, grad)

    def gradients(s, slot, here_ref, there_ref, dq):
        prob = s_ref[slot] * scale
        dscore = (prob * (dp_ref[slot] - delta)).astype(jnp.bfloat16)
        picked = jnp.where(is_key, dscore, prob.astype(jnp.bfloat16))
        back_ref[slot] = dot(picked, other, ((1,), (0,))).astype(jnp.bfloat16)
        key = jnp.where(is_key, here_ref[s, 0:rows, :], there_ref[s, 0:rows, :])
        return dq + dot(key, dscore, ((0,), (0,)))

    dq = everywhere(gradients, jnp.zeros((size, wide), jnp.float32)) * inv_root
    for h in range(wide // rows):
        block = dq[:, h * rows : (h + 1) * rows]
        dq_ref[:, h * size : (h + 1) * size] = block.T.astype(jnp.bfloat16)


def attention(core, positions, doc_ids, q_mine, q_other, g_mine, g_other, pieces):
    rows, width = q_mine.shape
    size = pieces[0].shape[2]
    count = sum(one.shape[0] for one in pieces) // 2
    wide = 2 * rows * (width // size)
    return pl.pallas_call(
        attention_kernel,
        out_shape=[
            jax.ShapeDtypeStruct((rows, 2 * width), jnp.bfloat16),
            jax.ShapeDtypeStruct((count, rows, size), jnp.bfloat16),
        ],
        in_specs=[SMEM] + [pl.BlockSpec()] * (6 + len(pieces)),
        out_specs=[pl.BlockSpec()] * 2,
        scratch_shapes=[pltpu.VMEM((count, rows, wide), jnp.float32)] * 2,
        compiler_params=params(8 + count * rows * wide // 2**17),
        cost_estimate=pl.CostEstimate(
            flops=10 * count * rows * wide * size,
            bytes_accessed=count * rows * size * 8,
            transcendentals=count * rows * wide,
        ),
        name="attention",
    )(
        core, positions.reshape(1, rows), doc_ids.reshape(1, rows), q_mine, q_other, g_mine, g_other, *pieces
    )


def product_kernel(first, dq_ref, wm_ref, wo_ref, out_ref):
    depth = wm_ref.shape[0]
    at = slice(first, first + out_ref.shape[1])
    acc = dot(dq_ref[:, 0:depth], wm_ref[:, at], ((1,), (0,)))
    acc = acc + dot(dq_ref[:, depth:], wo_ref[:, at], ((1,), (0,)))
    out_ref[...] = acc.astype(out_ref.dtype)


def product(dq, w_mine, w_other, first, width, dtype):
    rows, depth = dq.shape
    return pl.pallas_call(
        functools.partial(product_kernel, first),
        out_shape=jax.ShapeDtypeStruct((rows, width), dtype),
        in_specs=[pl.BlockSpec()] * 3,
        out_specs=pl.BlockSpec(),
        compiler_params=params(),
        cost_estimate=pl.CostEstimate(
            flops=2 * rows * depth * width, bytes_accessed=2 * depth * width, transcendentals=0
        ),
        name="product",
    )(dq, w_mine, w_other)


def own_kernel(dq_ref, wn_ref, wo_ref, acc_ref, *give_refs):
    depth, share = wn_ref.shape
    dq = dq_ref[:, 0:depth]
    width = share // len(give_refs)
    for i, give_ref in enumerate(give_refs):
        give_ref[...] = dot(dq, wo_ref[:, i * width : (i + 1) * width], ((1,), (0,))).astype(jnp.bfloat16)
    acc_ref[...] = dot(dq, wn_ref[...], ((1,), (0,)))


def own(dq, w_near, w_other):
    rows = dq.shape[0]
    share = w_near.shape[1]
    return pl.pallas_call(
        own_kernel,
        out_shape=[jax.ShapeDtypeStruct((rows, share), jnp.float32)]
        + [jax.ShapeDtypeStruct((rows, share // GIVES), jnp.bfloat16)] * GIVES,
        in_specs=[pl.BlockSpec()] * 3,
        out_specs=[pl.BlockSpec()] * (1 + GIVES),
        compiler_params=params(),
        cost_estimate=pl.CostEstimate(flops=0, bytes_accessed=0, transcendentals=0),
        name="own",
    )(dq, w_near, w_other)


def finish_kernel(core_ref, kv_ref, kv_far_ref, w_ref, acc_ref, far_ref, *refs):
    out_ref, hold_ref, sems = refs[GIVES:]
    rows, share = acc_ref.shape
    pair = kv_ref.shape[1]
    size = pair // 2
    tile = share // TILES
    inv_root = 1.0 / math.sqrt(size)
    column = lax.broadcasted_iota(jnp.int32, (1, pair), 1)
    is_key = (column < size) == (core_ref[0] == 0)
    kv = kv_ref[...].astype(jnp.float32) + kv_far_ref[...].astype(jnp.float32)
    kv = (kv * jnp.where(is_key, inv_root, 1.0)).astype(jnp.bfloat16)
    at_mine = pl.ds(pl.multiple_of(core_ref[0] * size, size), size)
    at_other = pl.ds(pl.multiple_of((1 - core_ref[0]) * size, size), size)
    copies = []
    for i in range(TILES):
        at = slice(i * tile, (i + 1) * tile)
        w = jnp.concatenate([w_ref[at_mine, at], w_ref[at_other, at]], axis=0)
        given_ref = refs[i * GIVES // TILES]
        skip = i * GIVES // TILES * (share // GIVES)
        given = given_ref[:, i * tile - skip : (i + 1) * tile - skip]
        acc = acc_ref[:, at] + far_ref[:, at].astype(jnp.float32) + given.astype(jnp.float32)
        acc = acc + dot(kv, w, ((1,), (0,)))
        hold_ref[:, at] = acc.astype(jnp.bfloat16)
        copies.append(pltpu.make_async_copy(hold_ref.at[:, at], out_ref.at[:, at], sems.at[i]))
        copies[i].start()
    for one in copies:
        one.wait()


def finish(core, kv, kv_far, w_kv, acc, far, given):
    rows, share = acc.shape
    return pl.pallas_call(
        finish_kernel,
        out_shape=jax.ShapeDtypeStruct((rows, share), jnp.bfloat16),
        in_specs=[SMEM] + [pl.BlockSpec()] * (5 + GIVES),
        out_specs=ANY,
        scratch_shapes=[pltpu.VMEM((rows, share), jnp.bfloat16), pltpu.SemaphoreType.DMA((TILES,))],
        compiler_params=params(),
        cost_estimate=pl.CostEstimate(
            flops=2 * rows * kv.shape[1] * share, bytes_accessed=10 * rows * share, transcendentals=0
        ),
        name="finish",
    )(core, kv, kv_far, w_kv, acc, far, *given)


def on_device(queries, keys, values, dout, positions, doc_ids, w_query, w_kv):
    half = lax.axis_size("ctx") // 2
    head = lax.axis_index("head").astype(jnp.int32)
    core = (head & 1).reshape(1)
    share = w_kv.shape[1]
    local_heads = queries.shape[1] // keys.shape[1]

    q_other = swapped(queries, "head", 1)
    g_other = swapped(dout, "head", 1)
    piece = pack(core, positions, keys, values)
    piece, q_other, g_other = lax.optimization_barrier((piece, q_other, g_other))
    along_z = [piece] + [swapped(piece, "ctx", 2 * s) for s in range(1, half)]
    early = (half + 1) // 2
    z_early, z_late = jnp.stack(along_z[:early]), jnp.stack(along_z[early:])
    x_early = swapped(z_early, "ctx", 1)
    far_send = column_block(w_query, head ^ 3, share, z_early)
    far_mine = column_block(w_query, head ^ 2, share, z_early)
    z_late, x_early, far_send, far_mine = lax.optimization_barrier((z_late, x_early, far_send, far_mine))
    x_late = swapped(z_late, "ctx", 1)
    far_other = swapped(far_send, "head", 1)
    here_z = jnp.concatenate([z_early, z_late])
    there_z = swapped(here_z, "head", 1)
    here_x = jnp.concatenate([x_early, x_late])
    pieces = (here_z, there_z, here_x, swapped(here_x, "head", 1))
    dq, back = attention(core, positions, doc_ids, queries, q_other, dout, g_other, pieces)

    part = product(dq, far_mine, far_other, 0, share, jnp.bfloat16)
    far = swapped(part, "head", 2)

    back, part = lax.optimization_barrier((back, part))
    pair = back[:half].astype(jnp.float32) + swapped(back[half:], "ctx", 1).astype(jnp.float32)
    mine = pair[0]
    for s in range(1, half):
        mine = mine + swapped(pair[s].astype(jnp.bfloat16), "ctx", 2 * s).astype(jnp.float32)
    mine = mine.astype(jnp.bfloat16)
    kv = jnp.concatenate([mine, swapped(mine, "head", 1)], axis=1)
    kv_far = swapped(kv, "head", 2)

    acc, *give = own(dq, *carve([head, head ^ 1], w_query, share, kv))
    given = [swapped(one, "head", 1) for one in give]
    return finish(core, kv, kv_far, w_kv, acc, far, given)


def solution(mesh):
    placed = (
        P("ctx", "head"),
        P("ctx", None),
        P("ctx", None),
        P("ctx", "head"),
        P("ctx"),
        P("ctx"),
        P("head", None),
        P(None, "head"),
    )
    return jax.shard_map(
        on_device, mesh=mesh, in_specs=placed, out_specs=P("ctx", "head"), check_vma=False
    )
```

```python
import functools
import math

import jax
import jax.numpy as jnp
from jax import lax
from jax.experimental import pallas as pl
from jax.experimental.pallas import tpu as pltpu
from jax.sharding import PartitionSpec as P

RUN = 64
META_ROWS = 16
TILES = 4
HALVES = 2
GIVES = 2
ANY = pl.BlockSpec(memory_space=pl.ANY)
HBM = pl.BlockSpec(memory_space=pltpu.HBM)
SMEM = pl.BlockSpec(memory_space=pltpu.SMEM)


def params(limit_mib=16):
    return pltpu.CompilerParams(vmem_limit_bytes=limit_mib * 1024 * 1024)


def swapped(value, axis, bits):
    count = lax.axis_size(axis)
    return lax.ppermute(value, axis, [(source, source ^ bits) for source in range(count)])


def dot(a, b, contract):
    return lax.dot_general(a, b, (contract, ((), ())), preferred_element_type=jnp.float32)


def each(count, body, state):
    if count > 8:
        return lax.fori_loop(0, count, body, state)
    for step in range(count):
        state = body(step, state)
    return state


def pack(core, positions, keys, values):
    rows, size = keys.shape
    held = jnp.where(core == 0, keys, values)
    runs = (positions.reshape(rows // RUN, RUN)[:, :1] // RUN).astype(jnp.bfloat16)
    meta = jnp.pad(jnp.broadcast_to(runs, (rows // RUN, size)), ((0, META_ROWS - rows // RUN), (0, 0)))
    return jnp.concatenate([held, meta], axis=0)


def column_block(w_query, block, share, after):
    w_query, _ = lax.optimization_barrier((w_query, after))
    return lax.dynamic_slice_in_dim(w_query, block * share, share, axis=1)


def carve_kernel(block_ref, w_ref, *refs):
    outs, sems = refs[1:-1], refs[-1]
    rows, share = outs[0].shape
    parts = sems.shape[1]
    copies = []
    for i, out_ref in enumerate(outs):
        at = pl.multiple_of(block_ref[i] * share, share)
        for j in range(parts):
            part = slice(j * (rows // parts), (j + 1) * (rows // parts))
            source = w_ref.at[part, pl.ds(at, share)]
            copies.append(pltpu.make_async_copy(source, out_ref.at[part, :], sems.at[i, j]))
            copies[-1].start()
    for one in copies:
        one.wait()


def carve(blocks, w_query, share, after):
    block = jax.ShapeDtypeStruct((w_query.shape[0], share), w_query.dtype)
    count = len(blocks)
    return pl.pallas_call(
        carve_kernel,
        out_shape=[block] * count,
        in_specs=[SMEM, HBM, ANY],
        out_specs=[pl.BlockSpec(memory_space=pltpu.VMEM)] * count,
        scratch_shapes=[pltpu.SemaphoreType.DMA((count, 4))],
        compiler_params=params(48),
        cost_estimate=pl.CostEstimate(flops=0, bytes_accessed=0, transcendentals=0),
        name="carve",
    )(jnp.stack(blocks), w_query, after)


def attention_kernel(core_ref, pos_ref, doc_ref, qm_ref, qo_ref, gm_ref, go_ref, *refs):
    groups = [refs[i : i + 2] for i in range(0, len(refs) - 4, 2)]
    dq_ref, back_ref, s_ref, dp_ref = refs[-4:]
    count, rows, size = back_ref.shape
    part = count // len(groups)
    heads = qm_ref.shape[1] // size
    is_key = core_ref[0] == 0
    inv_root = 1.0 / math.sqrt(size)

    def stack(mine_ref, other_ref):
        parts = [ref[:, h * size : (h + 1) * size] for ref in (mine_ref, other_ref) for h in range(heads)]
        return jnp.concatenate(parts, axis=0)

    query = stack(qm_ref, qo_ref)
    grad = stack(gm_ref, go_ref)
    wide = query.shape[0]
    last = jnp.concatenate([pos_ref[...].astype(jnp.float32)] * (2 * heads), axis=1)
    first = jnp.concatenate([(doc_ref[...] * RUN).astype(jnp.float32)] * (2 * heads), axis=1)
    offset = lax.broadcasted_iota(jnp.int32, (RUN, wide), 0).astype(jnp.float32)

    def everywhere(body, state):
        for group, (here_ref, there_ref) in enumerate(groups):
            state = each(part, lambda s, now: body(s, group * part + s, here_ref, there_ref, now), state)
        return state

    def scores(s, slot, here_ref, there_ref, top):
        here = here_ref[s, 0:rows, :]
        there = there_ref[s, 0:rows, :]
        key = jnp.where(is_key, here, there)
        value = jnp.where(is_key, there, here)
        score = dot(key, query, ((1,), (1,))) * inv_root
        dp_ref[slot] = dot(value, grad, ((1,), (1,)))
        meta = here_ref[s, rows : rows + META_ROWS, :].astype(jnp.float32)
        for run in range(rows // RUN):
            start = meta[run : run + 1, 0:1] * float(RUN)
            pos = offset + start
            allowed = (pos <= last) & (pos >= first)
            held = jnp.where(allowed, score[run * RUN : (run + 1) * RUN], -1e30)
            s_ref[slot, run * RUN : (run + 1) * RUN, :] = held
            top = jnp.maximum(top, jnp.max(held, axis=0, keepdims=True))
        return top

    top = everywhere(scores, jnp.full((1, wide), -1e30, jnp.float32))

    def weights(slot, state):
        total, mixed = state
        weight = jnp.exp(s_ref[slot] - top)
        s_ref[slot] = weight
        total = total + jnp.sum(weight, axis=0, keepdims=True)
        mixed = mixed + jnp.sum(weight * dp_ref[slot], axis=0, keepdims=True)
        return total, mixed

    zeros = jnp.zeros((1, wide), jnp.float32)
    total, mixed = each(count, weights, (zeros, zeros))
    scale = 1.0 / total
    delta = mixed * scale
    other = jnp.where(is_key, query, grad)

    def gradients(s, slot, here_ref, there_ref, dq):
        prob = s_ref[slot] * scale
        dscore = (prob * (dp_ref[slot] - delta)).astype(jnp.bfloat16)
        picked = jnp.where(is_key, dscore, prob.astype(jnp.bfloat16))
        back_ref[slot] = dot(picked, other, ((1,), (0,))).astype(jnp.bfloat16)
        key = jnp.where(is_key, here_ref[s, 0:rows, :], there_ref[s, 0:rows, :])
        return dq + dot(key, dscore, ((0,), (0,)))

    dq = everywhere(gradients, jnp.zeros((size, wide), jnp.float32)) * inv_root
    for h in range(wide // rows):
        block = dq[:, h * rows : (h + 1) * rows]
        dq_ref[:, h * size : (h + 1) * size] = block.T.astype(jnp.bfloat16)


def attention(core, positions, doc_ids, q_mine, q_other, g_mine, g_other, pieces):
    rows, width = q_mine.shape
    size = pieces[0].shape[2]
    count = sum(one.shape[0] for one in pieces) // 2
    wide = 2 * rows * (width // size)
    return pl.pallas_call(
        attention_kernel,
        out_shape=[
            jax.ShapeDtypeStruct((rows, 2 * width), jnp.bfloat16),
            jax.ShapeDtypeStruct((count, rows, size), jnp.bfloat16),
        ],
        in_specs=[SMEM] + [pl.BlockSpec()] * (6 + len(pieces)),
        out_specs=[pl.BlockSpec()] * 2,
        scratch_shapes=[pltpu.VMEM((count, rows, wide), jnp.float32)] * 2,
        compiler_params=params(8 + count * rows * wide // 2**17),
        cost_estimate=pl.CostEstimate(
            flops=10 * count * rows * wide * size,
            bytes_accessed=count * rows * size * 8,
            transcendentals=count * rows * wide,
        ),
        name="attention",
    )(
        core, positions.reshape(1, rows), doc_ids.reshape(1, rows), q_mine, q_other, g_mine, g_other, *pieces
    )


def product_kernel(dq_ref, *refs):
    out_ref = refs[-1]
    for i in range(HALVES):
        mine_ref, other_ref = refs[i], refs[HALVES + i]
        depth, width = mine_ref.shape
        acc = dot(dq_ref[:, 0:depth], mine_ref[...], ((1,), (0,)))
        acc = acc + dot(dq_ref[:, depth:], other_ref[...], ((1,), (0,)))
        out_ref[:, i * width : (i + 1) * width] = acc.astype(out_ref.dtype)


def product(dq, w_mine, w_other, dtype):
    rows, depth = dq.shape
    share = HALVES * w_mine[0].shape[1]
    return pl.pallas_call(
        product_kernel,
        out_shape=jax.ShapeDtypeStruct((rows, share), dtype),
        in_specs=[pl.BlockSpec()] * (1 + 2 * HALVES),
        out_specs=pl.BlockSpec(),
        compiler_params=params(),
        cost_estimate=pl.CostEstimate(
            flops=2 * rows * depth * share, bytes_accessed=2 * depth * share, transcendentals=0
        ),
        name="product",
    )(dq, *w_mine, *w_other)


def own_kernel(dq_ref, wn_ref, wo_ref, acc_ref, *give_refs):
    depth, share = wn_ref.shape
    dq = dq_ref[:, 0:depth]
    width = share // len(give_refs)
    for i, give_ref in enumerate(give_refs):
        give_ref[...] = dot(dq, wo_ref[:, i * width : (i + 1) * width], ((1,), (0,))).astype(jnp.bfloat16)
    acc_ref[...] = dot(dq, wn_ref[...], ((1,), (0,)))


def own(dq, w_near, w_other):
    rows = dq.shape[0]
    share = w_near.shape[1]
    return pl.pallas_call(
        own_kernel,
        out_shape=[jax.ShapeDtypeStruct((rows, share), jnp.float32)]
        + [jax.ShapeDtypeStruct((rows, share // GIVES), jnp.bfloat16)] * GIVES,
        in_specs=[pl.BlockSpec()] * 3,
        out_specs=[pl.BlockSpec()] * (1 + GIVES),
        compiler_params=params(),
        cost_estimate=pl.CostEstimate(flops=0, bytes_accessed=0, transcendentals=0),
        name="own",
    )(dq, w_near, w_other)


def finish_kernel(core_ref, kv_ref, kv_far_ref, w_ref, acc_ref, far_ref, *refs):
    out_ref, hold_ref, sems = refs[GIVES:]
    rows, share = acc_ref.shape
    pair = kv_ref.shape[1]
    size = pair // 2
    tile = share // TILES
    inv_root = 1.0 / math.sqrt(size)
    column = lax.broadcasted_iota(jnp.int32, (1, pair), 1)
    is_key = (column < size) == (core_ref[0] == 0)
    kv = kv_ref[...].astype(jnp.float32) + kv_far_ref[...].astype(jnp.float32)
    kv = (kv * jnp.where(is_key, inv_root, 1.0)).astype(jnp.bfloat16)
    at_mine = pl.ds(pl.multiple_of(core_ref[0] * size, size), size)
    at_other = pl.ds(pl.multiple_of((1 - core_ref[0]) * size, size), size)
    copies = []
    for i in range(TILES):
        at = slice(i * tile, (i + 1) * tile)
        w = jnp.concatenate([w_ref[at_mine, at], w_ref[at_other, at]], axis=0)
        given_ref = refs[i * GIVES // TILES]
        skip = i * GIVES // TILES * (share // GIVES)
        given = given_ref[:, i * tile - skip : (i + 1) * tile - skip]
        acc = acc_ref[:, at] + far_ref[:, at].astype(jnp.float32) + given.astype(jnp.float32)
        acc = acc + dot(kv, w, ((1,), (0,)))
        hold_ref[:, at] = acc.astype(jnp.bfloat16)
        copies.append(pltpu.make_async_copy(hold_ref.at[:, at], out_ref.at[:, at], sems.at[i]))
        copies[i].start()
    for one in copies:
        one.wait()


def finish(core, kv, kv_far, w_kv, acc, far, given):
    rows, share = acc.shape
    return pl.pallas_call(
        finish_kernel,
        out_shape=jax.ShapeDtypeStruct((rows, share), jnp.bfloat16),
        in_specs=[SMEM] + [pl.BlockSpec()] * (5 + GIVES),
        out_specs=ANY,
        scratch_shapes=[pltpu.VMEM((rows, share), jnp.bfloat16), pltpu.SemaphoreType.DMA((TILES,))],
        compiler_params=params(),
        cost_estimate=pl.CostEstimate(
            flops=2 * rows * kv.shape[1] * share, bytes_accessed=10 * rows * share, transcendentals=0
        ),
        name="finish",
    )(core, kv, kv_far, w_kv, acc, far, *given)


def on_device(queries, keys, values, dout, positions, doc_ids, w_query, w_kv):
    half = lax.axis_size("ctx") // 2
    head = lax.axis_index("head").astype(jnp.int32)
    core = (head & 1).reshape(1)
    share = w_kv.shape[1]
    local_heads = queries.shape[1] // keys.shape[1]

    q_other = swapped(queries, "head", 1)
    g_other = swapped(dout, "head", 1)
    piece = pack(core, positions, keys, values)
    piece, q_other, g_other = lax.optimization_barrier((piece, q_other, g_other))
    along_z = [piece] + [swapped(piece, "ctx", 2 * s) for s in range(1, half)]
    early = (half + 1) // 2
    z_early, z_late = jnp.stack(along_z[:early]), jnp.stack(along_z[early:])
    x_early = swapped(z_early, "ctx", 1)
    z_late, x_early = lax.optimization_barrier((z_late, x_early))
    x_late = swapped(z_late, "ctx", 1)
    here_z = jnp.concatenate([z_early, z_late])
    there_z = swapped(here_z, "head", 1)

    def halves(block):
        return [column_block(w_query, block * HALVES + i, share // HALVES, z_late) for i in range(HALVES)]

    x_late, there_z, *far = lax.optimization_barrier((x_late, there_z, *halves(head ^ 3), *halves(head ^ 2)))
    far_send, far_mine = far[:HALVES], far[HALVES:]
    here_x = jnp.concatenate([x_early, x_late])
    there_x = swapped(here_x, "head", 1)
    far_other = [swapped(far_send[0], "head", 1)]
    there_x, *rest = lax.optimization_barrier((there_x, *far_send[1:]))
    far_other += [swapped(one, "head", 1) for one in rest]
    pieces = (here_z, there_z, here_x, there_x)
    dq, back = attention(core, positions, doc_ids, queries, q_other, dout, g_other, pieces)

    part = product(dq, far_mine, far_other, jnp.bfloat16)
    far = swapped(part, "head", 2)

    back, part = lax.optimization_barrier((back, part))
    pair = back[:half].astype(jnp.float32) + swapped(back[half:], "ctx", 1).astype(jnp.float32)
    mine = pair[0]
    for s in range(1, half):
        mine = mine + swapped(pair[s].astype(jnp.bfloat16), "ctx", 2 * s).astype(jnp.float32)
    mine = mine.astype(jnp.bfloat16)
    kv = jnp.concatenate([mine, swapped(mine, "head", 1)], axis=1)
    kv_far = swapped(kv, "head", 2)

    acc, *give = own(dq, *carve([head, head ^ 1], w_query, share, kv))
    given = [swapped(one, "head", 1) for one in give]
    return finish(core, kv, kv_far, w_kv, acc, far, given)


def solution(mesh):
    placed = (
        P("ctx", "head"),
        P("ctx", None),
        P("ctx", None),
        P("ctx", "head"),
        P("ctx"),
        P("ctx"),
        P("head", None),
        P(None, "head"),
    )
    return jax.shard_map(
        on_device, mesh=mesh, in_specs=placed, out_specs=P("ctx", "head"), check_vma=False
    )
```

```python
import functools
import math

import jax
import jax.numpy as jnp
from jax import lax
from jax.experimental import pallas as pl
from jax.experimental.pallas import tpu as pltpu
from jax.sharding import PartitionSpec as P

RUN = 64
META_ROWS = 16
TILES = 4
GIVES = 2
ANY = pl.BlockSpec(memory_space=pl.ANY)
HBM = pl.BlockSpec(memory_space=pltpu.HBM)
SMEM = pl.BlockSpec(memory_space=pltpu.SMEM)


def params(limit_mib=16):
    return pltpu.CompilerParams(vmem_limit_bytes=limit_mib * 1024 * 1024)


def swapped(value, axis, bits):
    count = lax.axis_size(axis)
    return lax.ppermute(value, axis, [(source, source ^ bits) for source in range(count)])


def dot(a, b, contract):
    return lax.dot_general(a, b, (contract, ((), ())), preferred_element_type=jnp.float32)


def each(count, body, state):
    if count > 8:
        return lax.fori_loop(0, count, body, state)
    for step in range(count):
        state = body(step, state)
    return state


def pack(core, positions, keys, values):
    rows, size = keys.shape
    held = jnp.where(core == 0, keys, values)
    runs = (positions.reshape(rows // RUN, RUN)[:, :1] // RUN).astype(jnp.bfloat16)
    meta = jnp.pad(jnp.broadcast_to(runs, (rows // RUN, size)), ((0, META_ROWS - rows // RUN), (0, 0)))
    return jnp.concatenate([held, meta], axis=0)


def column_block(w_query, block, share, after):
    w_query, _ = lax.optimization_barrier((w_query, after))
    return lax.dynamic_slice_in_dim(w_query, block * share, share, axis=1)


def carve_kernel(block_ref, w_ref, *refs):
    outs, sems = refs[1:-1], refs[-1]
    rows, share = outs[0].shape
    parts = sems.shape[1]
    copies = []
    for i, out_ref in enumerate(outs):
        at = pl.multiple_of(block_ref[i] * share, share)
        for j in range(parts):
            part = slice(j * (rows // parts), (j + 1) * (rows // parts))
            source = w_ref.at[part, pl.ds(at, share)]
            copies.append(pltpu.make_async_copy(source, out_ref.at[part, :], sems.at[i, j]))
            copies[-1].start()
    for one in copies:
        one.wait()


def carve(blocks, w_query, share, after):
    block = jax.ShapeDtypeStruct((w_query.shape[0], share), w_query.dtype)
    count = len(blocks)
    return pl.pallas_call(
        carve_kernel,
        out_shape=[block] * count,
        in_specs=[SMEM, HBM, ANY],
        out_specs=[pl.BlockSpec(memory_space=pltpu.VMEM)] * count,
        scratch_shapes=[pltpu.SemaphoreType.DMA((count, 4))],
        compiler_params=params(48),
        cost_estimate=pl.CostEstimate(flops=0, bytes_accessed=0, transcendentals=0),
        name="carve",
    )(jnp.stack(blocks), w_query, after)


def attention_kernel(core_ref, pos_ref, doc_ref, qm_ref, qo_ref, gm_ref, go_ref, *refs):
    groups = [refs[i : i + 2] for i in range(0, len(refs) - 4, 2)]
    dq_ref, back_ref, s_ref, dp_ref = refs[-4:]
    count, rows, size = back_ref.shape
    part = count // len(groups)
    heads = qm_ref.shape[1] // size
    is_key = core_ref[0] == 0
    inv_root = 1.0 / math.sqrt(size)

    def stack(mine_ref, other_ref):
        parts = [ref[:, h * size : (h + 1) * size] for ref in (mine_ref, other_ref) for h in range(heads)]
        return jnp.concatenate(parts, axis=0)

    query = stack(qm_ref, qo_ref)
    grad = stack(gm_ref, go_ref)
    wide = query.shape[0]
    last = jnp.concatenate([pos_ref[...].astype(jnp.float32)] * (2 * heads), axis=1)
    first = jnp.concatenate([(doc_ref[...] * RUN).astype(jnp.float32)] * (2 * heads), axis=1)
    offset = lax.broadcasted_iota(jnp.int32, (RUN, wide), 0).astype(jnp.float32)

    def everywhere(body, state):
        for group, (here_ref, there_ref) in enumerate(groups):
            state = each(part, lambda s, now: body(s, group * part + s, here_ref, there_ref, now), state)
        return state

    def scores(s, slot, here_ref, there_ref, top):
        here = here_ref[s, 0:rows, :]
        there = there_ref[s, 0:rows, :]
        key = jnp.where(is_key, here, there)
        value = jnp.where(is_key, there, here)
        score = dot(key, query, ((1,), (1,)))
        dp_ref[slot] = dot(value, grad, ((1,), (1,)))
        meta = here_ref[s, rows : rows + META_ROWS, :].astype(jnp.float32)
        for run in range(rows // RUN):
            start = meta[run : run + 1, 0:1] * float(RUN)
            pos = offset + start
            allowed = (pos <= last) & (pos >= first)
            held = jnp.where(allowed, score[run * RUN : (run + 1) * RUN], -1e30)
            s_ref[slot, run * RUN : (run + 1) * RUN, :] = held
            top = jnp.maximum(top, jnp.max(held, axis=0, keepdims=True))
        return top

    top = everywhere(scores, jnp.full((1, wide), -1e30, jnp.float32))

    def weights(slot, state):
        total, mixed = state
        weight = jnp.exp((s_ref[slot] - top) * inv_root)
        s_ref[slot] = weight
        total = total + jnp.sum(weight, axis=0, keepdims=True)
        mixed = mixed + jnp.sum(weight * dp_ref[slot], axis=0, keepdims=True)
        return total, mixed

    zeros = jnp.zeros((1, wide), jnp.float32)
    total, mixed = each(count, weights, (zeros, zeros))
    scale = 1.0 / total
    delta = mixed * scale
    other = jnp.where(is_key, query, grad)

    def gradients(s, slot, here_ref, there_ref, dq):
        prob = s_ref[slot] * scale
        dscore = (prob * (dp_ref[slot] - delta)).astype(jnp.bfloat16)
        picked = jnp.where(is_key, dscore, prob.astype(jnp.bfloat16))
        back_ref[slot] = dot(picked, other, ((1,), (0,))).astype(jnp.bfloat16)
        key = jnp.where(is_key, here_ref[s, 0:rows, :], there_ref[s, 0:rows, :])
        return dq + dot(key, dscore, ((0,), (0,)))

    dq = everywhere(gradients, jnp.zeros((size, wide), jnp.float32)) * inv_root
    for h in range(wide // rows):
        block = dq[:, h * rows : (h + 1) * rows]
        dq_ref[:, h * size : (h + 1) * size] = block.T.astype(jnp.bfloat16)


def attention(core, positions, doc_ids, q_mine, q_other, g_mine, g_other, pieces):
    rows, width = q_mine.shape
    size = pieces[0].shape[2]
    count = sum(one.shape[0] for one in pieces) // 2
    wide = 2 * rows * (width // size)
    return pl.pallas_call(
        attention_kernel,
        out_shape=[
            jax.ShapeDtypeStruct((rows, 2 * width), jnp.bfloat16),
            jax.ShapeDtypeStruct((count, rows, size), jnp.bfloat16),
        ],
        in_specs=[SMEM] + [pl.BlockSpec()] * (6 + len(pieces)),
        out_specs=[pl.BlockSpec()] * 2,
        scratch_shapes=[pltpu.VMEM((count, rows, wide), jnp.float32)] * 2,
        compiler_params=params(8 + count * rows * wide // 2**17),
        cost_estimate=pl.CostEstimate(
            flops=10 * count * rows * wide * size,
            bytes_accessed=count * rows * size * 8,
            transcendentals=count * rows * wide,
        ),
        name="attention",
    )(
        core, positions.reshape(1, rows), doc_ids.reshape(1, rows), q_mine, q_other, g_mine, g_other, *pieces
    )


def product_kernel(first, dq_ref, wm_ref, wo_ref, out_ref):
    depth = wm_ref.shape[0]
    at = slice(first, first + out_ref.shape[1])
    acc = dot(dq_ref[:, 0:depth], wm_ref[:, at], ((1,), (0,)))
    acc = acc + dot(dq_ref[:, depth:], wo_ref[:, at], ((1,), (0,)))
    out_ref[...] = acc.astype(out_ref.dtype)


def product(dq, w_mine, w_other, first, width, dtype):
    rows, depth = dq.shape
    return pl.pallas_call(
        functools.partial(product_kernel, first),
        out_shape=jax.ShapeDtypeStruct((rows, width), dtype),
        in_specs=[pl.BlockSpec()] * 3,
        out_specs=pl.BlockSpec(),
        compiler_params=params(),
        cost_estimate=pl.CostEstimate(
            flops=2 * rows * depth * width, bytes_accessed=2 * depth * width, transcendentals=0
        ),
        name="product",
    )(dq, w_mine, w_other)


def own_kernel(dq_ref, wn_ref, wo_ref, acc_ref, *give_refs):
    depth, share = wn_ref.shape
    dq = dq_ref[:, 0:depth]
    width = share // len(give_refs)
    for i, give_ref in enumerate(give_refs):
        give_ref[...] = dot(dq, wo_ref[:, i * width : (i + 1) * width], ((1,), (0,))).astype(jnp.bfloat16)
    acc_ref[...] = dot(dq, wn_ref[...], ((1,), (0,)))


def own(dq, w_near, w_other):
    rows = dq.shape[0]
    share = w_near.shape[1]
    return pl.pallas_call(
        own_kernel,
        out_shape=[jax.ShapeDtypeStruct((rows, share), jnp.float32)]
        + [jax.ShapeDtypeStruct((rows, share // GIVES), jnp.bfloat16)] * GIVES,
        in_specs=[pl.BlockSpec()] * 3,
        out_specs=[pl.BlockSpec()] * (1 + GIVES),
        compiler_params=params(),
        cost_estimate=pl.CostEstimate(flops=0, bytes_accessed=0, transcendentals=0),
        name="own",
    )(dq, w_near, w_other)


def gather_kernel(acc_ref, far_ref, *refs):
    given, out_ref = refs[:GIVES], refs[GIVES]
    width = out_ref.shape[1] // GIVES
    for i in range(GIVES):
        at = slice(i * width, (i + 1) * width)
        out_ref[:, at] = acc_ref[:, at] + far_ref[:, at].astype(jnp.float32) + given[i][...].astype(jnp.float32)


def gathered(acc, far, given):
    return pl.pallas_call(
        gather_kernel,
        out_shape=jax.ShapeDtypeStruct(acc.shape, acc.dtype),
        in_specs=[pl.BlockSpec()] * (2 + GIVES),
        out_specs=pl.BlockSpec(),
        input_output_aliases={0: 0},
        compiler_params=params(),
        cost_estimate=pl.CostEstimate(flops=0, bytes_accessed=0, transcendentals=0),
        name="gathered",
    )(acc, far, *given)


def finish_kernel(core_ref, kv_ref, kv_far_ref, w_ref, sum_ref, out_ref, hold_ref, sems):
    rows, share = sum_ref.shape
    size = kv_ref.shape[1] // 2
    tile = share // TILES
    kv = kv_ref[...].astype(jnp.float32) + kv_far_ref[...].astype(jnp.float32)
    mine, other = kv[:, :size], kv[:, size:]
    is_key = core_ref[0] == 0
    key = jnp.where(is_key, mine, other) * (1.0 / math.sqrt(size))
    kv = jnp.concatenate([key, jnp.where(is_key, other, mine)], axis=1).astype(jnp.bfloat16)
    copies = []
    for i in range(TILES):
        at = slice(i * tile, (i + 1) * tile)
        hold_ref[:, at] = (sum_ref[:, at] + dot(kv, w_ref[:, at], ((1,), (0,)))).astype(jnp.bfloat16)
        copies.append(pltpu.make_async_copy(hold_ref.at[:, at], out_ref.at[:, at], sems.at[i]))
        copies[i].start()
    for one in copies:
        one.wait()


def finish(core, kv, kv_far, w_kv, total):
    return pl.pallas_call(
        finish_kernel,
        out_shape=jax.ShapeDtypeStruct(total.shape, jnp.bfloat16),
        in_specs=[SMEM] + [pl.BlockSpec()] * 4,
        out_specs=ANY,
        scratch_shapes=[pltpu.VMEM(total.shape, jnp.bfloat16), pltpu.SemaphoreType.DMA((TILES,))],
        compiler_params=params(),
        name="finish",
    )(core, kv, kv_far, w_kv, total)


def on_device(queries, keys, values, dout, positions, doc_ids, w_query, w_kv):
    half = lax.axis_size("ctx") // 2
    head = lax.axis_index("head").astype(jnp.int32)
    core = (head & 1).reshape(1)
    share = w_kv.shape[1]
    local_heads = queries.shape[1] // keys.shape[1]

    q_other = swapped(queries, "head", 1)
    g_other = swapped(dout, "head", 1)
    piece = pack(core, positions, keys, values)
    piece, q_other, g_other = lax.optimization_barrier((piece, q_other, g_other))
    along_z = [piece] + [swapped(piece, "ctx", 2 * s) for s in range(1, half)]
    early = (half + 1) // 2
    z_early, z_late = jnp.stack(along_z[:early]), jnp.stack(along_z[early:])
    x_early = swapped(z_early, "ctx", 1)
    far_send = column_block(w_query, head ^ 3, share, z_early)
    far_mine = column_block(w_query, head ^ 2, share, z_early)
    there_early = swapped(z_early, "head", 1)
    z_late, x_early, there_early, far_send, far_mine = lax.optimization_barrier(
        (z_late, x_early, there_early, far_send, far_mine)
    )
    x_late = swapped(z_late, "ctx", 1)
    far_other = swapped(far_send, "head", 1)
    pieces = [z_early, there_early]
    for here in (z_late, x_early, x_late):
        pieces += [here, swapped(here, "head", 1)]
    dq, back = attention(core, positions, doc_ids, queries, q_other, dout, g_other, pieces)

    part = product(dq, far_mine, far_other, 0, share, jnp.bfloat16)
    far = swapped(part, "head", 2)

    back, part = lax.optimization_barrier((back, part))
    pair = back[:half].astype(jnp.float32) + swapped(back[half:], "ctx", 1).astype(jnp.float32)
    mine = pair[0]
    for s in range(1, half):
        mine = mine + swapped(pair[s].astype(jnp.bfloat16), "ctx", 2 * s).astype(jnp.float32)
    mine = mine.astype(jnp.bfloat16)
    kv = jnp.concatenate([mine, swapped(mine, "head", 1)], axis=1)
    kv_far = swapped(kv, "head", 2)

    acc, *give = own(dq, *carve([head, head ^ 1], w_query, share, kv))
    given = [swapped(one, "head", 1) for one in give]
    return finish(core, kv, kv_far, w_kv, gathered(acc, far, given))


def solution(mesh):
    placed = (
        P("ctx", "head"),
        P("ctx", None),
        P("ctx", None),
        P("ctx", "head"),
        P("ctx"),
        P("ctx"),
        P("head", None),
        P(None, "head"),
    )
    return jax.shard_map(
        on_device, mesh=mesh, in_specs=placed, out_specs=P("ctx", "head"), check_vma=False
    )
```

```python
import functools
import math

import jax
import jax.numpy as jnp
from jax import lax
from jax.experimental import pallas as pl
from jax.experimental.pallas import tpu as pltpu
from jax.sharding import PartitionSpec as P

RUN = 64
META_ROWS = 16
TILES = 4
GIVES = 2
ANY = pl.BlockSpec(memory_space=pl.ANY)
HBM = pl.BlockSpec(memory_space=pltpu.HBM)
SMEM = pl.BlockSpec(memory_space=pltpu.SMEM)


def params(limit_mib=16):
    return pltpu.CompilerParams(vmem_limit_bytes=limit_mib * 1024 * 1024)


def swapped(value, axis, bits):
    count = lax.axis_size(axis)
    return lax.ppermute(value, axis, [(source, source ^ bits) for source in range(count)])


def dot(a, b, contract):
    return lax.dot_general(a, b, (contract, ((), ())), preferred_element_type=jnp.float32)


def each(count, body, state):
    if count > 8:
        return lax.fori_loop(0, count, body, state)
    for step in range(count):
        state = body(step, state)
    return state


def pack(core, positions, keys, values):
    rows, size = keys.shape
    held = jnp.where(core == 0, keys, values)
    runs = (positions.reshape(rows // RUN, RUN)[:, :1] // RUN).astype(jnp.bfloat16)
    meta = jnp.pad(jnp.broadcast_to(runs, (rows // RUN, size)), ((0, META_ROWS - rows // RUN), (0, 0)))
    return jnp.concatenate([held, meta], axis=0)


def column_block(w_query, block, share, after):
    w_query, _ = lax.optimization_barrier((w_query, after))
    return lax.dynamic_slice_in_dim(w_query, block * share, share, axis=1)


def carve_kernel(block_ref, w_ref, *refs):
    outs, sems = refs[1:-1], refs[-1]
    rows, share = outs[0].shape
    parts = sems.shape[1]
    copies = []
    for i, out_ref in enumerate(outs):
        at = pl.multiple_of(block_ref[i] * share, share)
        for j in range(parts):
            part = slice(j * (rows // parts), (j + 1) * (rows // parts))
            source = w_ref.at[part, pl.ds(at, share)]
            copies.append(pltpu.make_async_copy(source, out_ref.at[part, :], sems.at[i, j]))
            copies[-1].start()
    for one in copies:
        one.wait()


def carve(blocks, w_query, share, after):
    block = jax.ShapeDtypeStruct((w_query.shape[0], share), w_query.dtype)
    count = len(blocks)
    return pl.pallas_call(
        carve_kernel,
        out_shape=[block] * count,
        in_specs=[SMEM, HBM, ANY],
        out_specs=[pl.BlockSpec(memory_space=pltpu.VMEM)] * count,
        scratch_shapes=[pltpu.SemaphoreType.DMA((count, 4))],
        compiler_params=params(48),
        cost_estimate=pl.CostEstimate(flops=0, bytes_accessed=0, transcendentals=0),
        name="carve",
    )(jnp.stack(blocks), w_query, after)


def attention_kernel(core_ref, pos_ref, doc_ref, qm_ref, qo_ref, gm_ref, go_ref, *refs):
    groups = [refs[i : i + 2] for i in range(0, len(refs) - 4, 2)]
    dq_ref, back_ref, s_ref, dp_ref = refs[-4:]
    count, rows, size = back_ref.shape
    part = count // len(groups)
    heads = qm_ref.shape[1] // size
    is_key = core_ref[0] == 0
    inv_root = 1.0 / math.sqrt(size)

    def stack(mine_ref, other_ref):
        parts = [ref[:, h * size : (h + 1) * size] for ref in (mine_ref, other_ref) for h in range(heads)]
        return jnp.concatenate(parts, axis=0)

    query = stack(qm_ref, qo_ref)
    grad = stack(gm_ref, go_ref)
    wide = query.shape[0]
    last = jnp.concatenate([pos_ref[...].astype(jnp.float32)] * (2 * heads), axis=1)
    first = jnp.concatenate([(doc_ref[...] * RUN).astype(jnp.float32)] * (2 * heads), axis=1)
    offset = lax.broadcasted_iota(jnp.int32, (RUN, wide), 0).astype(jnp.float32)

    def everywhere(body, state):
        for group, (here_ref, there_ref) in enumerate(groups):
            state = each(part, lambda s, now: body(s, group * part + s, here_ref, there_ref, now), state)
        return state

    def scores(s, slot, here_ref, there_ref, top):
        here = here_ref[s, 0:rows, :]
        there = there_ref[s, 0:rows, :]
        key = jnp.where(is_key, here, there)
        value = jnp.where(is_key, there, here)
        score = dot(key, query, ((1,), (1,))) * inv_root
        dp_ref[slot] = dot(value, grad, ((1,), (1,)))
        meta = here_ref[s, rows : rows + META_ROWS, :].astype(jnp.float32)
        for run in range(rows // RUN):
            start = meta[run : run + 1, 0:1] * float(RUN)
            pos = offset + start
            allowed = (pos <= last) & (pos >= first)
            held = jnp.where(allowed, score[run * RUN : (run + 1) * RUN], -1e30)
            s_ref[slot, run * RUN : (run + 1) * RUN, :] = held
            top = jnp.maximum(top, jnp.max(held, axis=0, keepdims=True))
        return top

    top = everywhere(scores, jnp.full((1, wide), -1e30, jnp.float32))

    def weights(slot, state):
        total, mixed = state
        weight = jnp.exp(s_ref[slot] - top)
        s_ref[slot] = weight
        total = total + jnp.sum(weight, axis=0, keepdims=True)
        mixed = mixed + jnp.sum(weight * dp_ref[slot], axis=0, keepdims=True)
        return total, mixed

    zeros = jnp.zeros((1, wide), jnp.float32)
    total, mixed = each(count, weights, (zeros, zeros))
    scale = 1.0 / total
    delta = mixed * scale
    other = jnp.where(is_key, query, grad)

    def gradients(s, slot, here_ref, there_ref, dq):
        prob = s_ref[slot] * scale
        dscore = (prob * (dp_ref[slot] - delta)).astype(jnp.bfloat16)
        picked = jnp.where(is_key, dscore, prob.astype(jnp.bfloat16))
        back_ref[slot] = dot(picked, other, ((1,), (0,))).astype(jnp.bfloat16)
        key = jnp.where(is_key, here_ref[s, 0:rows, :], there_ref[s, 0:rows, :])
        return dq + dot(key, dscore, ((0,), (0,)))

    dq = everywhere(gradients, jnp.zeros((size, wide), jnp.float32)) * inv_root
    for h in range(wide // rows):
        block = dq[:, h * rows : (h + 1) * rows]
        dq_ref[:, h * size : (h + 1) * size] = block.T.astype(jnp.bfloat16)


def attention(core, positions, doc_ids, q_mine, q_other, g_mine, g_other, pieces):
    rows, width = q_mine.shape
    size = pieces[0].shape[2]
    count = sum(one.shape[0] for one in pieces) // 2
    wide = 2 * rows * (width // size)
    return pl.pallas_call(
        attention_kernel,
        out_shape=[
            jax.ShapeDtypeStruct((rows, 2 * width), jnp.bfloat16),
            jax.ShapeDtypeStruct((count, rows, size), jnp.bfloat16),
        ],
        in_specs=[SMEM] + [pl.BlockSpec()] * (6 + len(pieces)),
        out_specs=[pl.BlockSpec()] * 2,
        scratch_shapes=[pltpu.VMEM((count, rows, wide), jnp.float32)] * 2,
        compiler_params=params(8 + count * rows * wide // 2**17),
        cost_estimate=pl.CostEstimate(
            flops=10 * count * rows * wide * size,
            bytes_accessed=count * rows * size * 8,
            transcendentals=count * rows * wide,
        ),
        name="attention",
    )(
        core, positions.reshape(1, rows), doc_ids.reshape(1, rows), q_mine, q_other, g_mine, g_other, *pieces
    )


def product_kernel(first, dq_ref, wm_ref, wo_ref, out_ref):
    depth = wm_ref.shape[0]
    at = slice(first, first + out_ref.shape[1])
    acc = dot(dq_ref[:, 0:depth], wm_ref[:, at], ((1,), (0,)))
    acc = acc + dot(dq_ref[:, depth:], wo_ref[:, at], ((1,), (0,)))
    out_ref[...] = acc.astype(out_ref.dtype)


def product(dq, w_mine, w_other, first, width, dtype):
    rows, depth = dq.shape
    return pl.pallas_call(
        functools.partial(product_kernel, first),
        out_shape=jax.ShapeDtypeStruct((rows, width), dtype),
        in_specs=[pl.BlockSpec()] * 3,
        out_specs=pl.BlockSpec(),
        compiler_params=params(),
        cost_estimate=pl.CostEstimate(
            flops=2 * rows * depth * width, bytes_accessed=2 * depth * width, transcendentals=0
        ),
        name="product",
    )(dq, w_mine, w_other)


def own_kernel(dq_ref, wn_ref, wo_ref, acc_ref, *give_refs):
    depth, share = wn_ref.shape
    dq = dq_ref[:, 0:depth]
    width = share // len(give_refs)
    for i, give_ref in enumerate(give_refs):
        give_ref[...] = dot(dq, wo_ref[:, i * width : (i + 1) * width], ((1,), (0,))).astype(jnp.bfloat16)
    acc_ref[...] = dot(dq, wn_ref[...], ((1,), (0,)))


def own(dq, w_near, w_other):
    rows = dq.shape[0]
    share = w_near.shape[1]
    return pl.pallas_call(
        own_kernel,
        out_shape=[jax.ShapeDtypeStruct((rows, share), jnp.float32)]
        + [jax.ShapeDtypeStruct((rows, share // GIVES), jnp.bfloat16)] * GIVES,
        in_specs=[pl.BlockSpec()] * 3,
        out_specs=[pl.BlockSpec()] * (1 + GIVES),
        compiler_params=params(),
        cost_estimate=pl.CostEstimate(flops=0, bytes_accessed=0, transcendentals=0),
        name="own",
    )(dq, w_near, w_other)


def finish_kernel(core_ref, kv_ref, kv_far_ref, w_ref, acc_ref, far_ref, *refs):
    out_ref, hold_ref, sems = refs[GIVES:]
    rows, share = acc_ref.shape
    pair = kv_ref.shape[1]
    size = pair // 2
    tile = share // TILES
    kv = kv_ref[...].astype(jnp.float32) + kv_far_ref[...].astype(jnp.float32)
    mine, other = kv[:, :size], kv[:, size:]
    is_key = core_ref[0] == 0
    key = jnp.where(is_key, mine, other) * (1.0 / math.sqrt(size))
    kv = jnp.concatenate([key, jnp.where(is_key, other, mine)], axis=1).astype(jnp.bfloat16)
    copies = []
    for i in range(TILES):
        at = slice(i * tile, (i + 1) * tile)
        given_ref = refs[i * GIVES // TILES]
        skip = i * GIVES // TILES * (share // GIVES)
        given = given_ref[:, i * tile - skip : (i + 1) * tile - skip]
        acc = acc_ref[:, at] + far_ref[:, at].astype(jnp.float32) + given.astype(jnp.float32)
        acc = acc + dot(kv, w_ref[:, at], ((1,), (0,)))
        hold_ref[:, at] = acc.astype(jnp.bfloat16)
        copies.append(pltpu.make_async_copy(hold_ref.at[:, at], out_ref.at[:, at], sems.at[i]))
        copies[i].start()
    for one in copies:
        one.wait()


def finish(core, kv, kv_far, w_kv, acc, far, given):
    rows, share = acc.shape
    return pl.pallas_call(
        finish_kernel,
        out_shape=jax.ShapeDtypeStruct((rows, share), jnp.bfloat16),
        in_specs=[SMEM] + [pl.BlockSpec()] * (5 + GIVES),
        out_specs=ANY,
        scratch_shapes=[pltpu.VMEM((rows, share), jnp.bfloat16), pltpu.SemaphoreType.DMA((TILES,))],
        compiler_params=params(),
        cost_estimate=pl.CostEstimate(
            flops=2 * rows * kv.shape[1] * share, bytes_accessed=10 * rows * share, transcendentals=0
        ),
        name="finish",
    )(core, kv, kv_far, w_kv, acc, far, *given)


def on_device(queries, keys, values, dout, positions, doc_ids, w_query, w_kv):
    half = lax.axis_size("ctx") // 2
    head = lax.axis_index("head").astype(jnp.int32)
    core = (head & 1).reshape(1)
    share = w_kv.shape[1]
    local_heads = queries.shape[1] // keys.shape[1]

    piece = pack(core, positions, keys, values)
    along_z = [piece] + [swapped(piece, "ctx", 2 * s) for s in range(1, half)]
    early = (half + 1) // 2
    z_early, z_late = jnp.stack(along_z[:early]), jnp.stack(along_z[early:])
    x_early = swapped(z_early, "ctx", 1)
    far_send = column_block(w_query, head ^ 3, share, z_early)
    far_mine = column_block(w_query, head ^ 2, share, z_early)
    z_late, x_early, far_send, far_mine = lax.optimization_barrier((z_late, x_early, far_send, far_mine))
    x_late = swapped(z_late, "ctx", 1)
    far_other = swapped(far_send, "head", 1)
    here_z = jnp.concatenate([z_early, z_late])
    there_z = swapped(here_z, "head", 1)
    queries, dout, here_z = lax.optimization_barrier((queries, dout, here_z))
    q_other, g_other = swapped(queries, "head", 1), swapped(dout, "head", 1)
    x_late, q_other, g_other = lax.optimization_barrier((x_late, q_other, g_other))
    here_x = jnp.concatenate([x_early, x_late])
    pieces = (here_z, there_z, here_x, swapped(here_x, "head", 1))
    dq, back = attention(core, positions, doc_ids, queries, q_other, dout, g_other, pieces)

    part = product(dq, far_mine, far_other, 0, share, jnp.bfloat16)
    far = swapped(part, "head", 2)

    back, part = lax.optimization_barrier((back, part))
    pair = back[:half].astype(jnp.float32) + swapped(back[half:], "ctx", 1).astype(jnp.float32)
    mine = pair[0]
    for s in range(1, half):
        mine = mine + swapped(pair[s].astype(jnp.bfloat16), "ctx", 2 * s).astype(jnp.float32)
    mine = mine.astype(jnp.bfloat16)
    kv = jnp.concatenate([mine, swapped(mine, "head", 1)], axis=1)
    kv_far = swapped(kv, "head", 2)

    acc, *give = own(dq, *carve([head, head ^ 1], w_query, share, kv))
    given = [swapped(one, "head", 1) for one in give]
    return finish(core, kv, kv_far, w_kv, acc, far, given)


def solution(mesh):
    placed = (
        P("ctx", "head"),
        P("ctx", None),
        P("ctx", None),
        P("ctx", "head"),
        P("ctx"),
        P("ctx"),
        P("head", None),
        P(None, "head"),
    )
    return jax.shard_map(
        on_device, mesh=mesh, in_specs=placed, out_specs=P("ctx", "head"), check_vma=False
    )
```

```python
import functools
import math

import jax
import jax.numpy as jnp
from jax import lax
from jax.experimental import pallas as pl
from jax.experimental.pallas import tpu as pltpu
from jax.sharding import PartitionSpec as P

RUN = 64
META_ROWS = 16
TILES = 4
GIVES = 2
ANY = pl.BlockSpec(memory_space=pl.ANY)
HBM = pl.BlockSpec(memory_space=pltpu.HBM)
SMEM = pl.BlockSpec(memory_space=pltpu.SMEM)


def params(limit_mib=16):
    return pltpu.CompilerParams(vmem_limit_bytes=limit_mib * 1024 * 1024)


def swapped(value, axis, bits):
    count = lax.axis_size(axis)
    return lax.ppermute(value, axis, [(source, source ^ bits) for source in range(count)])


def dot(a, b, contract):
    return lax.dot_general(a, b, (contract, ((), ())), preferred_element_type=jnp.float32)


def each(count, body, state):
    if count > 8:
        return lax.fori_loop(0, count, body, state)
    for step in range(count):
        state = body(step, state)
    return state


def pack(core, positions, keys, values):
    rows, size = keys.shape
    held = jnp.where(core == 0, keys, values)
    runs = (positions.reshape(rows // RUN, RUN)[:, :1] // RUN).astype(jnp.bfloat16)
    meta = jnp.pad(jnp.broadcast_to(runs, (rows // RUN, size)), ((0, META_ROWS - rows // RUN), (0, 0)))
    return jnp.concatenate([held, meta], axis=0)


def column_block(w_query, block, share, after):
    w_query, _ = lax.optimization_barrier((w_query, after))
    return lax.dynamic_slice_in_dim(w_query, block * share, share, axis=1)


def carve_kernel(block_ref, w_ref, *refs):
    outs, sems = refs[1:-1], refs[-1]
    rows, share = outs[0].shape
    parts = sems.shape[1]
    copies = []
    for i, out_ref in enumerate(outs):
        at = pl.multiple_of(block_ref[i] * share, share)
        for j in range(parts):
            part = slice(j * (rows // parts), (j + 1) * (rows // parts))
            source = w_ref.at[part, pl.ds(at, share)]
            copies.append(pltpu.make_async_copy(source, out_ref.at[part, :], sems.at[i, j]))
            copies[-1].start()
    for one in copies:
        one.wait()


def carve(blocks, w_query, share, after):
    block = jax.ShapeDtypeStruct((w_query.shape[0], share), w_query.dtype)
    count = len(blocks)
    return pl.pallas_call(
        carve_kernel,
        out_shape=[block] * count,
        in_specs=[SMEM, HBM, ANY],
        out_specs=[pl.BlockSpec(memory_space=pltpu.VMEM)] * count,
        scratch_shapes=[pltpu.SemaphoreType.DMA((count, 4))],
        compiler_params=params(48),
        cost_estimate=pl.CostEstimate(flops=0, bytes_accessed=0, transcendentals=0),
        name="carve",
    )(jnp.stack(blocks), w_query, after)


def attention_kernel(core_ref, pos_ref, doc_ref, qm_ref, qo_ref, gm_ref, go_ref, *refs):
    groups = [refs[i : i + 2] for i in range(0, len(refs) - 4, 2)]
    dq_ref, back_ref, s_ref, dp_ref = refs[-4:]
    count, rows, size = back_ref.shape
    part = count // len(groups)
    heads = qm_ref.shape[1] // size
    is_key = core_ref[0] == 0
    inv_root = 1.0 / math.sqrt(size)

    def stack(mine_ref, other_ref):
        parts = [ref[:, h * size : (h + 1) * size] for ref in (mine_ref, other_ref) for h in range(heads)]
        return jnp.concatenate(parts, axis=0)

    query = stack(qm_ref, qo_ref)
    grad = stack(gm_ref, go_ref)
    wide = query.shape[0]
    last = jnp.concatenate([pos_ref[...].astype(jnp.float32)] * (2 * heads), axis=1)
    first = jnp.concatenate([(doc_ref[...] * RUN).astype(jnp.float32)] * (2 * heads), axis=1)
    offset = lax.broadcasted_iota(jnp.int32, (RUN, wide), 0).astype(jnp.float32)

    def everywhere(body, state):
        for group, (here_ref, there_ref) in enumerate(groups):
            state = each(part, lambda s, now: body(s, group * part + s, here_ref, there_ref, now), state)
        return state

    def scores(s, slot, here_ref, there_ref, top):
        here = here_ref[s, 0:rows, :]
        there = there_ref[s, 0:rows, :]
        key = jnp.where(is_key, here, there)
        value = jnp.where(is_key, there, here)
        score = dot(key, query, ((1,), (1,))) * inv_root
        dp_ref[slot] = dot(value, grad, ((1,), (1,)))
        meta = here_ref[s, rows : rows + META_ROWS, :].astype(jnp.float32)
        for run in range(rows // RUN):
            start = meta[run : run + 1, 0:1] * float(RUN)
            pos = offset + start
            allowed = (pos <= last) & (pos >= first)
            held = jnp.where(allowed, score[run * RUN : (run + 1) * RUN], -1e30)
            s_ref[slot, run * RUN : (run + 1) * RUN, :] = held
            top = jnp.maximum(top, jnp.max(held, axis=0, keepdims=True))
        return top

    top = everywhere(scores, jnp.full((1, wide), -1e30, jnp.float32))

    def weights(slot, state):
        total, mixed = state
        weight = jnp.exp(s_ref[slot] - top)
        s_ref[slot] = weight
        total = total + jnp.sum(weight, axis=0, keepdims=True)
        mixed = mixed + jnp.sum(weight * dp_ref[slot], axis=0, keepdims=True)
        return total, mixed

    zeros = jnp.zeros((1, wide), jnp.float32)
    total, mixed = each(count, weights, (zeros, zeros))
    scale = 1.0 / total
    delta = mixed * scale
    other = jnp.where(is_key, query, grad)

    def gradients(s, slot, here_ref, there_ref, dq):
        prob = s_ref[slot] * scale
        dscore = (prob * (dp_ref[slot] - delta)).astype(jnp.bfloat16)
        picked = jnp.where(is_key, dscore, prob.astype(jnp.bfloat16))
        back_ref[slot] = dot(picked, other, ((1,), (0,))).astype(jnp.bfloat16)
        key = jnp.where(is_key, here_ref[s, 0:rows, :], there_ref[s, 0:rows, :])
        return dq + dot(key, dscore, ((0,), (0,)))

    dq = everywhere(gradients, jnp.zeros((size, wide), jnp.float32)) * inv_root
    for h in range(wide // rows):
        block = dq[:, h * rows : (h + 1) * rows]
        dq_ref[:, h * size : (h + 1) * size] = block.T.astype(jnp.bfloat16)


def attention(core, positions, doc_ids, q_mine, q_other, g_mine, g_other, pieces):
    rows, width = q_mine.shape
    size = pieces[0].shape[2]
    count = sum(one.shape[0] for one in pieces) // 2
    wide = 2 * rows * (width // size)
    return pl.pallas_call(
        attention_kernel,
        out_shape=[
            jax.ShapeDtypeStruct((rows, 2 * width), jnp.bfloat16),
            jax.ShapeDtypeStruct((count, rows, size), jnp.bfloat16),
        ],
        in_specs=[SMEM] + [pl.BlockSpec()] * (6 + len(pieces)),
        out_specs=[pl.BlockSpec()] * 2,
        scratch_shapes=[pltpu.VMEM((count, rows, wide), jnp.float32)] * 2,
        compiler_params=params(8 + count * rows * wide // 2**17),
        cost_estimate=pl.CostEstimate(
            flops=10 * count * rows * wide * size,
            bytes_accessed=count * rows * size * 8,
            transcendentals=count * rows * wide,
        ),
        name="attention",
    )(
        core, positions.reshape(1, rows), doc_ids.reshape(1, rows), q_mine, q_other, g_mine, g_other, *pieces
    )


def product_kernel(first, dq_ref, wm_ref, wo_ref, out_ref):
    depth = wm_ref.shape[0]
    at = slice(first, first + out_ref.shape[1])
    acc = dot(dq_ref[:, 0:depth], wm_ref[:, at], ((1,), (0,)))
    acc = acc + dot(dq_ref[:, depth:], wo_ref[:, at], ((1,), (0,)))
    out_ref[...] = acc.astype(out_ref.dtype)


def product(dq, w_mine, w_other, first, width, dtype):
    rows, depth = dq.shape
    return pl.pallas_call(
        functools.partial(product_kernel, first),
        out_shape=jax.ShapeDtypeStruct((rows, width), dtype),
        in_specs=[pl.BlockSpec()] * 3,
        out_specs=pl.BlockSpec(),
        compiler_params=params(),
        cost_estimate=pl.CostEstimate(
            flops=2 * rows * depth * width, bytes_accessed=2 * depth * width, transcendentals=0
        ),
        name="product",
    )(dq, w_mine, w_other)


def own_kernel(dq_ref, wn_ref, wo_ref, acc_ref, *give_refs):
    depth, share = wn_ref.shape
    dq = dq_ref[:, 0:depth]
    width = share // len(give_refs)
    for i, give_ref in enumerate(give_refs):
        give_ref[...] = dot(dq, wo_ref[:, i * width : (i + 1) * width], ((1,), (0,))).astype(jnp.bfloat16)
    acc_ref[...] = dot(dq, wn_ref[...], ((1,), (0,)))


def own(dq, w_near, w_other):
    rows = dq.shape[0]
    share = w_near.shape[1]
    return pl.pallas_call(
        own_kernel,
        out_shape=[jax.ShapeDtypeStruct((rows, share), jnp.float32)]
        + [jax.ShapeDtypeStruct((rows, share // GIVES), jnp.bfloat16)] * GIVES,
        in_specs=[pl.BlockSpec()] * 3,
        out_specs=[pl.BlockSpec()] * (1 + GIVES),
        compiler_params=params(),
        cost_estimate=pl.CostEstimate(flops=0, bytes_accessed=0, transcendentals=0),
        name="own",
    )(dq, w_near, w_other)


def finish_kernel(core_ref, kv_ref, kv_far_ref, w_ref, acc_ref, far_ref, *refs):
    out_ref, hold_ref, sems = refs[GIVES:]
    rows, share = acc_ref.shape
    pair = kv_ref.shape[1]
    size = pair // 2
    tile = share // TILES
    kv = kv_ref[...].astype(jnp.float32) + kv_far_ref[...].astype(jnp.float32)
    mine, other = kv[:, :size], kv[:, size:]
    is_key = core_ref[0] == 0
    key = jnp.where(is_key, mine, other) * (1.0 / math.sqrt(size))
    kv = jnp.concatenate([key, jnp.where(is_key, other, mine)], axis=1).astype(jnp.bfloat16)
    copies = []
    for i in range(TILES):
        at = slice(i * tile, (i + 1) * tile)
        given_ref = refs[i * GIVES // TILES]
        skip = i * GIVES // TILES * (share // GIVES)
        given = given_ref[:, i * tile - skip : (i + 1) * tile - skip]
        acc = acc_ref[:, at] + far_ref[:, at].astype(jnp.float32) + given.astype(jnp.float32)
        acc = acc + dot(kv, w_ref[:, at], ((1,), (0,)))
        hold_ref[:, at] = acc.astype(jnp.bfloat16)
        copies.append(pltpu.make_async_copy(hold_ref.at[:, at], out_ref.at[:, at], sems.at[i]))
        copies[i].start()
    for one in copies:
        one.wait()


def finish(core, kv, kv_far, w_kv, acc, far, given):
    rows, share = acc.shape
    return pl.pallas_call(
        finish_kernel,
        out_shape=jax.ShapeDtypeStruct((rows, share), jnp.bfloat16),
        in_specs=[SMEM] + [pl.BlockSpec()] * (5 + GIVES),
        out_specs=ANY,
        scratch_shapes=[pltpu.VMEM((rows, share), jnp.bfloat16), pltpu.SemaphoreType.DMA((TILES,))],
        compiler_params=params(),
        cost_estimate=pl.CostEstimate(
            flops=2 * rows * kv.shape[1] * share, bytes_accessed=10 * rows * share, transcendentals=0
        ),
        name="finish",
    )(core, kv, kv_far, w_kv, acc, far, *given)


def on_device(queries, keys, values, dout, positions, doc_ids, w_query, w_kv):
    half = lax.axis_size("ctx") // 2
    head = lax.axis_index("head").astype(jnp.int32)
    core = (head & 1).reshape(1)
    share = w_kv.shape[1]
    local_heads = queries.shape[1] // keys.shape[1]

    piece = pack(core, positions, keys, values)
    along_z = [piece] + [swapped(piece, "ctx", 2 * s) for s in range(1, half)]
    early = 1
    z_early, z_late = jnp.stack(along_z[:early]), jnp.stack(along_z[early:])
    x_early = swapped(z_early, "ctx", 1)
    far_send = column_block(w_query, head ^ 3, share, z_early)
    far_mine = column_block(w_query, head ^ 2, share, z_early)
    z_late, x_early, far_send, far_mine = lax.optimization_barrier((z_late, x_early, far_send, far_mine))
    x_late = swapped(z_late, "ctx", 1)
    far_other = swapped(far_send, "head", 1)
    here_z = jnp.concatenate([z_early, z_late])
    there_z = swapped(here_z, "head", 1)
    queries, dout, here_z = lax.optimization_barrier((queries, dout, here_z))
    q_other, g_other = swapped(queries, "head", 1), swapped(dout, "head", 1)
    x_late, q_other, g_other = lax.optimization_barrier((x_late, q_other, g_other))
    here_x = jnp.concatenate([x_early, x_late])
    pieces = (here_z, there_z, here_x, swapped(here_x, "head", 1))
    dq, back = attention(core, positions, doc_ids, queries, q_other, dout, g_other, pieces)

    part = product(dq, far_mine, far_other, 0, share, jnp.bfloat16)
    far = swapped(part, "head", 2)

    back, part = lax.optimization_barrier((back, part))
    pair = back[:half].astype(jnp.float32) + swapped(back[half:], "ctx", 1).astype(jnp.float32)
    mine = pair[0]
    for s in range(1, half):
        mine = mine + swapped(pair[s].astype(jnp.bfloat16), "ctx", 2 * s).astype(jnp.float32)
    mine = mine.astype(jnp.bfloat16)
    kv = jnp.concatenate([mine, swapped(mine, "head", 1)], axis=1)
    kv_far = swapped(kv, "head", 2)

    acc, *give = own(dq, *carve([head, head ^ 1], w_query, share, kv))
    given = [swapped(one, "head", 1) for one in give]
    return finish(core, kv, kv_far, w_kv, acc, far, given)


def solution(mesh):
    placed = (
        P("ctx", "head"),
        P("ctx", None),
        P("ctx", None),
        P("ctx", "head"),
        P("ctx"),
        P("ctx"),
        P("head", None),
        P(None, "head"),
    )
    return jax.shard_map(
        on_device, mesh=mesh, in_specs=placed, out_specs=P("ctx", "head"), check_vma=False
    )
```

```python
import functools
import math

import jax
import jax.numpy as jnp
from jax import lax
from jax.experimental import pallas as pl
from jax.experimental.pallas import tpu as pltpu
from jax.sharding import PartitionSpec as P

RUN = 64
META_ROWS = 16
TILES = 4
GIVES = 2
ANY = pl.BlockSpec(memory_space=pl.ANY)
HBM = pl.BlockSpec(memory_space=pltpu.HBM)
SMEM = pl.BlockSpec(memory_space=pltpu.SMEM)


def params(limit_mib=16):
    return pltpu.CompilerParams(vmem_limit_bytes=limit_mib * 1024 * 1024)


def swapped(value, axis, bits):
    count = lax.axis_size(axis)
    return lax.ppermute(value, axis, [(source, source ^ bits) for source in range(count)])


def dot(a, b, contract):
    return lax.dot_general(a, b, (contract, ((), ())), preferred_element_type=jnp.float32)


def each(count, body, state):
    if count > 8:
        return lax.fori_loop(0, count, body, state)
    for step in range(count):
        state = body(step, state)
    return state


def pack(core, positions, keys, values):
    rows, size = keys.shape
    held = jnp.where(core == 0, keys, values)
    runs = (positions.reshape(rows // RUN, RUN)[:, :1] // RUN).astype(jnp.bfloat16)
    meta = jnp.pad(jnp.broadcast_to(runs, (rows // RUN, size)), ((0, META_ROWS - rows // RUN), (0, 0)))
    return jnp.concatenate([held, meta], axis=0)


def column_block(w_query, block, share, after):
    w_query, _ = lax.optimization_barrier((w_query, after))
    return lax.dynamic_slice_in_dim(w_query, block * share, share, axis=1)


def carve_kernel(block_ref, w_ref, *refs):
    outs, sems = refs[1:-1], refs[-1]
    rows, share = outs[0].shape
    parts = sems.shape[1]
    copies = []
    for i, out_ref in enumerate(outs):
        at = pl.multiple_of(block_ref[i] * share, share)
        for j in range(parts):
            part = slice(j * (rows // parts), (j + 1) * (rows // parts))
            source = w_ref.at[part, pl.ds(at, share)]
            copies.append(pltpu.make_async_copy(source, out_ref.at[part, :], sems.at[i, j]))
            copies[-1].start()
    for one in copies:
        one.wait()


def carve(blocks, w_query, share, after):
    block = jax.ShapeDtypeStruct((w_query.shape[0], share), w_query.dtype)
    count = len(blocks)
    return pl.pallas_call(
        carve_kernel,
        out_shape=[block] * count,
        in_specs=[SMEM, HBM, ANY],
        out_specs=[pl.BlockSpec(memory_space=pltpu.VMEM)] * count,
        scratch_shapes=[pltpu.SemaphoreType.DMA((count, 4))],
        compiler_params=params(48),
        cost_estimate=pl.CostEstimate(flops=0, bytes_accessed=0, transcendentals=0),
        name="carve",
    )(jnp.stack(blocks), w_query, after)


def attention_kernel(core_ref, pos_ref, doc_ref, qm_ref, qo_ref, gm_ref, go_ref, *refs):
    groups = [refs[i : i + 2] for i in range(0, len(refs) - 4, 2)]
    dq_ref, back_ref, s_ref, dp_ref = refs[-4:]
    count, rows, size = back_ref.shape
    part = count // len(groups)
    heads = qm_ref.shape[1] // size
    is_key = core_ref[0] == 0
    inv_root = 1.0 / math.sqrt(size)

    def stack(mine_ref, other_ref):
        parts = [ref[:, h * size : (h + 1) * size] for ref in (mine_ref, other_ref) for h in range(heads)]
        return jnp.concatenate(parts, axis=0)

    query = stack(qm_ref, qo_ref)
    grad = stack(gm_ref, go_ref)
    wide = query.shape[0]
    last = jnp.concatenate([pos_ref[...].astype(jnp.float32)] * (2 * heads), axis=1)
    first = jnp.concatenate([(doc_ref[...] * RUN).astype(jnp.float32)] * (2 * heads), axis=1)
    offset = lax.broadcasted_iota(jnp.int32, (RUN, wide), 0).astype(jnp.float32)

    def everywhere(body, state):
        for group, (here_ref, there_ref) in enumerate(groups):
            state = each(part, lambda s, now: body(s, group * part + s, here_ref, there_ref, now), state)
        return state

    def scores(s, slot, here_ref, there_ref, top):
        here = here_ref[s, 0:rows, :]
        there = there_ref[s, 0:rows, :]
        key = jnp.where(is_key, here, there)
        value = jnp.where(is_key, there, here)
        score = dot(key, query, ((1,), (1,))) * inv_root
        dp_ref[slot] = dot(value, grad, ((1,), (1,)))
        meta = here_ref[s, rows : rows + META_ROWS, :].astype(jnp.float32)
        for run in range(rows // RUN):
            start = meta[run : run + 1, 0:1] * float(RUN)
            pos = offset + start
            allowed = (pos <= last) & (pos >= first)
            held = jnp.where(allowed, score[run * RUN : (run + 1) * RUN], -1e30)
            s_ref[slot, run * RUN : (run + 1) * RUN, :] = held
            top = jnp.maximum(top, jnp.max(held, axis=0, keepdims=True))
        return top

    top = everywhere(scores, jnp.full((1, wide), -1e30, jnp.float32))

    def weights(slot, state):
        total, mixed = state
        weight = jnp.exp(s_ref[slot] - top)
        s_ref[slot] = weight
        total = total + jnp.sum(weight, axis=0, keepdims=True)
        mixed = mixed + jnp.sum(weight * dp_ref[slot], axis=0, keepdims=True)
        return total, mixed

    zeros = jnp.zeros((1, wide), jnp.float32)
    total, mixed = each(count, weights, (zeros, zeros))
    scale = 1.0 / total
    delta = mixed * scale
    other = jnp.where(is_key, query, grad)

    def gradients(s, slot, here_ref, there_ref, dq):
        prob = s_ref[slot] * scale
        dscore = (prob * (dp_ref[slot] - delta)).astype(jnp.bfloat16)
        picked = jnp.where(is_key, dscore, prob.astype(jnp.bfloat16))
        back_ref[slot] = dot(picked, other, ((1,), (0,))).astype(jnp.bfloat16)
        key = jnp.where(is_key, here_ref[s, 0:rows, :], there_ref[s, 0:rows, :])
        return dq + dot(key, dscore, ((0,), (0,)))

    dq = everywhere(gradients, jnp.zeros((size, wide), jnp.float32)) * inv_root
    for h in range(wide // rows):
        block = dq[:, h * rows : (h + 1) * rows]
        dq_ref[:, h * size : (h + 1) * size] = block.T.astype(jnp.bfloat16)


def attention(core, positions, doc_ids, q_mine, q_other, g_mine, g_other, pieces):
    rows, width = q_mine.shape
    size = pieces[0].shape[2]
    count = sum(one.shape[0] for one in pieces) // 2
    wide = 2 * rows * (width // size)
    return pl.pallas_call(
        attention_kernel,
        out_shape=[
            jax.ShapeDtypeStruct((rows, 2 * width), jnp.bfloat16),
            jax.ShapeDtypeStruct((count, rows, size), jnp.bfloat16),
        ],
        in_specs=[SMEM] + [pl.BlockSpec()] * (6 + len(pieces)),
        out_specs=[pl.BlockSpec()] * 2,
        scratch_shapes=[pltpu.VMEM((count, rows, wide), jnp.float32)] * 2,
        compiler_params=params(8 + count * rows * wide // 2**17),
        cost_estimate=pl.CostEstimate(
            flops=10 * count * rows * wide * size,
            bytes_accessed=count * rows * size * 8,
            transcendentals=count * rows * wide,
        ),
        name="attention",
    )(
        core, positions.reshape(1, rows), doc_ids.reshape(1, rows), q_mine, q_other, g_mine, g_other, *pieces
    )


def product_kernel(first, dq_ref, wm_ref, wo_ref, out_ref):
    depth = wm_ref.shape[0]
    at = slice(first, first + out_ref.shape[1])
    acc = dot(dq_ref[:, 0:depth], wm_ref[:, at], ((1,), (0,)))
    acc = acc + dot(dq_ref[:, depth:], wo_ref[:, at], ((1,), (0,)))
    out_ref[...] = acc.astype(out_ref.dtype)


def product(dq, w_mine, w_other, first, width, dtype):
    rows, depth = dq.shape
    return pl.pallas_call(
        functools.partial(product_kernel, first),
        out_shape=jax.ShapeDtypeStruct((rows, width), dtype),
        in_specs=[pl.BlockSpec()] * 3,
        out_specs=pl.BlockSpec(),
        compiler_params=params(),
        cost_estimate=pl.CostEstimate(
            flops=2 * rows * depth * width, bytes_accessed=2 * depth * width, transcendentals=0
        ),
        name="product",
    )(dq, w_mine, w_other)


def own_kernel(dq_ref, wn_ref, wo_ref, acc_ref, *give_refs):
    depth, share = wn_ref.shape
    dq = dq_ref[:, 0:depth]
    width = share // len(give_refs)
    for i, give_ref in enumerate(give_refs):
        give_ref[...] = dot(dq, wo_ref[:, i * width : (i + 1) * width], ((1,), (0,))).astype(jnp.bfloat16)
    acc_ref[...] = dot(dq, wn_ref[...], ((1,), (0,)))


def own(dq, w_near, w_other):
    rows = dq.shape[0]
    share = w_near.shape[1]
    return pl.pallas_call(
        own_kernel,
        out_shape=[jax.ShapeDtypeStruct((rows, share), jnp.float32)]
        + [jax.ShapeDtypeStruct((rows, share // GIVES), jnp.bfloat16)] * GIVES,
        in_specs=[pl.BlockSpec()] * 3,
        out_specs=[pl.BlockSpec()] * (1 + GIVES),
        compiler_params=params(),
        cost_estimate=pl.CostEstimate(flops=0, bytes_accessed=0, transcendentals=0),
        name="own",
    )(dq, w_near, w_other)


def finish_kernel(core_ref, kv_ref, kv_far_ref, w_ref, acc_ref, far_ref, *refs):
    out_ref, hold_ref, sems = refs[GIVES:]
    rows, share = acc_ref.shape
    pair = kv_ref.shape[1]
    size = pair // 2
    tile = share // TILES
    kv = kv_ref[...].astype(jnp.float32) + kv_far_ref[...].astype(jnp.float32)
    mine, other = kv[:, :size], kv[:, size:]
    is_key = core_ref[0] == 0
    key = jnp.where(is_key, mine, other) * (1.0 / math.sqrt(size))
    kv = jnp.concatenate([key, jnp.where(is_key, other, mine)], axis=1).astype(jnp.bfloat16)
    copies = []
    for i in range(TILES):
        at = slice(i * tile, (i + 1) * tile)
        given_ref = refs[i * GIVES // TILES]
        skip = i * GIVES // TILES * (share // GIVES)
        given = given_ref[:, i * tile - skip : (i + 1) * tile - skip]
        acc = acc_ref[:, at] + far_ref[:, at].astype(jnp.float32) + given.astype(jnp.float32)
        acc = acc + dot(kv, w_ref[:, at], ((1,), (0,)))
        hold_ref[:, at] = acc.astype(jnp.bfloat16)
        copies.append(pltpu.make_async_copy(hold_ref.at[:, at], out_ref.at[:, at], sems.at[i]))
        copies[i].start()
    for one in copies:
        one.wait()


def finish(core, kv, kv_far, w_kv, acc, far, given):
    rows, share = acc.shape
    return pl.pallas_call(
        finish_kernel,
        out_shape=jax.ShapeDtypeStruct((rows, share), jnp.bfloat16),
        in_specs=[SMEM] + [pl.BlockSpec()] * (5 + GIVES),
        out_specs=ANY,
        scratch_shapes=[pltpu.VMEM((rows, share), jnp.bfloat16), pltpu.SemaphoreType.DMA((TILES,))],
        compiler_params=params(),
        cost_estimate=pl.CostEstimate(
            flops=2 * rows * kv.shape[1] * share, bytes_accessed=10 * rows * share, transcendentals=0
        ),
        name="finish",
    )(core, kv, kv_far, w_kv, acc, far, *given)


def on_device(queries, keys, values, dout, positions, doc_ids, w_query, w_kv):
    half = lax.axis_size("ctx") // 2
    head = lax.axis_index("head").astype(jnp.int32)
    core = (head & 1).reshape(1)
    share = w_kv.shape[1]
    local_heads = queries.shape[1] // keys.shape[1]

    piece = pack(core, positions, keys, values)
    along_z = [piece] + [swapped(piece, "ctx", 2 * s) for s in range(1, half)]
    early = (half + 1) // 2
    z_early, z_late = jnp.stack(along_z[:early]), jnp.stack(along_z[early:])
    x_early = swapped(z_early, "ctx", 1)
    far_send = column_block(w_query, head ^ 3, share, z_early)
    far_mine = column_block(w_query, head ^ 2, share, z_early)
    there_early = swapped(z_early, "head", 1)
    z_late, x_early, there_early, far_send, far_mine = lax.optimization_barrier(
        (z_late, x_early, there_early, far_send, far_mine)
    )
    x_late = swapped(z_late, "ctx", 1)
    far_other = swapped(far_send, "head", 1)
    queries, dout, z_late = lax.optimization_barrier((queries, dout, z_late))
    q_other, g_other = swapped(queries, "head", 1), swapped(dout, "head", 1)
    x_late, q_other, g_other = lax.optimization_barrier((x_late, q_other, g_other))
    pieces = [z_early, there_early]
    for here in (z_late, x_early, x_late):
        pieces += [here, swapped(here, "head", 1)]
    dq, back = attention(core, positions, doc_ids, queries, q_other, dout, g_other, pieces)

    part = product(dq, far_mine, far_other, 0, share, jnp.bfloat16)
    far = swapped(part, "head", 2)

    back, part = lax.optimization_barrier((back, part))
    pair = back[:half].astype(jnp.float32) + swapped(back[half:], "ctx", 1).astype(jnp.float32)
    mine = pair[0]
    for s in range(1, half):
        mine = mine + swapped(pair[s].astype(jnp.bfloat16), "ctx", 2 * s).astype(jnp.float32)
    mine = mine.astype(jnp.bfloat16)
    kv = jnp.concatenate([mine, swapped(mine, "head", 1)], axis=1)
    kv_far = swapped(kv, "head", 2)

    acc, *give = own(dq, *carve([head, head ^ 1], w_query, share, kv))
    given = [swapped(one, "head", 1) for one in give]
    return finish(core, kv, kv_far, w_kv, acc, far, given)


def solution(mesh):
    placed = (
        P("ctx", "head"),
        P("ctx", None),
        P("ctx", None),
        P("ctx", "head"),
        P("ctx"),
        P("ctx"),
        P("head", None),
        P(None, "head"),
    )
    return jax.shard_map(
        on_device, mesh=mesh, in_specs=placed, out_specs=P("ctx", "head"), check_vma=False
    )
```

```python
import functools
import math

import jax
import jax.numpy as jnp
from jax import lax
from jax.experimental import pallas as pl
from jax.experimental.pallas import tpu as pltpu
from jax.sharding import PartitionSpec as P

RUN = 64
META_ROWS = 16
TILES = 4
GIVES = 2
ANY = pl.BlockSpec(memory_space=pl.ANY)
HBM = pl.BlockSpec(memory_space=pltpu.HBM)
SMEM = pl.BlockSpec(memory_space=pltpu.SMEM)


def params(limit_mib=16):
    return pltpu.CompilerParams(vmem_limit_bytes=limit_mib * 1024 * 1024)


def swapped(value, axis, bits):
    count = lax.axis_size(axis)
    return lax.ppermute(value, axis, [(source, source ^ bits) for source in range(count)])


def dot(a, b, contract):
    return lax.dot_general(a, b, (contract, ((), ())), preferred_element_type=jnp.float32)


def each(count, body, state):
    if count > 8:
        return lax.fori_loop(0, count, body, state)
    for step in range(count):
        state = body(step, state)
    return state


def pack(core, positions, keys, values):
    rows, size = keys.shape
    held = jnp.where(core == 0, keys, values)
    runs = (positions.reshape(rows // RUN, RUN)[:, :1] // RUN).astype(jnp.bfloat16)
    meta = jnp.pad(jnp.broadcast_to(runs, (rows // RUN, size)), ((0, META_ROWS - rows // RUN), (0, 0)))
    return jnp.concatenate([held, meta], axis=0)


def column_block(w_query, block, share, after):
    w_query, _ = lax.optimization_barrier((w_query, after))
    return lax.dynamic_slice_in_dim(w_query, block * share, share, axis=1)


def carve_kernel(block_ref, w_ref, *refs):
    outs, sems = refs[1:-1], refs[-1]
    rows, share = outs[0].shape
    parts = sems.shape[1]
    copies = []
    for i, out_ref in enumerate(outs):
        at = pl.multiple_of(block_ref[i] * share, share)
        for j in range(parts):
            part = slice(j * (rows // parts), (j + 1) * (rows // parts))
            source = w_ref.at[part, pl.ds(at, share)]
            copies.append(pltpu.make_async_copy(source, out_ref.at[part, :], sems.at[i, j]))
            copies[-1].start()
    for one in copies:
        one.wait()


def carve(blocks, w_query, share, after):
    block = jax.ShapeDtypeStruct((w_query.shape[0], share), w_query.dtype)
    count = len(blocks)
    return pl.pallas_call(
        carve_kernel,
        out_shape=[block] * count,
        in_specs=[SMEM, HBM, ANY],
        out_specs=[pl.BlockSpec(memory_space=pltpu.VMEM)] * count,
        scratch_shapes=[pltpu.SemaphoreType.DMA((count, 4))],
        compiler_params=params(48),
        cost_estimate=pl.CostEstimate(flops=0, bytes_accessed=0, transcendentals=0),
        name="carve",
    )(jnp.stack(blocks), w_query, after)


def attention_kernel(core_ref, pos_ref, doc_ref, qm_ref, qo_ref, gm_ref, go_ref, *refs):
    groups = [refs[i : i + 2] for i in range(0, len(refs) - 4, 2)]
    dq_ref, back_ref, s_ref, dp_ref = refs[-4:]
    count, rows, size = back_ref.shape
    part = count // len(groups)
    heads = qm_ref.shape[1] // size
    is_key = core_ref[0] == 0
    inv_root = 1.0 / math.sqrt(size)

    def stack(mine_ref, other_ref):
        parts = [ref[:, h * size : (h + 1) * size] for ref in (mine_ref, other_ref) for h in range(heads)]
        return jnp.concatenate(parts, axis=0)

    query = stack(qm_ref, qo_ref)
    grad = stack(gm_ref, go_ref)
    wide = query.shape[0]
    last = jnp.concatenate([pos_ref[...].astype(jnp.float32)] * (2 * heads), axis=1)
    first = jnp.concatenate([(doc_ref[...] * RUN).astype(jnp.float32)] * (2 * heads), axis=1)
    offset = lax.broadcasted_iota(jnp.int32, (RUN, wide), 0).astype(jnp.float32)

    def everywhere(body, state):
        for group, (here_ref, there_ref) in enumerate(groups):
            state = each(part, lambda s, now: body(s, group * part + s, here_ref, there_ref, now), state)
        return state

    def scores(s, slot, here_ref, there_ref, top):
        here = here_ref[s, 0:rows, :]
        there = there_ref[s, 0:rows, :]
        key = jnp.where(is_key, here, there)
        value = jnp.where(is_key, there, here)
        score = dot(key, query, ((1,), (1,))) * inv_root
        dp_ref[slot] = dot(value, grad, ((1,), (1,)))
        meta = here_ref[s, rows : rows + META_ROWS, :].astype(jnp.float32)
        for run in range(rows // RUN):
            start = meta[run : run + 1, 0:1] * float(RUN)
            pos = offset + start
            allowed = (pos <= last) & (pos >= first)
            held = jnp.where(allowed, score[run * RUN : (run + 1) * RUN], -1e30)
            s_ref[slot, run * RUN : (run + 1) * RUN, :] = held
            top = jnp.maximum(top, jnp.max(held, axis=0, keepdims=True))
        return top

    top = everywhere(scores, jnp.full((1, wide), -1e30, jnp.float32))

    def weights(slot, state):
        total, mixed = state
        weight = jnp.exp(s_ref[slot] - top)
        s_ref[slot] = weight
        total = total + jnp.sum(weight, axis=0, keepdims=True)
        mixed = mixed + jnp.sum(weight * dp_ref[slot], axis=0, keepdims=True)
        return total, mixed

    zeros = jnp.zeros((1, wide), jnp.float32)
    total, mixed = each(count, weights, (zeros, zeros))
    scale = 1.0 / total
    delta = mixed * scale
    other = jnp.where(is_key, query, grad)

    def gradients(s, slot, here_ref, there_ref, dq):
        prob = s_ref[slot] * scale
        dscore = (prob * (dp_ref[slot] - delta)).astype(jnp.bfloat16)
        picked = jnp.where(is_key, dscore, prob.astype(jnp.bfloat16))
        back_ref[slot] = dot(picked, other, ((1,), (0,))).astype(jnp.bfloat16)
        key = jnp.where(is_key, here_ref[s, 0:rows, :], there_ref[s, 0:rows, :])
        return dq + dot(key, dscore, ((0,), (0,)))

    dq = everywhere(gradients, jnp.zeros((size, wide), jnp.float32)) * inv_root
    for h in range(wide // rows):
        block = dq[:, h * rows : (h + 1) * rows]
        dq_ref[:, h * size : (h + 1) * size] = block.T.astype(jnp.bfloat16)


def attention(core, positions, doc_ids, q_mine, q_other, g_mine, g_other, pieces):
    rows, width = q_mine.shape
    size = pieces[0].shape[2]
    count = sum(one.shape[0] for one in pieces) // 2
    wide = 2 * rows * (width // size)
    return pl.pallas_call(
        attention_kernel,
        out_shape=[
            jax.ShapeDtypeStruct((rows, 2 * width), jnp.bfloat16),
            jax.ShapeDtypeStruct((count, rows, size), jnp.bfloat16),
        ],
        in_specs=[SMEM] + [pl.BlockSpec()] * (6 + len(pieces)),
        out_specs=[pl.BlockSpec()] * 2,
        scratch_shapes=[pltpu.VMEM((count, rows, wide), jnp.float32)] * 2,
        compiler_params=params(8 + count * rows * wide // 2**17),
        cost_estimate=pl.CostEstimate(
            flops=10 * count * rows * wide * size,
            bytes_accessed=count * rows * size * 8,
            transcendentals=count * rows * wide,
        ),
        name="attention",
    )(
        core, positions.reshape(1, rows), doc_ids.reshape(1, rows), q_mine, q_other, g_mine, g_other, *pieces
    )


def product_kernel(first, dq_ref, wm_ref, wo_ref, out_ref):
    depth = wm_ref.shape[0]
    at = slice(first, first + out_ref.shape[1])
    acc = dot(dq_ref[:, 0:depth], wm_ref[:, at], ((1,), (0,)))
    acc = acc + dot(dq_ref[:, depth:], wo_ref[:, at], ((1,), (0,)))
    out_ref[...] = acc.astype(out_ref.dtype)


def product(dq, w_mine, w_other, first, width, dtype):
    rows, depth = dq.shape
    return pl.pallas_call(
        functools.partial(product_kernel, first),
        out_shape=jax.ShapeDtypeStruct((rows, width), dtype),
        in_specs=[pl.BlockSpec()] * 3,
        out_specs=pl.BlockSpec(),
        compiler_params=params(),
        cost_estimate=pl.CostEstimate(
            flops=2 * rows * depth * width, bytes_accessed=2 * depth * width, transcendentals=0
        ),
        name="product",
    )(dq, w_mine, w_other)


def own_kernel(dq_ref, wn_ref, wo_ref, acc_ref, *give_refs):
    depth, share = wn_ref.shape
    dq = dq_ref[:, 0:depth]
    width = share // len(give_refs)
    for i, give_ref in enumerate(give_refs):
        give_ref[...] = dot(dq, wo_ref[:, i * width : (i + 1) * width], ((1,), (0,))).astype(jnp.bfloat16)
    acc_ref[...] = dot(dq, wn_ref[...], ((1,), (0,)))


def own(dq, w_near, w_other):
    rows = dq.shape[0]
    share = w_near.shape[1]
    return pl.pallas_call(
        own_kernel,
        out_shape=[jax.ShapeDtypeStruct((rows, share), jnp.float32)]
        + [jax.ShapeDtypeStruct((rows, share // GIVES), jnp.bfloat16)] * GIVES,
        in_specs=[pl.BlockSpec()] * 3,
        out_specs=[pl.BlockSpec()] * (1 + GIVES),
        compiler_params=params(),
        cost_estimate=pl.CostEstimate(flops=0, bytes_accessed=0, transcendentals=0),
        name="own",
    )(dq, w_near, w_other)


def finish_kernel(core_ref, kv_ref, kv_far_ref, w_ref, acc_ref, far_ref, *refs):
    out_ref, hold_ref, sems = refs[GIVES:]
    rows, share = acc_ref.shape
    pair = kv_ref.shape[1]
    size = pair // 2
    tile = share // TILES
    kv = kv_ref[...].astype(jnp.float32) + kv_far_ref[...].astype(jnp.float32)
    mine, other = kv[:, :size], kv[:, size:]
    is_key = core_ref[0] == 0
    key = jnp.where(is_key, mine, other) * (1.0 / math.sqrt(size))
    kv = jnp.concatenate([key, jnp.where(is_key, other, mine)], axis=1).astype(jnp.bfloat16)
    copies = []
    for i in range(TILES):
        at = slice(i * tile, (i + 1) * tile)
        given_ref = refs[i * GIVES // TILES]
        skip = i * GIVES // TILES * (share // GIVES)
        given = given_ref[:, i * tile - skip : (i + 1) * tile - skip]
        acc = acc_ref[:, at] + far_ref[:, at].astype(jnp.float32) + given.astype(jnp.float32)
        acc = acc + dot(kv, w_ref[:, at], ((1,), (0,)))
        hold_ref[:, at] = acc.astype(jnp.bfloat16)
        copies.append(pltpu.make_async_copy(hold_ref.at[:, at], out_ref.at[:, at], sems.at[i]))
        copies[i].start()
    for one in copies:
        one.wait()


def finish(core, kv, kv_far, w_kv, acc, far, given):
    rows, share = acc.shape
    return pl.pallas_call(
        finish_kernel,
        out_shape=jax.ShapeDtypeStruct((rows, share), jnp.bfloat16),
        in_specs=[SMEM] + [pl.BlockSpec()] * (5 + GIVES),
        out_specs=ANY,
        scratch_shapes=[pltpu.VMEM((rows, share), jnp.bfloat16), pltpu.SemaphoreType.DMA((TILES,))],
        compiler_params=params(),
        cost_estimate=pl.CostEstimate(
            flops=2 * rows * kv.shape[1] * share, bytes_accessed=10 * rows * share, transcendentals=0
        ),
        name="finish",
    )(core, kv, kv_far, w_kv, acc, far, *given)


def on_device(queries, keys, values, dout, positions, doc_ids, w_query, w_kv):
    half = lax.axis_size("ctx") // 2
    head = lax.axis_index("head").astype(jnp.int32)
    core = (head & 1).reshape(1)
    share = w_kv.shape[1]
    local_heads = queries.shape[1] // keys.shape[1]

    piece = pack(core, positions, keys, values)
    ways = [1] + list(range(half - 1, 1, -1))
    along_z = [piece] + [swapped(piece, "ctx", 2 * way) for way in ways]
    early = (half + 1) // 2
    z_early, z_late = jnp.stack(along_z[:early]), jnp.stack(along_z[early:])
    x_early = swapped(z_early, "ctx", 1)
    far_send = column_block(w_query, head ^ 3, share, z_early)
    far_mine = column_block(w_query, head ^ 2, share, z_early)
    there_early = swapped(z_early, "head", 1)
    z_late, x_early, there_early, far_send, far_mine = lax.optimization_barrier(
        (z_late, x_early, there_early, far_send, far_mine)
    )
    x_late = swapped(z_late, "ctx", 1)
    far_other = swapped(far_send, "head", 1)
    queries, dout, z_late = lax.optimization_barrier((queries, dout, z_late))
    q_other, g_other = swapped(queries, "head", 1), swapped(dout, "head", 1)
    x_late, q_other, g_other = lax.optimization_barrier((x_late, q_other, g_other))
    pieces = [z_early, there_early]
    for here in (z_late, x_early, x_late):
        pieces += [here, swapped(here, "head", 1)]
    dq, back = attention(core, positions, doc_ids, queries, q_other, dout, g_other, pieces)

    part = product(dq, far_mine, far_other, 0, share, jnp.bfloat16)
    far = swapped(part, "head", 2)

    back, part = lax.optimization_barrier((back, part))
    pair = back[:half].astype(jnp.float32) + swapped(back[half:], "ctx", 1).astype(jnp.float32)
    mine = pair[0]
    for s, way in enumerate(ways, 1):
        mine = mine + swapped(pair[s].astype(jnp.bfloat16), "ctx", 2 * way).astype(jnp.float32)
    mine = mine.astype(jnp.bfloat16)
    kv = jnp.concatenate([mine, swapped(mine, "head", 1)], axis=1)
    kv_far = swapped(kv, "head", 2)

    acc, *give = own(dq, *carve([head, head ^ 1], w_query, share, kv))
    given = [swapped(one, "head", 1) for one in give]
    return finish(core, kv, kv_far, w_kv, acc, far, given)


def solution(mesh):
    placed = (
        P("ctx", "head"),
        P("ctx", None),
        P("ctx", None),
        P("ctx", "head"),
        P("ctx"),
        P("ctx"),
        P("head", None),
        P(None, "head"),
    )
    return jax.shard_map(
        on_device, mesh=mesh, in_specs=placed, out_specs=P("ctx", "head"), check_vma=False
    )
```
